32 devices in a mesh: dp: 8 (over y, x, core), ctx: 4 (over z).
Axes of the slice: x: 2, y: 2, z: 4, core: 2. Of those that a mesh axis runs over, the one named last changes fastest.
Arguments:
- tokens: bfloat16 [16, 1024, 1024], P('dp', 'ctx'), may hold values from -6 to 6
- cotangent: bfloat16 [16, 1024, 1024], P('dp', 'ctx'), may hold values from -6 to 6
- norm_weight: bfloat16 [1024], P(('dp', 'ctx')), may hold values from 0.25 to 1.75
- input_weight: bfloat16 [1024, 4384], P(('dp', 'ctx')), may hold values from -0.1875 to 0.1875
- kernel_weight: bfloat16 [4, 2304], P(None, ('dp', 'ctx')), may hold values from -3 to 3
- kernel_bias: bfloat16 [2304], P(('dp', 'ctx')), may hold values from -3 to 3
- step_bias: bfloat16 [32], replicated, may hold values from -1.5 to 0.5
- decay_log: bfloat16 [32], replicated, may hold values from -8 to -3.1875
- skip_gain: bfloat16 [32], replicated, may hold values from 0.5 to 1.5
- gate_norm_weight: bfloat16 [2048], P(('dp', 'ctx')), may hold values from 0.25 to 1.75
- output_weight: bfloat16 [2048, 1024], P(('dp', 'ctx')), may hold values from -0.125 to 0.125
Outputs:
- activations: bfloat16 [16, 1024, 1024], P('dp', 'ctx')
- tokens_grad: float32 [16, 1024, 1024], P('dp', 'ctx')
- norm_weight_grad: float32 [1024], P(('dp', 'ctx'))
- input_weight_grad: float32 [1024, 4384], P(('dp', 'ctx'))
- kernel_weight_grad: float32 [4, 2304], P(None, ('dp', 'ctx'))
- kernel_bias_grad: float32 [2304], P(('dp', 'ctx'))
- step_bias_grad: float32 [32], replicated
- decay_log_grad: float32 [32], replicated
- skip_gain_grad: float32 [32], replicated
- gate_norm_weight_grad: float32 [2048], P(('dp', 'ctx'))
- output_weight_grad: float32 [2048, 1024], P(('dp', 'ctx'))
The draws below stay inside these ranges and needn't reach their ends.
All inputs are finite; a program needn't handle non-finite values.
Results may differ from the reference program's by a relative error of at most 0.017.
The reference program's roundings to bfloat16 on the way count: a program that leaves them out, or rounds other values in their place, can miss the bound.
Values may be sent and summed in bfloat16 or wider, within the bound.
No kernel may reach another device: no remote copies, remote signals or barrier semaphores. Data moves between devices by JAX's collectives and lax.ppermute only.
A program may use at most 120 MiB of HBM per device.

```python
import jax
import jax.numpy as jnp
from jax import lax

D = 1024
HEADS = 32
HEAD = 64
STATE = 128
CONV = 4
GROUP = 256
INNER = 2048
XBC = 2304
PROJ = 4384
SEQ_LEN = 1024
SEQUENCES = 16
N_CTX = 4


def levels(stream_key, dims, shards, low, top_value):
    def one(dim, shards_of):
        draws = jax.random.uniform(jax.random.fold_in(jax.random.fold_in(stream_key, 6), dim), (shards_of,), jnp.float32, low / len(shards), top_value / len(shards))
        return jnp.repeat(jnp.exp(draws), dims[dim] // shards_of).reshape((-1,) + (1,) * (len(dims) - dim - 1))

    level = one(*shards[0])
    for cut in shards[1:]:
        level = level * one(*cut)
    return level


def noise(stream_key, extent, spread, bound, cuts=(), held_as=jnp.bfloat16):
    loudness = levels(stream_key, extent, cuts, -0.22, 0.18) if cuts else 1.0
    values = jax.random.normal(stream_key, extent, jnp.float32) * spread * loudness
    return jnp.minimum(jnp.maximum(values, -bound), bound).astype(held_as)


def setup_inputs(seed: int = 0) -> dict:
    key_list = jax.random.split(jax.random.key(seed), 12)
    return {
        "tokens": noise(key_list[0], (SEQUENCES, SEQ_LEN, D), 1.0, 6.0, ((0, 8), (1, 4))),
        "cotangent": noise(key_list[1], (SEQUENCES, SEQ_LEN, D), 1.0, 6.0, ((0, 8), (1, 4))),
        "norm_weight": jnp.clip(1.0 + 0.15 * jax.random.normal(key_list[2], (D,), jnp.float32), 0.25, 1.75).astype(jnp.bfloat16),
        "input_weight": noise(key_list[3], (D, PROJ), D ** -0.5, 0.1875, ((0, 32),)),
        "kernel_weight": noise(key_list[4], (CONV, XBC), CONV ** -0.5, 3.0, ((1, 32),)),
        "kernel_bias": noise(key_list[5], (XBC,), 0.5, 3.0, ((0, 32),)),
        "step_bias": jnp.clip(jax.random.uniform(key_list[6], (HEADS,), jnp.float32, -1.5, 0.5), -1.5, 0.5).astype(jnp.bfloat16),
        "decay_log": jnp.clip(jax.random.uniform(key_list[7], (HEADS,), jnp.float32, -8.0, -3.1875), -8.0, -3.1875).astype(jnp.bfloat16),
        "skip_gain": jnp.clip(jax.random.uniform(key_list[8], (HEADS,), jnp.float32, 0.5, 1.5), 0.5, 1.5).astype(jnp.bfloat16),
        "gate_norm_weight": jnp.clip(1.0 + 0.15 * jax.random.normal(key_list[9], (INNER,), jnp.float32), 0.25, 1.75).astype(jnp.bfloat16),
        "output_weight": noise(key_list[10], (INNER, D), INNER ** -0.5, 0.125, ((0, 32),)),
    }


@jax.custom_vjp
def low(v):
    return lax.optimization_barrier(v.astype(jnp.bfloat16)).astype(jnp.float32)

@jax.custom_vjp
def low_back(v):
    return v

def low_keep(v):
    return (low(v), None)

def low_pass(kept, grad):
    return (grad,)

def back_keep(v):
    return (v, None)

def back_low(kept, grad):
    return (low(grad),)
low.defvjp(low_keep, low_pass)
low_back.defvjp(back_keep, back_low)
epsilon = 1e-05
highest = lax.Precision.HIGHEST

def group_scan(carried, pieces):
    head_values, write_rows, read_rows, step_sizes, log_decay = pieces
    cumulate = jnp.cumsum(log_decay, axis=0)
    length = write_rows.shape[0]
    intersection = jnp.dot(read_rows, write_rows.T, precision=highest)
    causal = (jnp.arange(length)[:, None] >= jnp.arange(length)[None, :])[:, :, None]
    differ = cumulate[:, None, :] - cumulate[None, :, :]
    factor = jnp.where(causal, jnp.exp(jnp.where(causal, differ, 0.0)), 0.0)
    scaled = head_values * step_sizes[:, :, None]
    within = jnp.einsum('tsh,shp->thp', intersection[:, :, None] * factor, scaled, precision=highest)
    entering = jnp.einsum('tn,hpn->thp', read_rows, carried, precision=highest) * jnp.exp(cumulate)[:, :, None]
    remain = jnp.exp(cumulate[-1][None, :] - cumulate)
    weighted = scaled * remain[:, :, None]
    new_state = jnp.exp(cumulate[-1])[:, None, None] * carried + jnp.einsum('shp,sn->hpn', weighted, write_rows, precision=highest)
    return (new_state, within + entering)

def block_forward(residual, norm_gain, input_matrix, kernel, kernel_shift, step_offset, rate_log, skip_term, output_gain, output_matrix):
    normed = low(residual * lax.rsqrt(lax.optimization_barrier(jnp.mean(residual * residual, axis=-1, keepdims=True)) + epsilon) * norm_gain)
    projected = low(low_back(jnp.dot(normed, input_matrix, precision=highest)))
    gate_raw = projected[:, :INNER]
    kernel_input = projected[:, INNER:INNER + XBC]
    step_raw = projected[:, INNER + XBC:]
    padded = jnp.concatenate([jnp.zeros((CONV - 1, XBC), jnp.float32), kernel_input], axis=0)
    summed = kernel_shift + kernel[0] * padded[0:SEQ_LEN]
    for offset in range(1, CONV):
        summed = summed + kernel[offset] * padded[offset:offset + SEQ_LEN]
    active = jax.nn.silu(summed)
    head_values = active[:, :INNER].reshape(SEQ_LEN, HEADS, HEAD)
    write_rows = active[:, INNER:INNER + STATE]
    read_rows = active[:, INNER + STATE:]
    step_sizes = jax.nn.softplus(step_raw + step_offset)
    log_decay = -step_sizes * jnp.exp(rate_log)
    pieces = (head_values.reshape(N_CTX, GROUP, HEADS, HEAD), write_rows.reshape(N_CTX, GROUP, STATE), read_rows.reshape(N_CTX, GROUP, STATE), step_sizes.reshape(N_CTX, GROUP, HEADS), log_decay.reshape(N_CTX, GROUP, HEADS))
    last_state, mixed_blocks = lax.scan(jax.checkpoint(group_scan), jnp.zeros((HEADS, HEAD, STATE), jnp.float32), pieces)
    mixture = mixed_blocks.reshape(SEQ_LEN, HEADS, HEAD) + skip_term[None, :, None] * head_values
    gated_out = mixture.reshape(SEQ_LEN, INNER) * jax.nn.silu(gate_raw)
    scaled = low(gated_out * lax.rsqrt(lax.optimization_barrier(jnp.mean(gated_out * gated_out, axis=-1, keepdims=True)) + epsilon) * output_gain)
    return residual + jnp.dot(scaled, output_matrix, precision=highest)

def reference(tokens, cotangent, norm_weight, input_weight, kernel_weight, kernel_bias, step_bias, decay_log, skip_gain, gate_norm_weight, output_weight):
    params = tuple((value.astype(jnp.float32) for value in (norm_weight, input_weight, kernel_weight, kernel_bias, step_bias, decay_log, skip_gain, gate_norm_weight, output_weight)))

    def one_sequence(totals, paired):
        sequence, sequence_grad = paired
        outputs, pullback = jax.vjp(block_forward, sequence.astype(jnp.float32), *params)
        gradients = pullback(sequence_grad.astype(jnp.float32))
        totals = tuple((first + second for first, second in zip(totals, gradients[1:])))
        return (totals, (outputs.astype(jnp.bfloat16), gradients[0]))
    initial = tuple((jnp.zeros_like(value) for value in params))
    totals, results = lax.scan(one_sequence, initial, (tokens, cotangent))
    return (results[0], results[1], totals[0], totals[1], totals[2], totals[3], totals[4], totals[5], totals[6], totals[7], totals[8])
```

```python
import functools

import jax
import jax.numpy as jnp
from jax import lax
from jax.experimental import pallas as pl
from jax.experimental.pallas import tpu as pltpu
from jax.sharding import PartitionSpec as P

HEADS = 32
HEAD = 64
STATE = 128
CONV = 4
INNER = 2048
XBC = 2304
BLOCK = 256
HALO = 16
LANES = 128
MINE = INNER // 2
PAIRS = MINE // LANES
CONVD = MINE + 2 * STATE

epsilon = 1e-05
bf16 = jnp.bfloat16
f32 = jnp.float32


def swap(value, axis, mask):
    count = lax.axis_size(axis)
    return lax.ppermute(value, axis, [(i, i ^ mask) for i in range(count)])


def hop(value, steps):
    count = lax.axis_size("ctx")
    pairs = [(i, i + steps) for i in range(count) if 0 <= i + steps < count]
    return lax.ppermute(value, "ctx", pairs)


def ordered(own, other, bit, place):
    first = bit == 0
    return jnp.stack([jnp.where(first, own, other), jnp.where(first, other, own)], axis=place)


def choose(value, index, place):
    return lax.dynamic_index_in_dim(value, index, place, keepdims=False)


def bits_of(count):
    return range(count.bit_length() - 1)


def gather_line(shard, z, n_ctx):
    grown = shard[None]
    for bit in bits_of(n_ctx):
        other = swap(grown, "ctx", 1 << bit)
        grown = ordered(grown, other, (z >> bit) & 1, 0).reshape((-1,) + shard.shape)
    return grown


def gather_plane(first, second, q, n_q):
    bits = list(bits_of(n_q))
    shape = first.shape
    for step, bit in enumerate(bits):
        back = bits[len(bits) - 1 - step]
        other = swap(first, "dp", 2 << bit)
        other_second = swap(second, "dp", 2 << back)
        first = ordered(first, other, (q >> bit) & 1, 0)
        second = ordered(second, other_second, (q >> back) & 1, step)
    return first.reshape((n_q,) + shape), second.reshape((n_q,) + shape)


def fold(value, axis, mask, bit, place):
    got = swap(choose(value, 1 - bit, place), axis, mask)
    return (choose(value, bit, place).astype(f32) + got.astype(f32)).astype(bf16)


def scatter_plane(first, second, q, n_q):
    bits = list(bits_of(n_q))
    rest = first.shape[1:]
    left = n_q
    for step, bit in enumerate(bits):
        back = bits[len(bits) - 1 - step]
        left //= 2
        first = fold(
            first.reshape((2, left) + rest), "dp", 2 << back, (q >> back) & 1, 0
        )
        second = fold(
            second.reshape((left, 2) + rest), "dp", 2 << bit, (q >> bit) & 1, 1
        )
    return first.reshape(rest), second.reshape(rest)


def scatter_line(value, z, n_ctx):
    rest = value.shape[1:]
    left = n_ctx
    for bit in reversed(bits_of(n_ctx)):
        left //= 2
        value = fold(value.reshape((2, left) + rest), "ctx", 1 << bit, (z >> bit) & 1, 0)
    return value.reshape(rest)


def dot(a, b):
    return jnp.dot(a, b, preferred_element_type=f32)


def dot_nt(a, b):
    return lax.dot_general(a, b, (((1,), (1,)), ((), ())), preferred_element_type=f32)


def dot_tn(a, b):
    return lax.dot_general(a, b, (((0,), (0,)), ((), ())), preferred_element_type=f32)


def split(value):
    high = value.astype(bf16)
    return high, (value - high.astype(f32)).astype(bf16)


def split3(value):
    high, low = split(value)
    least = (value - high.astype(f32) - low.astype(f32)).astype(bf16)
    return high, low, least


def spread(value, spreader):
    high, low = split(value)
    return dot(high, spreader) + dot(low, spreader)


def pool(value, spreader):
    high, low = split(value)
    return dot_nt(high, spreader) + dot_nt(low, spreader)


def conv_rows(px, halo, block):
    begin = pl.multiple_of(jnp.maximum(block * BLOCK - HALO, 0), HALO)
    before = jnp.where(block == 0, halo[...], px[pl.ds(begin, HALO), :])
    here = px[pl.ds(pl.multiple_of(block * BLOCK, BLOCK), BLOCK), :]
    return jnp.concatenate([before, here], axis=0)


def conv_sum(rows, kw, kb):
    wide = rows[:, :CONVD].astype(f32)
    taps = [wide[HALO - CONV + 1 + k : HALO - CONV + 1 + k + BLOCK] for k in range(CONV)]
    total = kb[...]
    for k in range(CONV):
        total = total + kw[k : k + 1, :] * taps[k]
    return total, taps


def steps_of(raw, sb, rate):
    biased = raw + sb
    step = jnp.maximum(biased, 0.0) + jnp.log1p(jnp.exp(-jnp.abs(biased)))
    return biased, step, -step * rate


def features_kernel(px, halo, kw, kb, sb, rate, tri, ex, x_o, u_o, bc_o, step_o, cum_o, cumt_o,
                    entry_o, factor_o, total_o, decay_o, state, passed):
    block = pl.program_id(1)
    rows = conv_rows(px.at[0], halo.at[0], block)
    total, _ = conv_sum(rows, kw, kb)
    active = total * jax.nn.sigmoid(total)
    _, step, log_decay = steps_of(rows[HALO:, CONVD:].astype(f32), sb[...], rate[...])
    cum = sum(dot(tri[...], part) for part in split3(log_decay))
    last = cum[BLOCK - 1 : BLOCK, :]
    x = active[:, :MINE]
    bc = active[:, MINE:].astype(bf16)
    u = x * spread(step, ex[...])
    remaining = spread(jnp.exp(last - cum), ex[...])
    whole = spread(jnp.broadcast_to(jnp.exp(last), (16, LANES)), ex[...])[:1]

    @pl.when(block == 0)
    def _():
        state[...] = jnp.zeros_like(state)
        passed[...] = jnp.ones_like(passed)

    entry_o[0] = state[...]
    factor_o[0] = jnp.broadcast_to(passed[...], (8, MINE))
    u16 = u.astype(bf16)
    grown = dot_tn(bc[:, :STATE], (u16.astype(f32) * remaining).astype(bf16))
    state[...] = whole * state[...] + grown
    passed[...] = passed[...] * whole
    total_o[0] = state[...].astype(bf16)
    decay_o[0] = jnp.broadcast_to(passed[...], (8, MINE))
    x_o[...] = x.astype(bf16)
    u_o[...] = u16
    bc_o[...] = bc
    step_o[...] = step
    cum_o[...] = cum
    cumt_o[0] = cum.T


def within_kernel(u, bc, cum, cumt, y_o):
    rows = lax.broadcasted_iota(jnp.int32, (BLOCK, BLOCK), 0)
    columns = lax.broadcasted_iota(jnp.int32, (BLOCK, BLOCK), 1)
    products = jnp.where(rows >= columns, dot_nt(bc[:, STATE:], bc[:, :STATE]), 0.0)
    lane = lax.broadcasted_iota(jnp.int32, (BLOCK, LANES), 1)
    for pair in range(PAIRS):
        values = u[:, pair * LANES : (pair + 1) * LANES]
        made = []
        for head in (2 * pair, 2 * pair + 1):
            decay = jnp.exp(jnp.minimum(cum[:, head : head + 1] - cumt[0, head : head + 1, :], 0.0))
            made.append(dot((products * decay).astype(bf16), values))
        y_o[:, pair * LANES : (pair + 1) * LANES] = jnp.where(lane < HEAD, made[0], made[1])


def gate_kernel(normed, cot, wg, wo, y, x, bc, cum, entry, factor, incoming, skip, gain, ex,
                mix_o, z_o, ds_o, state_o, sums_o):
    begin = pl.multiple_of(HALO + pl.program_id(1) * BLOCK, HALO)
    z = dot(normed[0, pl.ds(begin, BLOCK), :], wg[...]).astype(bf16)
    z_o[...] = z
    ds = dot_nt(cot[...], wo[...])
    ds_o[...] = ds
    entering = (entry[0] + factor[0][:1] * incoming[0].astype(f32)).astype(bf16)
    state_o[0] = entering
    from_state = spread(jnp.exp(cum[...]), ex[...]) * dot(bc[:, STATE:], entering)
    mix = y[...] + from_state + skip[...] * x[...].astype(f32)
    mix_o[...] = mix
    z = z.astype(f32)
    g = mix * (z * jax.nn.sigmoid(z))
    ones = jnp.ones((8, MINE), bf16)
    squares = sum(dot_nt(ones, part) for part in split(g * g))
    crossed = sum(dot_nt(ones, part) for part in split(ds * gain[...] * g))
    which = lax.broadcasted_iota(jnp.int32, (8, BLOCK), 0)
    sums_o[...] = jnp.where(which < 4, squares, crossed)


def mixture_kernel(mix_r, z_r, ds_r, x, bc, cum, r, t, skip, gain, ex,
                   scaled_o, dy_o, dz_o, inner_o, exit_o, factor_o, send_o, gain_o, skip_o,
                   state, passed):
    j, i = pl.program_id(0), pl.program_id(1)

    @pl.when((j == 0) & (i == 0))
    def _():
        gain_o[...] = jnp.zeros_like(gain_o)
        skip_o[...] = jnp.zeros_like(skip_o)

    @pl.when(i == 0)
    def _():
        state[...] = jnp.zeros_like(state)
        passed[...] = jnp.ones_like(passed)

    mix = mix_r[...]
    z = z_r[...].astype(f32)
    ds = ds_r[...]
    scale = r[:, :1]
    sig = jax.nn.sigmoid(z)
    silu = z * sig
    g = mix * silu
    normalized = g * scale
    scaled_o[...] = (normalized * gain[...]).astype(bf16)
    gain_o[...] += jnp.sum(ds * normalized, axis=0, keepdims=True)
    dg = ds * (scale * gain[...]) - g * t[:, :1]
    dmix = dg * silu
    dz_o[...] = (dg * mix * (sig * (1.0 + z * (1.0 - sig)))).astype(bf16)
    xs = x[...].astype(f32)
    skip_o[...] += jnp.sum(dmix * xs, axis=0, keepdims=True)
    dy = dmix.astype(bf16)
    dy_o[...] = dy
    dyf = dy.astype(f32)
    inner_o[...] = pool(dyf * (mix - skip[...] * xs), ex[...])
    grown = spread(jnp.exp(cum[...]), ex[...])
    last = cum[BLOCK - 1 : BLOCK, :]
    whole = spread(jnp.broadcast_to(jnp.exp(last), (16, LANES)), ex[...])[:1]
    exit_o[0] = state[...]
    factor_o[0] = jnp.broadcast_to(passed[...], (8, MINE))
    state[...] = whole * state[...] + dot_tn(bc[:, STATE:], (dyf * grown).astype(bf16))
    passed[...] = passed[...] * whole
    send_o[0] = state[...].astype(bf16)


def within_back_kernel(u, dy, bc, cum, cumt, du_o, dbc_o):
    rows = lax.broadcasted_iota(jnp.int32, (BLOCK, BLOCK), 0)
    columns = lax.broadcasted_iota(jnp.int32, (BLOCK, BLOCK), 1)
    causal = columns >= rows
    products = jnp.where(causal, dot_nt(bc[:, :STATE], bc[:, STATE:]), 0.0)
    lane = lax.broadcasted_iota(jnp.int32, (BLOCK, LANES), 1)
    total = jnp.zeros((BLOCK, BLOCK), f32)
    for pair in range(PAIRS):
        values = u[:, pair * LANES : (pair + 1) * LANES]
        grads = dy[:, pair * LANES : (pair + 1) * LANES]
        made = []
        for half in range(2):
            head = 2 * pair + half
            decay = jnp.exp(jnp.minimum(cumt[0, head : head + 1, :] - cum[:, head : head + 1], 0.0))
            made.append(dot((products * decay).astype(bf16), grads))
            own = jnp.where((lane < HEAD) == (half == 0), values, jnp.zeros_like(values))
            total = total + dot_nt(own, grads) * decay
        du_o[:, pair * LANES : (pair + 1) * LANES] = jnp.where(lane < HEAD, made[0], made[1])
    total = jnp.where(causal, total, 0.0).astype(bf16)
    dbc_o[:, :STATE] = dot(total, bc[:, STATE:])
    dbc_o[:, STATE:] = dot_tn(total, bc[:, :STATE])


def features_back_kernel(px, halo, kw, kb, sb, rate, tri, ex, u, dy, du_r, dbc, inner, cum,
                         entering, exit_r, factor, incoming, skip,
                         gp_o, gpt_o, rim_o, tail_o, kw_o, kb_o, sb_o, rate_o, after):
    j, i = pl.program_id(0), pl.program_id(1)
    block = pl.num_programs(1) - 1 - i

    @pl.when((j == 0) & (i == 0))
    def _():
        kw_o[...] = jnp.zeros_like(kw_o)
        kb_o[...] = jnp.zeros_like(kb_o)
        sb_o[...] = jnp.zeros_like(sb_o)
        rate_o[...] = jnp.zeros_like(rate_o)

    @pl.when(i == 0)
    def _():
        after[...] = jnp.zeros_like(after)

    rows = conv_rows(px.at[0], halo.at[0], block)
    total, taps = conv_sum(rows, kw, kb)
    sig = jax.nn.sigmoid(total)
    active = total * sig
    x = active[:, :MINE]
    bc = active[:, MINE:].astype(bf16)
    biased, step, log_decay = steps_of(rows[HALO:, CONVD:].astype(f32), sb[...], rate[...])
    c = cum[...]
    last = c[BLOCK - 1 : BLOCK, :]
    leaving = exit_r[0] + factor[0][:1] * incoming[0].astype(f32)
    leaving16 = leaving.astype(bf16)
    remaining = spread(jnp.exp(last - c), ex[...])
    grown = spread(jnp.exp(c), ex[...])
    uf = u[...].astype(f32)
    dyf = dy[...].astype(f32)
    du_in = du_r[...]
    du_state = remaining * dot(bc[:, :STATE], leaving16)
    held = pool(uf * du_state, ex[...])
    crossing = jnp.sum(leaving * entering[0].astype(f32), axis=0, keepdims=True)
    crossing = pool(jnp.broadcast_to(crossing, (16, MINE)), ex[...])[:1] * jnp.exp(last)
    flow = inner[...] - pool(uf * du_in, ex[...])
    dlog = crossing + sum(dot_tn(tri[...], part) for part in split3(flow))
    dlog = dlog + sum(dot(tri[...], part) for part in split3(held)) - held
    du = du_in + du_state
    dstep = pool(du * x, ex[...]) - dlog * rate[...]
    draw = dstep * jax.nn.sigmoid(biased)
    gpt_o[...] = draw.astype(bf16)
    sb_o[...] += jnp.sum(draw, axis=0, keepdims=True)
    rate_o[...] += jnp.sum(dlog * log_decay, axis=0, keepdims=True)
    dx = du * spread(step, ex[...]) + skip[...] * dyf
    db = dbc[:, :STATE] + dot_nt((uf * remaining).astype(bf16), leaving16)
    dc = dbc[:, STATE:] + dot_nt((dyf * grown).astype(bf16), entering[0])
    dact = jnp.concatenate([dx, db, dc], axis=1)
    dpre = dact * (sig * (1.0 + total * (1.0 - sig)))
    kb_o[...] += jnp.sum(dpre, axis=0, keepdims=True)
    for k in range(CONV):
        kw_o[k : k + 1, :] += jnp.sum(dpre * taps[k], axis=0, keepdims=True)
    wide = jnp.concatenate([dpre, after[...]], axis=0)
    din = sum(kw[k : k + 1, :] * wide[CONV - 1 - k : CONV - 1 - k + BLOCK] for k in range(CONV))
    gp_o[0] = din.astype(bf16)
    after[...] = dpre[:8]

    @pl.when(i == 0)
    def _():
        tail_o[0] = din[BLOCK - 16 :]

    early = jnp.concatenate([jnp.zeros((8, CONVD), f32), dpre[:8]], axis=0)
    rim_o[0] = sum(kw[k : k + 1, :] * early[CONV - 1 - k : CONV - 1 - k + 8] for k in range(CONV))


def call(kernel, grid, in_specs, out_specs, out_shape, scratch=()):
    return pl.pallas_call(
        kernel,
        grid=grid,
        in_specs=in_specs,
        out_specs=out_specs,
        out_shape=out_shape,
        scratch_shapes=scratch,
        compiler_params=pltpu.CompilerParams(
            vmem_limit_bytes=56 << 20, dimension_semantics=("arbitrary",) * len(grid)
        ),
    )


def sds(shape, dtype=f32):
    return jax.ShapeDtypeStruct(shape, dtype)


def on_device(
    tokens,
    cotangent,
    norm_weight,
    input_weight,
    kernel_weight,
    kernel_bias,
    step_bias,
    decay_log,
    skip_gain,
    gate_norm_weight,
    output_weight,
):
    n_dp, n_ctx = lax.axis_size("dp"), lax.axis_size("ctx")
    n_q, n_all = n_dp // 2, n_dp * n_ctx
    place, z = lax.axis_index("dp"), lax.axis_index("ctx")
    q, core = place >> 1, place & 1
    side = z & 1
    seqs, piece, width = tokens.shape
    length = 2 * piece
    blocks = length // BLOCK
    rows = seqs * length
    run = INNER // n_dp
    heads_run = HEADS // n_dp
    r_in, r_out = input_weight.shape[0], output_weight.shape[0]
    every = ("dp", "ctx")

    def of_core(value, which):
        lead = value.shape[:-1]
        cut = value.reshape(lead + (n_q, 2, -1))
        return jnp.where(which == 0, cut[..., 0, :], cut[..., 1, :]).reshape(lead + (-1,))

    def to_all(value):
        lead = value.shape[:-1]
        cut = value.reshape(lead + (n_q, 1, -1))
        mask = (lax.broadcasted_iota(jnp.int32, (n_q, 2, 1), 1) == core).astype(value.dtype)
        return (cut * mask).reshape(lead + (-1,))

    def columns_for(which):
        return jnp.concatenate(
            [
                of_core(input_weight[:, INNER : 2 * INNER], which),
                input_weight[:, 2 * INNER : INNER + XBC],
                of_core(input_weight[:, :INNER], which),
            ],
            axis=1,
        )

    got = swap(columns_for(1 - core), "dp", 1)
    shard = ordered(columns_for(core), got, core, 0)

    small = jnp.concatenate(
        [
            norm_weight,
            kernel_bias,
            gate_norm_weight,
            kernel_weight.reshape(-1),
            input_weight[:, INNER + XBC :].reshape(-1),
        ]
    )
    small_size = small.shape[0]
    small_pad = -small_size % LANES
    small = jnp.pad(small, (0, small_pad)).reshape(-1, LANES)
    small = lax.all_to_all(jnp.broadcast_to(small[None], (n_all,) + small.shape), every, 0, 0)
    small = small.reshape(n_all, -1)
    cuts = [r_in, XBC // n_all, INNER // n_all, CONV * (XBC // n_all), r_in * HEADS]
    ends = [sum(cuts[: n + 1]) for n in range(len(cuts))]
    norm_all, bias_all, gain_all, taps_all, step_all = (
        small[:, end - cut : end] for cut, end in zip(cuts, ends)
    )
    norm_full = norm_all.reshape(-1).astype(f32)
    bias_full = bias_all.reshape(-1).astype(f32)
    gain = of_core(gain_all.reshape(-1), core).astype(f32)[None]
    taps_full = taps_all.reshape(n_all, CONV, -1).transpose(1, 0, 2).reshape(CONV, XBC).astype(f32)
    w_step = of_core(step_all.reshape(width, HEADS), core)

    def conv_columns(value):
        return jnp.concatenate([of_core(value[..., :INNER], core), value[..., INNER:]], axis=-1)

    kb = conv_columns(bias_full[None])
    kw = jnp.pad(conv_columns(taps_full), ((0, 8 - CONV), (0, 0)))

    def heads_of_core(value):
        return jnp.pad(of_core(value.astype(f32)[None], core), ((0, 0), (0, LANES - HEADS // 2)))

    sb = heads_of_core(step_bias)
    rate = heads_of_core(decay_log)
    rate = jnp.where(jnp.arange(LANES)[None] < HEADS // 2, jnp.exp(rate), 0.0)
    skip = jnp.repeat(of_core(skip_gain.astype(f32)[None], core), HEAD, axis=1)
    ex = (jnp.arange(LANES)[:, None] == (jnp.arange(MINE)[None] // HEAD)).astype(bf16)
    tri = (jnp.arange(BLOCK)[:, None] >= jnp.arange(BLOCK)[None]).astype(bf16)

    line = gather_line(shard[:, :, :CONVD], z, n_ctx)
    first, second = gather_plane(line[:, 0], line[:, 1], q, n_q)
    w_conv = jnp.stack([first, second], axis=1).reshape(width, CONVD)
    w_front = jnp.concatenate(
        [w_conv, jnp.pad(w_step, ((0, 0), (0, LANES - HEADS // 2)))], axis=1
    )

    shard = jnp.concatenate([shard[:, :, CONVD:], output_weight.reshape(2, r_out // 2, width)], axis=1)
    line = gather_line(shard, z, n_ctx)
    first, second = gather_plane(line[:, 0], line[:, 1], q, n_q)
    w_gate = jnp.stack([first[:, :, :r_in], second[:, :, :r_in]], axis=1).reshape(width, MINE)
    w_out = jnp.stack([first[:, :, r_in:], second[:, :, r_in:]], axis=2).reshape(MINE, width)

    def enter(value):
        got = swap(choose(value, 1 - side, 0), "ctx", 1)
        mine = ordered(choose(value, side, 0), got, side, 0).reshape(length, width)
        return ordered(mine, swap(mine, "dp", 1), core, 0)

    def leave(value):
        got = swap(choose(value, 1 - core, 0), "dp", 1)
        mine = (choose(value, core, 0).astype(f32) + got.astype(f32)).astype(bf16)
        mine = mine.reshape(2, piece, width)
        return ordered(choose(mine, side, 0), swap(choose(mine, 1 - side, 0), "ctx", 1), side, 0)

    inside = enter(tokens)
    before = hop(inside[:, length - HALO :], 2)
    extended = jnp.concatenate([before, inside], axis=1).astype(f32)
    normed = (
        extended
        * lax.rsqrt(jnp.mean(extended * extended, axis=-1, keepdims=True) + epsilon)
        * norm_full
    ).astype(bf16)
    normed_flat = normed[:, HALO:].reshape(rows, width)
    projected = jnp.dot(
        normed.reshape(-1, width), w_front, preferred_element_type=f32
    ).astype(bf16).reshape(seqs, length + HALO, CONVD + LANES)
    halo, px = projected[:, :HALO], projected[:, HALO:]
    cot = enter(cotangent).reshape(rows, width)

    grid = (seqs, blocks)

    def here(shape, back=False):
        lead = len(shape)
        if back:
            return pl.BlockSpec(shape, lambda j, i: (j * blocks + blocks - 1 - i,) + (0,) * (lead - 1))
        return pl.BlockSpec(shape, lambda j, i: (j * blocks + i,) + (0,) * (lead - 1))

    def per_seq(shape):
        return pl.BlockSpec(shape, lambda j, i: (j,) + (0,) * (len(shape) - 1))

    def fixed(shape):
        return pl.BlockSpec(shape, lambda j, i: (0,) * len(shape))

    steps_n = seqs * blocks
    wide, heads_s, both = (BLOCK, MINE), (BLOCK, LANES), (BLOCK, 2 * STATE)
    state_s, row8 = (1, STATE, MINE), (1, 8, MINE)
    conv_specs = [
        per_seq((1, length, CONVD + LANES)),
        per_seq((1, HALO, CONVD + LANES)),
        fixed((8, CONVD)),
        fixed((1, CONVD)),
        fixed((1, LANES)),
        fixed((1, LANES)),
        fixed((BLOCK, BLOCK)),
        fixed((LANES, MINE)),
    ]
    conv_args = (px, halo, kw, kb, sb, rate, tri, ex)
    x, u, bc, _, cum, cumt, entry, entry_factor, state_total, state_decay = call(
        features_kernel,
        grid,
        conv_specs,
        [here(wide), here(wide), here(both), here(heads_s), here(heads_s),
         here((1, LANES, BLOCK)), here(state_s), here(row8), per_seq(state_s), per_seq(row8)],
        [sds((rows, MINE), bf16), sds((rows, MINE), bf16), sds((rows, 2 * STATE), bf16),
         sds((rows, LANES)), sds((rows, LANES)), sds((steps_n, LANES, BLOCK)),
         sds((steps_n, STATE, MINE)), sds((steps_n, 8, MINE)),
         sds((seqs, STATE, MINE), bf16), sds((seqs, 8, MINE))],
        [pltpu.VMEM((STATE, MINE), f32), pltpu.VMEM((1, MINE), f32)],
    )(*conv_args)

    def relay(local, decay, steps):
        received = hop(local, steps)
        for _ in range(n_ctx // 2 - 2):
            received = hop((decay[:, :1] * received.astype(f32) + local.astype(f32)).astype(bf16), steps)
        return received

    incoming = relay(state_total, state_decay, 2)
    y = call(
        within_kernel,
        grid,
        [here(wide), here(both), here(heads_s), here((1, LANES, BLOCK))],
        here(wide),
        sds((rows, MINE)),
    )(u, bc, cum, cumt)

    mix, gate_raw, ds, entering, sums = call(
        gate_kernel,
        grid,
        [per_seq((1, length + HALO, width)), here((BLOCK, width)), fixed((width, MINE)),
         fixed((MINE, width)), here(wide), here(wide), here(both), here(heads_s),
         here(state_s), here(row8), per_seq(state_s), fixed((1, MINE)), fixed((1, MINE)),
         fixed((LANES, MINE))],
        [here(wide), here(wide), here(wide), here(state_s),
         pl.BlockSpec((8, BLOCK), lambda j, i: (0, j * blocks + i))],
        [sds((rows, MINE)), sds((rows, MINE), bf16), sds((rows, MINE)),
         sds((steps_n, STATE, MINE), bf16), sds((8, rows))],
    )(normed, cot, w_gate, w_out, y, x, bc, cum, entry, entry_factor, incoming, skip, gain, ex)
    sums = sums + swap(sums, "dp", 1)
    scale = lax.rsqrt(sums[0] / INNER + epsilon)
    back_scale = scale * scale * scale / INNER * sums[4]
    scale = jnp.broadcast_to(scale[:, None], (rows, LANES))
    back_scale = jnp.broadcast_to(back_scale[:, None], (rows, LANES))

    scaled, dy, dz, inner, leaving, leave_factor, grad_send, gain_sum, skip_sum = call(
        mixture_kernel,
        grid,
        [here(wide, True)] * 4
        + [here(both, True), here(heads_s, True), here(heads_s, True), here(heads_s, True),
           fixed((1, MINE)), fixed((1, MINE)), fixed((LANES, MINE))],
        [here(wide, True)] * 3
        + [here(heads_s, True), here(state_s, True), here(row8, True), per_seq(state_s),
           fixed((1, MINE)), fixed((1, MINE))],
        [sds((rows, MINE), bf16)] * 3
        + [sds((rows, LANES)), sds((steps_n, STATE, MINE)), sds((steps_n, 8, MINE)),
           sds((seqs, STATE, MINE), bf16), sds((1, MINE)), sds((1, MINE))],
        [pltpu.VMEM((STATE, MINE), f32), pltpu.VMEM((1, MINE), f32)],
    )(mix, gate_raw, ds, x, bc, cum, scale, back_scale, skip, gain, ex)
    grad_incoming = relay(grad_send, state_decay, -2)

    def weight_grad(left, right):
        return lax.dot_general(
            left, right, (((0,), (0,)), ((), ())), preferred_element_type=f32
        ).astype(bf16)

    d_out = weight_grad(scaled, cot).reshape(n_q, n_ctx, 2, r_out // 2, width)
    d_gate = weight_grad(normed_flat, dz).reshape(n_q, 2, n_ctx, r_in, MINE)
    halves = [
        jnp.concatenate([d_gate[:, half], d_out[:, :, half]], axis=2) for half in range(2)
    ]
    halves = scatter_plane(halves[0], halves[1], q, n_q)
    late = scatter_line(jnp.stack(halves, axis=1), z, n_ctx)

    partial_out = jnp.dot(scaled, w_out, preferred_element_type=f32).astype(bf16)
    activations = (
        tokens.astype(f32) + leave(partial_out.reshape(seqs, length, width)).astype(f32)
    ).astype(bf16)

    du, dbc = call(
        within_back_kernel,
        grid,
        [here(wide), here(wide), here(both), here(heads_s), here((1, LANES, BLOCK))],
        [here(wide), here(both)],
        [sds((rows, MINE)), sds((rows, 2 * STATE))],
    )(u, dy, bc, cum, cumt)

    gp, gpt, rim, tail, kw_sum, kb_sum, sb_sum, rate_sum = call(
        features_back_kernel,
        grid,
        conv_specs
        + [here(wide, True), here(wide, True), here(wide, True), here(both, True),
           here(heads_s, True), here(heads_s, True), here(state_s, True), here(state_s, True),
           here(row8, True), per_seq(state_s), fixed((1, MINE))],
        [pl.BlockSpec((1, BLOCK, CONVD), lambda j, i: (j, blocks - 1 - i, 0)),
         here(heads_s, True), per_seq((1, 8, CONVD)), per_seq((1, 16, CONVD)),
         fixed((8, CONVD)), fixed((1, CONVD)), fixed((1, LANES)), fixed((1, LANES))],
        [sds((seqs, length, CONVD), bf16), sds((rows, LANES), bf16), sds((seqs, 8, CONVD)),
         sds((seqs, 16, CONVD)), sds((8, CONVD)), sds((1, CONVD)), sds((1, LANES)),
         sds((1, LANES))],
        [pltpu.VMEM((8, CONVD), f32)],
    )(*conv_args, u, dy, du, dbc, inner, cum, entering, leaving, leave_factor, grad_incoming, skip)

    tail = tail.at[:, 8:].add(hop(rim, -2)).astype(bf16)
    gp = lax.dynamic_update_slice(gp, tail, (0, length - 16, 0)).reshape(rows, CONVD)
    d_conv = weight_grad(normed_flat, gp).reshape(n_q, 2, n_ctx, r_in, CONVD)
    halves = scatter_plane(d_conv[:, 0], d_conv[:, 1], q, n_q)
    early = scatter_line(jnp.stack(halves, axis=1), z, n_ctx)

    d_step = lax.dot_general(
        normed_flat, gpt, (((0,), (0,)), ((), ())), preferred_element_type=f32
    )[:, : HEADS // 2]

    def times(left, right):
        return lax.dot_general(left, right, (((1,), (1,)), ((), ())), preferred_element_type=f32)

    grad_normed = times(dz, w_gate) + times(jnp.concatenate([gp, gpt], axis=1), w_front)
    inside_f = inside.reshape(rows, width).astype(f32)
    inverse = lax.rsqrt(jnp.mean(inside_f * inside_f, axis=-1, keepdims=True) + epsilon)
    norm_sum = jnp.sum(grad_normed * inside_f * inverse, axis=0)
    back = leave(grad_normed.astype(bf16).reshape(seqs, length, width)).astype(f32)

    residual = tokens.astype(f32)
    inverse = lax.rsqrt(jnp.mean(residual * residual, axis=-1, keepdims=True) + epsilon)
    weighted = back * norm_full
    along = jnp.mean(weighted * residual, axis=-1, keepdims=True)
    tokens_grad = (
        cotangent.astype(f32)
        + inverse * weighted
        - residual * (inverse * inverse * inverse * along)
    )

    both_cores = jnp.concatenate([early, late[:, :r_in]], axis=2)
    own = choose(both_cores, core, 0).astype(f32)
    got = swap(choose(both_cores, 1 - core, 0), "dp", 1).astype(f32)

    def join(mine, others):
        mine, others = (v.reshape(r_in, n_q, run) for v in (mine, others))
        return ordered(mine, others, core, 2).reshape(r_in, INNER)

    output_weight_grad = late[:, r_in:].reshape(r_out, width).astype(f32)

    def conv_to_all(value):
        return jnp.concatenate([to_all(value[:, :MINE]), value[:, MINE:]], axis=1)

    def heads_to_all(value):
        return to_all(value[:, : HEADS // 2])

    skip_heads = jnp.sum(skip_sum.reshape(1, HEADS // 2, HEAD), axis=2)
    head_sums = jnp.concatenate(
        [heads_to_all(sb_sum), heads_to_all(rate_sum), heads_to_all(skip_heads)], axis=1
    )
    packed = jnp.concatenate(
        [
            norm_sum.reshape(n_all, r_in),
            conv_to_all(kb_sum).reshape(n_all, -1),
            to_all(gain_sum).reshape(n_all, -1),
            conv_to_all(kw_sum[:CONV]).reshape(CONV, n_all, -1).transpose(1, 0, 2).reshape(n_all, -1),
            to_all(d_step).reshape(n_all, -1),
            jnp.broadcast_to(head_sums, (n_all, 3 * HEADS)),
        ],
        axis=1,
    )
    size = packed.shape[1]
    packed = jnp.pad(packed, ((0, 0), (0, -size % LANES))).reshape(n_all, -1, LANES)
    sums = jnp.sum(lax.all_to_all(packed, every, 0, 0), axis=0).reshape(-1)
    norm_grad, bias_grad, gain_grad, taps_grad, step_grad = (
        sums[end - cut : end] for cut, end in zip(cuts, ends)
    )
    head_sums = sums[ends[-1] : size].reshape(3, HEADS)
    input_weight_grad = jnp.concatenate(
        [
            join(own[:, CONVD:], got[:, CONVD:]),
            join(own[:, :MINE], got[:, :MINE]),
            own[:, MINE:CONVD] + got[:, MINE:CONVD],
            step_grad.reshape(r_in, HEADS),
        ],
        axis=1,
    )
    return (
        activations,
        tokens_grad,
        norm_grad,
        input_weight_grad,
        taps_grad.reshape(CONV, -1),
        bias_grad,
        head_sums[0],
        head_sums[1],
        head_sums[2],
        gain_grad,
        output_weight_grad,
    )


def solution(mesh):
    data, rows_spec, vector = P("dp", "ctx", None), P(("dp", "ctx"), None), P(("dp", "ctx"))
    taps = P(None, ("dp", "ctx"))
    return jax.shard_map(
        on_device,
        mesh=mesh,
        in_specs=(data, data, vector, rows_spec, taps, vector, P(), P(), P(), vector, rows_spec),
        out_specs=(data, data, vector, rows_spec, taps, vector, P(), P(), P(), vector, rows_spec),
        check_vma=False,
    )
```

```python
import functools

import jax
import jax.numpy as jnp
import ml_dtypes
import numpy as np
from jax import lax
from jax.experimental import pallas as pl
from jax.experimental.pallas import tpu as pltpu
from jax.sharding import PartitionSpec as P

HEADS = 32
HEAD = 64
STATE = 128
CONV = 4
INNER = 2048
XBC = 2304
BLOCK = 256
HALO = 16
LANES = 128
MINE = INNER // 2
PAIRS = MINE // LANES
CONVD = MINE + 2 * STATE
FRONT = CONVD + LANES

epsilon = 1e-05
bf16 = jnp.bfloat16
f32 = jnp.float32


def swap(value, axis, mask):
    count = lax.axis_size(axis)
    return lax.ppermute(value, axis, [(i, i ^ mask) for i in range(count)])


def hop(value, steps):
    count = lax.axis_size("ctx")
    pairs = [(i, i + steps) for i in range(count) if 0 <= i + steps < count]
    return lax.ppermute(value, "ctx", pairs)


def ordered(own, other, bit, place):
    first = bit == 0
    return jnp.stack([jnp.where(first, own, other), jnp.where(first, other, own)], axis=place)


def choose(value, index, place):
    return lax.dynamic_index_in_dim(value, index, place, keepdims=False)


def bits_of(count):
    return range(count.bit_length() - 1)


def gather_line(shard, z, n_ctx, least=0):
    grown = shard
    for place, bit in enumerate(reversed(range(least, n_ctx.bit_length() - 1))):
        grown = ordered(grown, swap(grown, "ctx", 1 << bit), (z >> bit) & 1, place)
    return grown.reshape((n_ctx >> least,) + shard.shape)


def gather_plane(first, second, q, n_q):
    bits = list(bits_of(n_q))
    shape = first.shape
    for step, bit in enumerate(bits):
        back = bits[len(bits) - 1 - step]
        other = swap(first, "dp", 2 << bit)
        other_second = swap(second, "dp", 2 << back)
        first = ordered(first, other, (q >> bit) & 1, 0)
        second = ordered(second, other_second, (q >> back) & 1, step)
    return first.reshape((n_q,) + shape), second.reshape((n_q,) + shape)


def fold(value, axis, mask, bit, place):
    got = swap(choose(value, 1 - bit, place), axis, mask)
    return (choose(value, bit, place).astype(f32) + got.astype(f32)).astype(bf16)


def scatter_plane(first, second, q, n_q):
    bits = list(bits_of(n_q))
    rest = first.shape[1:]
    left = n_q
    for step, bit in enumerate(bits):
        back = bits[len(bits) - 1 - step]
        left //= 2
        first = fold(
            first.reshape((2, left) + rest), "dp", 2 << back, (q >> back) & 1, 0
        )
        second = fold(
            second.reshape((left, 2) + rest), "dp", 2 << bit, (q >> bit) & 1, 1
        )
    return first.reshape(rest), second.reshape(rest)


def gather_rest(near, far, z, n_ctx, q, n_q):
    near_halves = gather_plane(near[:, 0], near[:, 1], q, n_q)
    far_halves = gather_plane(far[:, 0], far[:, 1], q, n_q)
    shape = (n_q, n_ctx) + near.shape[2:]
    return tuple(ordered(a, b, z & 1, 2).reshape(shape) for a, b in zip(near_halves, far_halves))


def scatter_both(first, second, z, n_ctx, q, n_q):
    shape = (n_q, n_ctx // 2, 2) + first.shape[2:]
    sums = []
    for which in (1 - (z & 1), z & 1):
        halves = (choose(value.reshape(shape), which, 2) for value in (first, second))
        sums.append(jnp.stack(scatter_plane(*halves, q, n_q), axis=1))
    got = swap(sums[0], "ctx", 1)
    total = (sums[1].astype(f32) + got.astype(f32)).astype(bf16)
    return scatter_line(total, z, n_ctx, 1)


def sides_of(value):
    return swap(value, "dp", 2), swap(value, "dp", 4)


def sides_of_each(along_x, along_y):
    return swap(along_x, "dp", 2), swap(along_y, "dp", 4)


def add(*values):
    return sum(value.astype(f32) for value in values).astype(bf16)


def after(value, *others):
    if not others:
        return value
    return pl.pallas_call(
        lambda *refs: None,
        in_specs=[pl.BlockSpec(memory_space=pl.ANY)] * (1 + len(others)),
        out_specs=pl.BlockSpec(memory_space=pl.ANY),
        out_shape=jax.ShapeDtypeStruct(value.shape, value.dtype),
        input_output_aliases={0: 0},
    )(value, *others)


def scatter_line(value, z, n_ctx, least=0):
    rest = value.shape[1:]
    left = n_ctx >> least
    for bit in range(least, n_ctx.bit_length() - 1):
        left //= 2
        value = fold(value.reshape((left, 2) + rest), "ctx", 1 << bit, (z >> bit) & 1, 1)
    return value.reshape(rest)


def dot(a, b):
    return jnp.dot(a, b, preferred_element_type=f32)


def dot_nt(a, b):
    return lax.dot_general(a, b, (((1,), (1,)), ((), ())), preferred_element_type=f32)


def dot_tn(a, b):
    return lax.dot_general(a, b, (((0,), (0,)), ((), ())), preferred_element_type=f32)


def split(value):
    high = value.astype(bf16)
    return high, (value - high.astype(f32)).astype(bf16)


def split3(value):
    high, low = split(value)
    least = (value - high.astype(f32) - low.astype(f32)).astype(bf16)
    return high, low, least


def halves_of(value):
    return jnp.concatenate(split(value), axis=1)


def spread(halves, ex, lanes):
    return dot(halves, ex[:, lanes])


def pool(value, pairs, strip):
    return dot_nt(halves_of(value), pairs[:, strip * 2 * LANES : (strip + 1) * 2 * LANES])


def strip_of(number, size=LANES):
    return slice(number * size, (number + 1) * size)


def conv_rows(px, block):
    return px[pl.ds(pl.multiple_of(block * BLOCK, BLOCK), BLOCK + HALO), :]


def conv_strip(wide, kw, lanes):
    taps = [wide[HALO - CONV + 1 + k : HALO - CONV + 1 + k + BLOCK, lanes] for k in range(CONV)]
    total = kw[CONV : CONV + 1, lanes]
    for k in range(CONV):
        total = total + kw[k : k + 1, lanes] * taps[k]
    return total, taps


def inverse_rms(rows):
    return lax.rsqrt(jnp.mean(rows * rows, axis=-1, keepdims=True) + epsilon)


def steps_of(raw, heads, pick):
    biased = dot(raw, pick[...]) + heads[0:1, :]
    rate = heads[1:2, :]
    step = jnp.maximum(biased, 0.0) + jnp.log1p(jnp.exp(-jnp.abs(biased)))
    return biased, step, -step * rate, rate


def features_kernel(mine, other, before, before_other, norm, front, kw, heads, pick, tri, ex, pairs,
                    normed_o, px_o, x_o, u_o, bc_o, cum_o, cumt_o, entry_o, factor_o, total_o,
                    decay_o, state, passed, wide, weighted):
    j, block = pl.program_id(0), pl.program_id(1)
    start = pl.multiple_of(block * BLOCK, BLOCK)
    early = pl.multiple_of(jnp.maximum(start - HALO, 0), HALO)

    def rows_of(begin, count):
        return jnp.where(j == 0, mine[pl.ds(begin, count), :], other[pl.ds(begin, count), :])

    ahead = jnp.where(j == 0, before[...], before_other[...])
    ahead = jnp.where(block == 0, ahead, rows_of(early, HALO))
    residual = jnp.concatenate([ahead, rows_of(start, BLOCK)], axis=0).astype(f32)
    normed = (residual * inverse_rms(residual) * norm[...]).astype(bf16)
    normed_o[...] = normed[HALO:]
    rows = dot(normed, front[...]).astype(bf16)
    px_o[0, pl.ds(start, BLOCK + HALO), :] = rows
    wide[...] = rows[:, :CONVD].astype(f32)

    @pl.when(block == 0)
    def _():
        state[...] = jnp.zeros_like(state)
        passed[...] = jnp.ones_like(passed)

    _, step, log_decay, _ = steps_of(rows[HALO:, CONVD:], heads, pick)
    cum = sum(dot(tri[...], part) for part in split3(log_decay))
    last = cum[BLOCK - 1 : BLOCK, :]
    cum_o[...] = cum
    cumt_o[0] = cum.T
    step, remaining = halves_of(step), halves_of(jnp.exp(last - cum))
    whole = halves_of(jnp.broadcast_to(jnp.exp(last), (16, LANES)))
    entry_o[0] = state[...].astype(bf16)
    factor_o[0] = jnp.broadcast_to(passed[...], (8, MINE))
    for number in range(2):
        lanes = strip_of(PAIRS + number)
        total, _ = conv_strip(wide, kw, lanes)
        bc_o[:, strip_of(number)] = (total * jax.nn.sigmoid(total)).astype(bf16)
    for number in range(PAIRS):
        lanes = strip_of(number)
        total, _ = conv_strip(wide, kw, lanes)
        x = total * jax.nn.sigmoid(total)
        x_o[:, lanes] = x.astype(bf16)
        u = (x * spread(step, ex, lanes)).astype(bf16)
        u_o[:, lanes] = u
        weighted[:, lanes] = (u.astype(f32) * spread(remaining, ex, lanes)).astype(bf16)
    whole = spread(whole, ex, slice(0, MINE))[:1]
    state[...] = whole * state[...] + dot_tn(bc_o[:, :STATE], weighted[...])
    passed[...] = passed[...] * whole
    total_o[0] = state[...].astype(bf16)
    decay_o[0] = jnp.broadcast_to(passed[...], (8, MINE))


def within_kernel(u, bc, cum, cumt, y_o):
    rows = lax.broadcasted_iota(jnp.int32, (BLOCK, BLOCK), 0)
    columns = lax.broadcasted_iota(jnp.int32, (BLOCK, BLOCK), 1)
    products = jnp.where(rows >= columns, dot_nt(bc[:, STATE:], bc[:, :STATE]), 0.0)
    lane = lax.broadcasted_iota(jnp.int32, (BLOCK, LANES), 1)
    for pair in range(PAIRS):
        values = u[:, pair * LANES : (pair + 1) * LANES]
        made = []
        for head in (2 * pair, 2 * pair + 1):
            decay = jnp.exp(jnp.minimum(cum[:, head : head + 1] - cumt[0, head : head + 1, :], 0.0))
            made.append(dot((products * decay).astype(bf16), values))
        made = jnp.where(lane < HEAD, made[0], made[1])
        y_o[:, pair * LANES : (pair + 1) * LANES] = made.astype(bf16)


def gate_kernel(normed, cot_mine, cot_other, wg, wo, y, x, bc, cum, entry, factor, incoming, skip,
                gain, ex, mix_o, z_o, ds_o, state_o, sums_o):
    cot = jnp.where(pl.program_id(0) == 0, cot_mine[...], cot_other[...])
    grown = halves_of(jnp.exp(cum[...]))
    squares = jnp.zeros((BLOCK, LANES), f32)
    crossed = jnp.zeros((BLOCK, LANES), f32)
    for chunk in range(PAIRS // 2):
        many = strip_of(chunk, 2 * LANES)
        z_all = dot(normed[...], wg[:, many]).astype(bf16)
        ds_all = dot_nt(cot, wo[many, :])
        entering = entry[0, :, many].astype(f32) + factor[0, :1, many] * incoming[0, :, many].astype(f32)
        entering = entering.astype(bf16)
        z_o[:, many] = z_all
        ds_o[:, many] = ds_all.astype(bf16)
        state_o[0, :, many] = entering
        mix_all = spread(grown, ex, many) * dot(bc[:, STATE:], entering)
        for half in range(2):
            part, lanes = strip_of(half), strip_of(2 * chunk + half)
            carried = mix_all[:, part] + y[:, lanes].astype(f32)
            mix_o[:, lanes] = carried.astype(bf16)
            mix = carried + skip[:, lanes] * x[:, lanes].astype(f32)
            z = z_all[:, part].astype(f32)
            g = mix * (z * jax.nn.sigmoid(z))
            squares = squares + g * g
            crossed = crossed + ds_all[:, part] * gain[:, lanes] * g
    ones = jnp.ones((8, 2 * LANES), bf16)
    which = lax.broadcasted_iota(jnp.int32, (8, BLOCK), 0)
    squares, crossed = dot_nt(ones, halves_of(squares)), dot_nt(ones, halves_of(crossed))
    sums_o[...] = jnp.where(which < 4, squares, crossed)


def mixture_kernel(mix_r, z_r, ds_r, x, bc, cum, sums, got, skip, gain, ex, pairs,
                   scaled_o, dy_o, dz_o, inner_o, exit_o, factor_o, send_o, gain_o, skip_o,
                   state, passed, weighted):
    j, i = pl.program_id(0), pl.program_id(1)

    @pl.when((j == 0) & (i == 0))
    def _():
        gain_o[...] = jnp.zeros_like(gain_o)
        skip_o[...] = jnp.zeros_like(skip_o)

    @pl.when(i == 0)
    def _():
        state[...] = jnp.zeros_like(state)
        passed[...] = jnp.ones_like(passed)

    summed = sums[...] + got[...]
    lane = lax.broadcasted_iota(jnp.int32, (8, 2 * LANES), 1)
    row = lax.broadcasted_iota(jnp.int32, (8, 2 * LANES), 0)
    turn = jnp.where(row == (lane // LANES) * 4, 1.0, 0.0).astype(bf16)
    summed = sum(dot_tn(part, turn) for part in split3(summed))
    scale = lax.rsqrt(summed[:, :LANES] / INNER + epsilon)
    back_scale = scale * scale * scale * (summed[:, LANES:] / INNER)
    grown = halves_of(jnp.exp(cum[...]))
    inner = jnp.zeros((BLOCK, LANES), f32)
    for number in range(PAIRS):
        lanes = strip_of(number)
        carried = mix_r[:, lanes].astype(f32)
        xs = x[:, lanes].astype(f32)
        mix = carried + skip[:, lanes] * xs
        z = z_r[:, lanes].astype(f32)
        ds = ds_r[:, lanes].astype(f32)
        sig = jax.nn.sigmoid(z)
        silu = z * sig
        g = mix * silu
        normalized = g * scale
        scaled_o[:, lanes] = (normalized * gain[:, lanes]).astype(bf16)
        gain_o[:, lanes] += jnp.sum(ds * normalized, axis=0, keepdims=True)
        dg = ds * (scale * gain[:, lanes]) - g * back_scale
        dmix = dg * silu
        dz_o[:, lanes] = (dg * mix * (sig * (1.0 + z * (1.0 - sig)))).astype(bf16)
        skip_o[:, lanes] += jnp.sum(dmix * xs, axis=0, keepdims=True)
        dy = dmix.astype(bf16)
        dy_o[:, lanes] = dy
        dyf = dy.astype(f32)
        inner = inner + pool(dyf * carried, pairs, number)
        weighted[:, lanes] = (dyf * spread(grown, ex, lanes)).astype(bf16)
    inner_o[...] = inner
    last = cum[BLOCK - 1 : BLOCK, :]
    whole = halves_of(jnp.broadcast_to(jnp.exp(last), (16, LANES)))
    whole = spread(whole, ex, slice(0, MINE))[:1]
    exit_o[0] = state[...].astype(bf16)
    factor_o[0] = jnp.broadcast_to(passed[...], (8, MINE))
    state[...] = whole * state[...] + dot_tn(bc[:, STATE:], weighted[...])
    passed[...] = passed[...] * whole
    send_o[0] = state[...].astype(bf16)


def within_back(u, dy, bc, cum, cumt, du_o, dbc_o):
    rows = lax.broadcasted_iota(jnp.int32, (BLOCK, BLOCK), 0)
    columns = lax.broadcasted_iota(jnp.int32, (BLOCK, BLOCK), 1)
    causal = columns >= rows
    products = jnp.where(causal, dot_nt(bc[:, :STATE], bc[:, STATE:]), 0.0)
    lane = lax.broadcasted_iota(jnp.int32, (BLOCK, LANES), 1)
    total = jnp.zeros((BLOCK, BLOCK), f32)
    for pair in range(PAIRS):
        values = u[:, pair * LANES : (pair + 1) * LANES]
        grads = dy[:, pair * LANES : (pair + 1) * LANES]
        made = []
        for half in range(2):
            head = 2 * pair + half
            decay = jnp.exp(jnp.minimum(cumt[0, head : head + 1, :] - cum[:, head : head + 1], 0.0))
            made.append(dot((products * decay).astype(bf16), grads))
            own = jnp.where((lane < HEAD) == (half == 0), values, jnp.zeros_like(values))
            total = total + dot_nt(own, grads) * decay
        made = jnp.where(lane < HEAD, made[0], made[1])
        du_o[:, pair * LANES : (pair + 1) * LANES] = made.astype(bf16)
    total = jnp.where(causal, total, 0.0).astype(bf16)
    dbc_o[:, :STATE] = dot(total, bc[:, STATE:])
    dbc_o[:, STATE:] = dot_tn(total, bc[:, :STATE])


def features_back_kernel(px, kw, heads, pick, tri, ex, pairs, u, dy, du_r, dbc, inner, cum,
                         entering, exit_r, factor, incoming, skip,
                         gp_o, rim_o, tail_o, kw_o, heads_o, after, wide, dpre, raw, held_u,
                         grown_dy):
    j, i = pl.program_id(0), pl.program_id(1)
    block = pl.num_programs(1) - 1 - i

    @pl.when((j == 0) & (i == 0))
    def _():
        kw_o[...] = jnp.zeros_like(kw_o)
        heads_o[...] = jnp.zeros_like(heads_o)

    @pl.when(i == 0)
    def _():
        after[...] = jnp.zeros_like(after)

    rows = conv_rows(px.at[0], block)
    wide[...] = rows[:, :CONVD].astype(f32)
    dpre[BLOCK:, :] = after[...]
    biased, step, log_decay, rate = steps_of(rows[HALO:, CONVD:], heads, pick)
    c = cum[...]
    last = c[BLOCK - 1 : BLOCK, :]
    leaving = exit_r[0].astype(f32) + factor[0][:1] * incoming[0].astype(f32)
    leaving16 = leaving.astype(bf16)
    crossing = jnp.sum(leaving * entering[0].astype(f32), axis=0, keepdims=True)
    crossing = jnp.broadcast_to(crossing, (16, MINE))
    crossing = sum(pool(crossing[:, strip_of(n)], pairs, n) for n in range(PAIRS))
    crossing = crossing[:1] * jnp.exp(last)
    remaining, grown, steps = (halves_of(v) for v in (jnp.exp(last - c), jnp.exp(c), step))
    total, _ = conv_strip(wide, kw, strip_of(PAIRS))
    raw[...] = dot((total * jax.nn.sigmoid(total)).astype(bf16), leaving16)

    def finish(dact, total, sig, taps, lanes):
        value = dact * (sig * (1.0 + total * (1.0 - sig)))
        kw_o[CONV : CONV + 1, lanes] += jnp.sum(value, axis=0, keepdims=True)
        for k in range(CONV):
            kw_o[k : k + 1, lanes] += jnp.sum(value * taps[k], axis=0, keepdims=True)
        dpre[:BLOCK, lanes] = value
        din = sum(
            kw[k : k + 1, lanes] * dpre[CONV - 1 - k : CONV - 1 - k + BLOCK, lanes]
            for k in range(CONV)
        )
        gp_o[0, :, lanes] = din.astype(bf16)

        @pl.when(i == 0)
        def _():
            tail_o[0, :, lanes] = din[BLOCK - 16 :]

    held = jnp.zeros((BLOCK, LANES), f32)
    flow = inner[...]
    dstep = jnp.zeros((BLOCK, LANES), f32)
    for number in range(PAIRS):
        lanes = strip_of(number)
        total, taps = conv_strip(wide, kw, lanes)
        sig = jax.nn.sigmoid(total)
        uf = u[:, lanes].astype(f32)
        dyf = dy[:, lanes].astype(f32)
        left = spread(remaining, ex, lanes)
        du_state = left * raw[:, lanes]
        du_in = du_r[:, lanes].astype(f32)
        held_u[:, lanes] = (uf * left).astype(bf16)
        grown_dy[:, lanes] = (dyf * spread(grown, ex, lanes)).astype(bf16)
        held = held + pool(uf * du_state, pairs, number)
        flow = flow - pool(uf * du_in, pairs, number)
        du = du_in + du_state
        dstep = dstep + pool(du * (total * sig), pairs, number)
        dx = du * spread(steps, ex, lanes) + skip[:, lanes] * dyf
        finish(dx, total, sig, taps, lanes)
    db = dbc[:, :STATE] + dot_nt(held_u[...], leaving16)
    dc = dbc[:, STATE:] + dot_nt(grown_dy[...], entering[0])
    for number, value in enumerate((db, dc)):
        lanes = strip_of(PAIRS + number)
        total, taps = conv_strip(wide, kw, lanes)
        finish(value, total, jax.nn.sigmoid(total), taps, lanes)
    after[...] = dpre[:8, :]
    dlog = crossing + sum(dot_tn(tri[...], part) for part in split3(flow))
    dlog = dlog + sum(dot(tri[...], part) for part in split3(held)) - held
    draw = (dstep - dlog * rate) * jax.nn.sigmoid(biased)
    gp_o[0, :, CONVD:] = dot_nt(draw.astype(bf16), pick[...]).astype(bf16)
    heads_o[0:1, :] += jnp.sum(draw, axis=0, keepdims=True)
    heads_o[1:2, :] += jnp.sum(dlog * log_decay, axis=0, keepdims=True)
    early = jnp.concatenate([jnp.zeros((8, CONVD), f32), dpre[:8, :]], axis=0)
    rim_o[0] = sum(kw[k : k + 1, :] * early[CONV - 1 - k : CONV - 1 - k + 8] for k in range(CONV))


def write_parts(j, mine_o, other_o, value):
    @pl.when(j == 0)
    def _():
        mine_o[...] = value

    @pl.when(j > 0)
    def _():
        other_o[...] = value


def added(*refs):
    return sum(ref.astype(f32) for ref in refs).astype(bf16)


def send_piece_kernel(place, value, out):
    out[...] = jnp.where(place[2] % 2 == 0, value[1], value[0])


def both_pieces_kernel(place, value, got, out):
    side = place[2] % 2
    kept = jnp.where(side == 0, value[0], value[1])
    out[0] = jnp.where(side == 0, kept, got[...])
    out[1] = jnp.where(side == 0, got[...], kept)


def copy_kernel(value, out):
    out[...] = value[...]


def shard_kernel(own, got, out_weight, front_o, late_o):
    r_in, half = own.shape[0], out_weight.shape[0] // 2
    for k, source in enumerate((own, got)):
        front_o[k] = source[:, :FRONT]
        late_o[k, :r_in] = source[:, FRONT:]
        late_o[k, r_in:] = out_weight[k * half : (k + 1) * half]


def pair_kernel(first, second, out):
    count = first.shape[1]
    out[:, :count] = first[...]
    out[:, count:] = second[...]


def halves_kernel(along_x, along_y, x_o, y_o):
    x_o[...] = along_x[0]
    y_o[...] = along_y[0]


def ends_grads_kernel(front, front_got, late, late_got, own_o, send_o, out_o):
    r_in = front.shape[1]
    for k, out in enumerate((own_o, send_o)):
        out[:, :CONVD] = added(front[k], front_got[k])
        out[:, CONVD:] = added(late[k, :r_in], late_got[k, :r_in])
        half = late.shape[1] - r_in
        out_o[k * half : (k + 1) * half] = late[k, r_in:].astype(f32) + late_got[k, r_in:].astype(f32)


def input_grad_kernel(n_dp, place, own, got, sums, out):
    run, first = INNER // n_dp, place[1] == 0
    part = own.shape[0] // 4
    for k in range(n_dp // 2):
        for source, target in ((0, INNER), (CONVD, 0)):
            mine = own[:, source + k * run : source + (k + 1) * run].astype(f32)
            others = got[:, source + k * run : source + (k + 1) * run].astype(f32)
            at = target + 2 * k * run
            out[:, at : at + run] = jnp.where(first, mine, others)
            out[:, at + run : at + 2 * run] = jnp.where(first, others, mine)
    both = own[:, MINE:CONVD].astype(f32) + got[:, MINE:CONVD].astype(f32)
    out[:, 2 * INNER : INNER + XBC] = both
    for k in range(4):
        out[k * part : (k + 1) * part, INNER + XBC :] = sums[8 : 8 + part, k * HEADS : (k + 1) * HEADS]


def sums_kernel(parts, out):
    out[...] = jnp.sum(parts[...], axis=0)


def activations_kernel(place, tokens, keep, got, out):
    value = jnp.where(pl.program_id(0) == place[2] % 2, keep[...], got[...])
    out[0] = (tokens[0].astype(f32) + value.astype(f32)).astype(bf16)


def tokens_grad_kernel(place, tokens, cot, keep, got, norm, out):
    value = jnp.where(pl.program_id(0) == place[2] % 2, keep[...], got[...])
    residual = tokens[0].astype(f32)
    inverse = inverse_rms(residual)
    weighted = value.astype(f32) * norm[...]
    along = jnp.mean(weighted * residual, axis=-1, keepdims=True)
    out[0] = (
        cot[0].astype(f32) + inverse * weighted - residual * (inverse * inverse * inverse * along)
    )


def relative(place, n_ctx, groups):
    for group in range(2):
        for slot in range(n_ctx // 2):
            z = place[2] ^ group ^ (2 * slot)
            at = slot if groups == 2 else group * (n_ctx // 2) + slot
            first = 5 * group if groups == 2 else 0
            for half in range(2):
                for chip in range(3):
                    yield first + chip, (half, at), place[0] ^ chip, z, half
                yield first + 3 + half, (at,), place[0] ^ 3, z, half


def relative_back(place, n_ctx, groups):
    spots = {(0, 0): (0, 0), (0, 1): (0, 1), (1, 1): (1, 1), (2, 0): (2, 1), (1, 0): (3, None),
             (2, 1): (4, None), (3, 1): (1, 0), (3, 0): (2, 0)}
    for group in range(2):
        for slot in range(n_ctx // 2):
            z = place[2] ^ group ^ (2 * slot)
            at = slot if groups == 2 else group * (n_ctx // 2) + slot
            first = 5 * group if groups == 2 else 0
            for (chip, half), (piece, lead) in spots.items():
                index = (at,) if lead is None else (lead, at)
                yield first + piece, index, place[0] ^ chip, z, half


def front_rows(place, n_ctx, chip, z, half, count):
    return pl.multiple_of(((chip * 2 + (place[1] ^ half)) * n_ctx + z) * count, count)


def out_rows(n_ctx, chip, z, half, count):
    return pl.multiple_of(((chip * n_ctx + z) * 2 + half) * count, count)


def front_weights_kernel(n_dp, n_ctx, r_in, place, heads_in, ex, *refs):
    pieces, refs = refs[:-10], refs[-10:]
    front, wide = refs[0], refs[7]
    if len(pieces) == 1:
        front[...] = pieces[0][...]
    else:
        for piece, index, chip, z, half in relative(place, n_ctx, 2):
            begin = front_rows(place, n_ctx, chip, z, half, r_in)
            front[pl.ds(begin, r_in), :] = pieces[piece][index]
    wide[...] = front[:, CONVD:].astype(f32)
    spread_small(n_dp, r_in, place[1], wide, heads_in, ex, *refs[1:7], *refs[8:])


def late_weights_kernel(n_ctx, r_in, place, *refs):
    pieces, gate, out = refs[:-2], refs[-2], refs[-1]
    r_out = pieces[0].shape[2] - r_in
    for piece, index, chip, z, half in relative(place, n_ctx, 1):
        block = pieces[piece][index]
        gate[pl.ds(front_rows(place, n_ctx, chip, z, half, r_in), r_in), :] = block[:r_in]
        out[pl.ds(out_rows(n_ctx, chip, z, half, r_out), r_out), :] = block[r_in:]


def middle_kernel(n_ctx, r_in, place, normed, dz, scaled, cot_mine, cot_other, wo, u, dy, bc, cum, cumt, *refs):
    mine_o, other_o, du_o, dbc_o = refs[:4]
    outputs, (gate, out) = refs[4:-2], refs[-2:]
    j, i = pl.program_id(0), pl.program_id(1)
    within_back(u, dy, bc, cum, cumt, du_o, dbc_o)
    step = j * pl.num_programs(1) + i
    cot = jnp.where(j == 0, cot_mine[...], cot_other[...])
    write_parts(j, mine_o, other_o, dot(scaled[...], wo[...]).astype(bf16))
    gate_part, out_part = dot_tn(normed[...], dz[...]), dot_tn(scaled[...], cot)

    @pl.when(step == 0)
    def _():
        gate[...] = gate_part
        out[...] = out_part

    @pl.when(step > 0)
    def _():
        gate[...] += gate_part
        out[...] += out_part

    @pl.when(step == pl.num_programs(0) * pl.num_programs(1) - 1)
    def _():
        if len(outputs) == 2:
            outputs[0][...] = gate[...].astype(bf16)
            outputs[1][...] = out[...].astype(bf16)
            return
        r_out = outputs[0].shape[2] - r_in
        for piece, index, chip, z, half in relative_back(place, n_ctx, 1):
            begin = front_rows(place, n_ctx, chip, z, half, r_in)
            outputs[piece][index + (slice(0, r_in),)] = gate[pl.ds(begin, r_in), :].astype(bf16)
            begin = out_rows(n_ctx, chip, z, half, r_out)
            outputs[piece][index + (slice(r_in, r_in + r_out),)] = out[
                pl.ds(begin, r_out), :
            ].astype(bf16)


def with_rim(gp, tail, rim, whole):
    whole[...] = gp[0]
    late = tail[0] + jnp.concatenate([jnp.zeros((8, CONVD), f32), rim[0]], axis=0)
    whole[whole.shape[0] - 16 :, :CONVD] = late.astype(bf16)


def front_grads_kernel(n_ctx, r_in, place, normed, gp, tail, rim, step_o, *refs):
    outputs, (total, whole) = refs[:-2], refs[-2:]
    j = pl.program_id(0)
    with_rim(gp, tail, rim, whole)
    part = dot_tn(normed[...], whole[...])

    @pl.when(j == 0)
    def _():
        total[...] = part

    @pl.when(j > 0)
    def _():
        total[...] += part

    @pl.when(j == pl.num_programs(0) - 1)
    def _():
        step_o[...] = total[:, CONVD:]
        if len(outputs) == 1:
            outputs[0][...] = total[:, :CONVD].astype(bf16)
            return
        for piece, index, chip, z, half in relative_back(place, n_ctx, 1):
            begin = front_rows(place, n_ctx, chip, z, half, r_in)
            outputs[piece][index] = total[pl.ds(begin, r_in), :CONVD].astype(bf16)


def normed_grads_kernel(mine, other, dz, wg, gp, tail, rim, front, mine_o, other_o, norm_o, whole):
    j = pl.program_id(0)
    with_rim(gp, tail, rim, whole)
    back = dot_nt(dz[...], wg[...]) + dot_nt(whole[...], front[...])
    write_parts(j, mine_o, other_o, back.astype(bf16))
    residual = jnp.where(j == 0, mine[...], other[...]).astype(f32)

    @pl.when(j == 0)
    def _():
        norm_o[...] = jnp.zeros_like(norm_o)

    norm_o[...] += jnp.sum(back * (residual * inverse_rms(residual)), axis=0, keepdims=True)


def small_place(n, k, r_in, n_all):
    rows = min(r_in, 8)
    span = (LANES - HEADS) // -(-7 // rows)
    width = (XBC // n_all,) * 5 + (INNER // n_all, r_in)
    return n * r_in + k % rows, HEADS + (k // rows) * span, width[k]


def prepare_kernel(n_dp, n_all, place, weight, vectors, own_o, other_o):
    r_in, run, first = weight.shape[0], INNER // n_dp, place[1] == 0
    for k in range(n_dp // 2):
        for source, target in ((INNER, 0), (0, FRONT)):
            low = weight[:, source + 2 * k * run : source + (2 * k + 1) * run]
            high = weight[:, source + (2 * k + 1) * run : source + (2 * k + 2) * run]
            at = target + k * run
            own_o[:, at : at + run] = jnp.where(first, low, high)
            other_o[:, at : at + run] = jnp.where(first, high, low)
    row = lax.broadcasted_iota(jnp.int32, (r_in, LANES), 0)
    small = jnp.concatenate(
        [weight[:, INNER + XBC :].astype(f32), jnp.zeros((r_in, LANES - HEADS), f32)], axis=1
    )
    at = 0
    for k in range(7):
        line, lane, count = small_place(0, k, r_in, n_all)
        piece = vectors[:, at : at + count].astype(f32)
        parts = [jnp.zeros((1, lane), f32), piece, jnp.zeros((1, LANES - lane - count), f32)]
        small = small + jnp.where(row == line, jnp.concatenate(parts, axis=1), 0.0)
        at += count
    for out in (own_o, other_o):
        out[:, MINE:CONVD] = weight[:, 2 * INNER : INNER + XBC]
        out[:, CONVD:FRONT] = small.astype(bf16)


def spread_small(n_dp, r_in, core, wide, heads_in, ex, kw_o, gain_o, norm_o, heads_o, skip_o, pick_o,
                 full, gains):
    n_all = wide.shape[0] // r_in
    run, heads_run, first = INNER // n_dp, HEADS // n_dp, core == 0
    full[...] = jnp.zeros_like(full)
    for n in range(n_all):
        for k in range(7):
            row, lane, count = small_place(n, k, r_in, n_all)
            target, at = ((full, k), (gains, 0), (norm_o, 0))[max(k - CONV, 0)]
            target[at : at + 1, n * count : (n + 1) * count] = wide[row : row + 1, lane : lane + count]
    for k in range(n_dp // 2):
        low, high = 2 * k * run, (2 * k + 1) * run
        kw_o[:, k * run : (k + 1) * run] = jnp.where(
            first, full[:, low : low + run], full[:, high : high + run]
        )
        gain_o[:, k * run : (k + 1) * run] = jnp.where(
            first, gains[:, low : low + run], gains[:, high : high + run]
        )
    kw_o[:, MINE:] = full[:, INNER:]
    source = lax.broadcasted_iota(jnp.int32, (LANES, LANES), 0)
    local = lax.broadcasted_iota(jnp.int32, (LANES, LANES), 1)
    position = ((local // heads_run) * 2 + core) * heads_run + local % heads_run
    chosen = (source == position) & (local < HEADS // 2)
    pick = jnp.where(chosen, 1.0, 0.0).astype(bf16)
    pick_o[...] = pick
    heads = dot(heads_in[...].astype(bf16), pick)
    row = lax.broadcasted_iota(jnp.int32, (8, LANES), 0)
    lane = lax.broadcasted_iota(jnp.int32, (8, LANES), 1)
    rate = jnp.where(lane < HEADS // 2, jnp.exp(heads), 0.0)
    heads_o[...] = jnp.where(row == 1, rate, heads)
    skip_o[...] = dot(heads.astype(bf16), ex[:LANES, :])[2:3]


def pack_kernel(n_dp, place, norm_sum, kw_sum, gain_sum, heads_sum, skip_sum, step_sum, pick, pairs,
                packed_o, full, gains):
    n_all = packed_o.shape[0]
    taps_n, gain_n, norm_n = XBC // n_all, INNER // n_all, norm_sum.shape[1] // n_all
    part, run = norm_n // 4, INNER // n_dp
    keep = [jnp.where(place[1] == which, 1.0, 0.0) for which in range(2)]
    for k in range(n_dp // 2):
        for which in range(2):
            begin = (2 * k + which) * run
            full[:, begin : begin + run] = kw_sum[:, k * run : (k + 1) * run] * keep[which]
            gains[:, begin : begin + run] = gain_sum[:, k * run : (k + 1) * run] * keep[which]
    full[:, INNER:] = kw_sum[:, MINE:]
    skips = jnp.broadcast_to(skip_sum[...], (16, MINE))
    skips = sum(pool(skips[:, strip_of(n)], pairs, n) for n in range(PAIRS))[:8]
    row = lax.broadcasted_iota(jnp.int32, (8, LANES), 0)
    heads = jnp.where(row == 2, skips, heads_sum[...])
    heads = sum(dot_nt(piece, pick[...]) for piece in split3(heads))
    packed_o[...] = jnp.zeros_like(packed_o)
    for n in range(n_all):
        packed_o[n, 0:5, :taps_n] = full[0:5, n * taps_n : (n + 1) * taps_n]
        packed_o[n, 5:6, :gain_n] = gains[:, n * gain_n : (n + 1) * gain_n]
        packed_o[n, 6:7, :norm_n] = norm_sum[:, n * norm_n : (n + 1) * norm_n]
        for k in range(3):
            packed_o[n, 7:8, k * HEADS : (k + 1) * HEADS] = heads[k : k + 1, :HEADS]
        for k in range(4):
            begin = n * norm_n + k * part
            packed_o[n, 8 : 8 + part, k * HEADS : (k + 1) * HEADS] = step_sum[
                begin : begin + part, :HEADS
            ]


def call(kernel, grid, in_specs, out_specs, out_shape, scratch=(), cost=0, needs=(), vmem=20):
    count = len(in_specs)

    def body(*refs):
        kernel(*refs[:count], *refs[count + len(needs) :])

    made = pl.pallas_call(
        body,
        grid=grid,
        in_specs=list(in_specs) + [pl.BlockSpec(memory_space=pl.ANY)] * len(needs),
        out_specs=out_specs,
        out_shape=out_shape,
        scratch_shapes=scratch,
        cost_estimate=pl.CostEstimate(
            flops=int(1 + cost * 1e9), transcendentals=0, bytes_accessed=int(1 + cost * 3.5e6)
        ),
        compiler_params=pltpu.CompilerParams(
            vmem_limit_bytes=vmem << 20, dimension_semantics=("arbitrary",) * len(grid)
        ),
    )
    return lambda *arrays: made(*arrays, *needs)


def sds(shape, dtype=f32):
    return jax.ShapeDtypeStruct(shape, dtype)


def main(value):
    return pltpu.with_memory_space_constraint(value, pltpu.HBM)


def on_device(
    tokens,
    cotangent,
    norm_weight,
    input_weight,
    kernel_weight,
    kernel_bias,
    step_bias,
    decay_log,
    skip_gain,
    gate_norm_weight,
    output_weight,
):
    n_dp, n_ctx = lax.axis_size("dp"), lax.axis_size("ctx")
    n_q, n_all = n_dp // 2, n_dp * n_ctx
    place, z = lax.axis_index("dp"), lax.axis_index("ctx")
    q, core = place >> 1, place & 1
    seqs, piece, width = tokens.shape
    length = 2 * piece
    blocks = length // BLOCK
    rows = seqs * length
    r_in, r_out = input_weight.shape[0], output_weight.shape[0]
    every = ("dp", "ctx")
    fast = n_q == 4 and n_ctx == 4 and r_in % 16 == 0
    where = jnp.stack([q, core, z]).astype(jnp.int32)
    smem = pl.BlockSpec(memory_space=pltpu.SMEM)

    def lanes(value, count, wide=LANES):
        return jnp.pad(value, ((0, count - value.shape[0]), (0, wide - value.shape[1])))

    def all_of(arrays):
        return [pl.BlockSpec(v.shape, lambda *_, n=len(v.shape): (0,) * n) for v in arrays]

    def once(kernel, arrays, made, scratch=(), cost=0, needs=(), placed=False):
        specs = ([smem] if placed else []) + all_of(arrays)
        single = not isinstance(made, list)
        outs = all_of([made])[0] if single else all_of(made)
        run = call(kernel, (1,), specs, outs, made, scratch, cost, needs)
        return run(*([where] if placed else []), *arrays)

    cuts = 2
    cut_s = pl.BlockSpec((piece // cuts, width), lambda i: (i, 0))
    both_cut_s = pl.BlockSpec((2, piece // cuts, width), lambda i: (0, i, 0))

    def piece_to_send(value, needs=()):
        made = sds((piece, width), bf16)
        run = call(send_piece_kernel, (cuts,), [smem, both_cut_s], cut_s, made, needs=needs)
        return run(where, value)

    def enter_line(value, send, needs=(), cost=0):
        made, got = sds((2, piece, width), bf16), swap(send, "ctx", 1)
        specs = [smem, both_cut_s, cut_s]
        run = call(both_pieces_kernel, (cuts,), specs, both_cut_s, made, (), cost, needs)
        return run(where, value, got).reshape(length, width)

    def leave_cores(mine, other, needs=()):
        total = add(after(mine, *needs), swap(other, "dp", 1)).reshape(2, piece, width)
        return choose(total, z & 1, 0), choose(total, 1 - (z & 1), 0)


    tokens_send = piece_to_send(tokens)
    vectors = jnp.concatenate([kernel_weight.reshape(-1), kernel_bias, gate_norm_weight, norm_weight])
    own_columns, other_columns = once(
        functools.partial(prepare_kernel, n_dp, n_all),
        [input_weight, vectors[None]],
        [sds((r_in, FRONT + MINE), bf16)] * 2,
        cost=8,
        needs=[tokens_send],
        placed=True,
    )
    got = swap(other_columns, "dp", 1)
    half = r_in + r_out // 2
    if fast:
        front_shard, late_shard = once(
            shard_kernel,
            [own_columns, got, output_weight],
            [sds((2, r_in, FRONT), bf16), sds((2, half, width), bf16)],
        )

        def pair(first, second, needs=(), cost=0):
            first, second = (v.reshape((2, -1) + v.shape[-2:]) for v in (first, second))
            count = first.shape[1] + second.shape[1]
            made = sds((2, count) + first.shape[2:], bf16)
            specs = [
                pl.BlockSpec((1,) + v.shape[1:], lambda k: (k, 0, 0, 0)) for v in (first, second, made)
            ]
            run = call(pair_kernel, (2,), specs[:2], specs[2], made, (), cost, needs)
            return run(first, second)

        def across_parts(along_x, along_y, needs=()):
            made = [sds(along_x.shape[1:], bf16)] * 2
            block = (1, 1) + along_x.shape[2:]
            specs = [
                pl.BlockSpec(block, lambda i, half=half: (half, i, 0, 0)) for half in range(2)
            ]
            outs = [pl.BlockSpec(block[1:], lambda i: (i, 0, 0))] * 2
            run = call(halves_kernel, along_x.shape[1:2], specs, outs, made, (), 0, needs)
            return run(along_x, along_y)

        def across_of(send_y, send_x):
            return swap(send_y, "dp", 4), swap(send_x, "dp", 2)

        first_got = swap(front_shard, "ctx", 2)
        inside = enter_line(tokens, tokens_send, needs=[front_shard], cost=8)
        other = swap(inside, "dp", 1)
        end_s = pl.BlockSpec((HALO, width), lambda i: (length // HALO - 1, 0))
        made = sds((HALO, width), bf16)
        ends = call(copy_kernel, (1,), [end_s], all_of([made])[0], made)(inside)
        before = hop(ends, 2)
        near = pair(front_shard, first_got, needs=[ends])
        sides = sides_of(near)
        far = swap(near, "ctx", 1)
        late_shard = after(late_shard, near)
        late_got = swap(late_shard, "ctx", 2)
        across = across_of(*across_parts(*sides, needs=[far, before]))
        far = after(far, *across)
        far_sides = sides_of(far)
        late_near = pair(late_shard, late_got, needs=[far], cost=8)
        far_across_send = across_parts(*far_sides, needs=[late_near])
        far_across = across_of(*far_across_send)
        late_far = swap(late_near, "ctx", 1)
        before_other = swap(before, "dp", 1)
        late_own = after(pair(late_near, late_far, needs=far_across_send, cost=8), *far_across)
        front_pieces = [near, *sides, *across, far, *far_sides, *far_across]
    else:
        shard = ordered(own_columns, got, core, 0)
        near = gather_line(shard[:, :, :FRONT], z, n_ctx, 1)
        far = swap(near, "ctx", 1)
        halves = gather_rest(near, far, z, n_ctx, q, n_q)
        front_pieces = [jnp.stack(halves, axis=1).reshape(width, FRONT)]
        inside = enter_line(tokens, tokens_send)
        other = swap(inside, "dp", 1)
        before = hop(inside[length - HALO :], 2)
        before_other = swap(before, "dp", 1)
        out_halves = output_weight.reshape(2, r_out // 2, width)
        late_shard = jnp.concatenate([shard[:, :, FRONT:], out_halves], axis=1)
        late_near = gather_line(late_shard, z, n_ctx, 1)
        late_far = swap(late_near, "ctx", 1)
        first, second = gather_rest(late_near, late_far, z, n_ctx, q, n_q)
        w_gate = jnp.stack([first[:, :, :r_in], second[:, :, :r_in]], axis=1).reshape(width, MINE)
        w_out = jnp.stack([first[:, :, r_in:], second[:, :, r_in:]], axis=2).reshape(MINE, width)

    ex = np.arange(LANES)[:, None] == (np.arange(MINE)[None] // HEAD)
    ex = ex.astype(ml_dtypes.bfloat16)
    pairs = [ex[:, strip_of(n)] for n in range(PAIRS) for _ in range(2)]
    pairs = jnp.asarray(np.concatenate(pairs, axis=1))
    ex = jnp.asarray(np.concatenate([ex, ex], axis=0))
    tri = np.arange(BLOCK)[:, None] >= np.arange(BLOCK)[None]
    tri = jnp.asarray(tri.astype(ml_dtypes.bfloat16))
    heads_in = lanes(jnp.stack([step_bias, decay_log, skip_gain]).astype(f32), 8)
    w_front, kw, gain, norm_full, heads, skip, pick = once(
        functools.partial(front_weights_kernel, n_dp, n_ctx, r_in),
        [heads_in, ex, *map(main, front_pieces)],
        [pltpu.HBM((width, FRONT), bf16), sds((8, CONVD)), sds((1, MINE)), sds((1, width)),
         sds((8, LANES)), sds((1, MINE)), sds((LANES, LANES), bf16)],
        [pltpu.VMEM((width, LANES), f32), pltpu.VMEM((8, XBC), f32), pltpu.VMEM((1, INNER), f32)],
        cost=8,
        needs=[late_own, before_other] if fast else (),
        placed=True,
    )
    if fast:
        late_sides = sides_of(late_own)
    cot_send = piece_to_send(cotangent, needs=[w_front])

    grid = (seqs, blocks)

    def here(shape, back=False):
        lead = len(shape)
        if back:
            return pl.BlockSpec(shape, lambda j, i: (j * blocks + blocks - 1 - i,) + (0,) * (lead - 1))
        return pl.BlockSpec(shape, lambda j, i: (j * blocks + i,) + (0,) * (lead - 1))

    def per_seq(shape):
        return pl.BlockSpec(shape, lambda j, i: (j,) + (0,) * (len(shape) - 1))

    def fixed(shape):
        return pl.BlockSpec(shape, lambda j, i: (0,) * len(shape))

    mine_s = pl.BlockSpec((BLOCK, width), lambda j, i: (i * (1 - j) + (blocks - 1) * j, 0))
    other_s = pl.BlockSpec((BLOCK, width), lambda j, i: (i * j, 0))
    part_s = sds((length, width), bf16)
    steps_n = seqs * blocks
    wide, heads_s, both = (BLOCK, MINE), (BLOCK, LANES), (BLOCK, 2 * STATE)
    state_s, row8 = (1, STATE, MINE), (1, 8, MINE)
    conv_specs = [
        fixed((8, CONVD)),
        fixed((8, LANES)),
        fixed((LANES, LANES)),
        fixed((BLOCK, BLOCK)),
        fixed((2 * LANES, MINE)),
        fixed((LANES, 2 * MINE)),
    ]
    conv_args = (kw, heads, pick, tri, ex, pairs)
    ext_front = per_seq((1, length + HALO, FRONT))
    front_s = fixed((width, FRONT))
    whole_s, halo_s = fixed((length, width)), fixed((HALO, width))
    normed, px, x, u, bc, cum, cumt, entry, entry_factor, state_total, state_decay = call(
        features_kernel,
        grid,
        [whole_s, whole_s, halo_s, halo_s, fixed((1, width)), front_s] + conv_specs,
        [here((BLOCK, width)), ext_front, here(wide), here(wide), here(both), here(heads_s),
         here((1, LANES, BLOCK)), here(state_s), here(row8), per_seq(state_s), per_seq(row8)],
        [pltpu.HBM((rows, width), bf16), pltpu.HBM((seqs, length + HALO, FRONT), bf16),
         pltpu.HBM((rows, MINE), bf16), pltpu.HBM((rows, MINE), bf16),
         pltpu.HBM((rows, 2 * STATE), bf16), pltpu.HBM((rows, LANES)  , f32),
         pltpu.HBM((steps_n, LANES, BLOCK), f32), pltpu.HBM((steps_n, STATE, MINE), bf16), sds((steps_n, 8, MINE)),
         sds((seqs, STATE, MINE), bf16), sds((seqs, 8, MINE))],
        [pltpu.VMEM((STATE, MINE), f32), pltpu.VMEM((1, MINE), f32),
         pltpu.VMEM((BLOCK + HALO, CONVD), f32), pltpu.VMEM((BLOCK, MINE), bf16)],
        cost=16,
        needs=[cot_send],
    )(main(inside), main(other), before, before_other, norm_full, main(w_front), *conv_args)

    cot = enter_line(cotangent, cot_send, needs=[state_total])
    cot_other = swap(cot, "dp", 1)

    def relay(local, decay, steps):
        received = hop(local, steps)
        for _ in range(n_ctx // 2 - 2):
            received = hop((decay[:, :1] * received.astype(f32) + local.astype(f32)).astype(bf16), steps)
        return received

    incoming = relay(state_total, state_decay, 2)
    late_across_send = across_parts(*late_sides, needs=[cot]) if fast else ()
    y = call(
        within_kernel,
        grid,
        [here(wide), here(both), here(heads_s), here((1, LANES, BLOCK))],
        here(wide),
        sds((rows, MINE), bf16),
        cost=8,
        needs=late_across_send,
    )(u, bc, cum, cumt)

    if fast:
        late_across = across_of(*late_across_send)
        w_gate, w_out = once(
            functools.partial(late_weights_kernel, n_ctx, r_in),
            [*map(main, (late_own, *late_sides, *late_across))],
            [sds((width, MINE), bf16), sds((MINE, width), bf16)],
            placed=True,
            needs=[y],
        )

    mix, gate_raw, ds, entering, sums = call(
        gate_kernel,
        grid,
        [here((BLOCK, width)), mine_s, other_s, fixed((width, MINE)),
         fixed((MINE, width)), here(wide), here(wide), here(both), here(heads_s),
         here(state_s), here(row8), per_seq(state_s), fixed((1, MINE)), fixed((1, MINE)),
         fixed((2 * LANES, MINE))],
        [here(wide), here(wide), here(wide), here(state_s),
         pl.BlockSpec((8, BLOCK), lambda j, i: (0, j * blocks + i))],
        [pltpu.HBM((rows, MINE), bf16)] * 3
        + [pltpu.HBM((steps_n, STATE, MINE), bf16), sds((8, rows))],
        cost=16,
    )(normed, cot, cot_other, w_gate, w_out, y, x, bc, cum, entry, entry_factor, incoming, skip, gain, ex)
    sums_got = swap(sums, "dp", 1)

    scaled, dy, dz, inner, leaving, leave_factor, grad_send, gain_sum, skip_sum = call(
        mixture_kernel,
        grid,
        [here(wide, True)] * 4
        + [here(both, True), here(heads_s, True)]
        + [pl.BlockSpec((8, BLOCK), lambda j, i: (0, j * blocks + blocks - 1 - i)),
           pl.BlockSpec((8, BLOCK), lambda j, i: (0, (1 - j) * blocks + blocks - 1 - i))]
        + [fixed((1, MINE)), fixed((1, MINE)), fixed((2 * LANES, MINE)), fixed((LANES, 2 * MINE))],
        [here(wide, True)] * 3
        + [here(heads_s, True), here(state_s, True), here(row8, True), per_seq(state_s),
           fixed((1, MINE)), fixed((1, MINE))],
        [sds((rows, MINE), bf16)] * 3
        + [sds((rows, LANES)), sds((steps_n, STATE, MINE), bf16), sds((steps_n, 8, MINE)),
           sds((seqs, STATE, MINE), bf16), sds((1, MINE)), sds((1, MINE))],
        [pltpu.VMEM((STATE, MINE), f32), pltpu.VMEM((1, MINE), f32), pltpu.VMEM((BLOCK, MINE), bf16)],
        cost=12,
    )(*map(main, (mix, gate_raw, ds, x, bc, cum)), sums, sums_got, skip, gain, ex, pairs)
    grad_incoming = relay(grad_send, state_decay, -2)

    def parts_of(rows_n, columns):
        wide_part, narrow = (2, n_ctx, rows_n, columns), (n_ctx, rows_n, columns)
        return [sds(shape, bf16) for shape in [wide_part] * 3 + [narrow] * 2]

    made = parts_of(half, width) if fast else [sds((width, MINE), bf16), sds((MINE, width), bf16)]
    out_mine, out_other, du, dbc, *late_parts = call(
        functools.partial(middle_kernel, n_ctx, r_in),
        grid,
        [smem, here((BLOCK, width)), here(wide), here(wide), mine_s, other_s, fixed((MINE, width)),
         here(wide), here(wide), here(both), here(heads_s), here((1, LANES, BLOCK))],
        [mine_s, other_s, here(wide), here(both)] + all_of(made),
        [part_s, part_s, sds((rows, MINE), bf16), sds((rows, 2 * STATE))] + made,
        [pltpu.VMEM((width, MINE), f32), pltpu.VMEM((MINE, width), f32)],
        cost=24,
    )(where, normed, dz, scaled, cot, cot_other, w_out, u, dy, bc, cum, cumt)

    def join_of(along_x, along_y, got_x, got_y, needs=()):
        return add(after(along_x, *needs), got_y[0]), add(along_y, got_x[0])

    def own_of(own, got_x, got_y, last_x, last_y, needs=()):
        own = after(own, *needs)
        far_n = n_ctx // 2
        return [
            jnp.stack(
                [
                    add(own[0, part], got_y[1, part], last_x[part]),
                    add(own[1, part], got_x[1, part], last_y[part]),
                ]
            )
            for part in (slice(0, far_n), slice(far_n, n_ctx))
        ]

    def fold_of(near_part, got):
        return [add(near_part[:, slot], got[:, slot]) for slot in range(2)]

    if fast:
        late_first = swap(late_parts[1], "dp", 2), swap(late_parts[2], "dp", 4)

    gp, rim, tail, kw_sum, heads_sum = call(
        features_back_kernel,
        grid,
        [ext_front]
        + conv_specs
        + [here(wide, True), here(wide, True), here(wide, True), here(both, True),
           here(heads_s, True), here(heads_s, True), here(state_s, True), here(state_s, True),
           here(row8, True), per_seq(state_s), fixed((1, MINE))],
        [pl.BlockSpec((1, BLOCK, FRONT), lambda j, i: (j, blocks - 1 - i, 0)),
         per_seq((1, 8, CONVD)), per_seq((1, 16, CONVD)), fixed((8, CONVD)), fixed((8, LANES))],
        [pltpu.HBM((seqs, length, FRONT), bf16), sds((seqs, 8, CONVD)),
         sds((seqs, 16, CONVD)), sds((8, CONVD)), sds((8, LANES))],
        [pltpu.VMEM((8, CONVD), f32), pltpu.VMEM((BLOCK + HALO, CONVD), f32),
         pltpu.VMEM((BLOCK + 8, CONVD), f32), pltpu.VMEM((BLOCK, MINE), f32),
         pltpu.VMEM((BLOCK, MINE), bf16), pltpu.VMEM((BLOCK, MINE), bf16)],
        cost=24,
    )(px, *conv_args, u, dy, du, dbc, inner, cum, entering, leaving, leave_factor, grad_incoming, skip)

    out_keep, out_send = leave_cores(out_mine, out_other, needs=[gp])
    out_got = swap(out_send, "ctx", 1)
    rim = hop(rim, -2)
    if fast:
        late_second = join_of(late_parts[3], late_parts[4], *late_first, needs=[gp])
        late_last = sides_of_each(*late_second)
    seq_wide = pl.BlockSpec((length, MINE), lambda j: (j, 0))
    seq_gp = pl.BlockSpec((1, length, FRONT), lambda j: (j, 0, 0))
    rims = [pl.BlockSpec((1, n, CONVD), lambda j: (j, 0, 0)) for n in (16, 8)]
    back_mine, back_other, norm_sum = call(
        normed_grads_kernel,
        (seqs,),
        all_of([inside, other]) + [seq_wide] + all_of([w_gate]) + [seq_gp] + rims + all_of([w_front]),
        all_of([part_s, part_s, sds((1, width))]),
        [part_s, part_s, sds((1, width))],
        [pltpu.VMEM((length, FRONT), bf16)],
        cost=12,
        needs=[*late_second, out_send] if fast else (),
    )(*map(main, (inside, other, dz, w_gate, gp)), tail, rim, main(w_front))
    if fast:
        late_near, late_far = own_of(late_parts[0], *late_first, *late_last, needs=[back_mine])
        late_got = swap(late_far, "ctx", 1)
    made = parts_of(r_in, CONVD) if fast else [sds((width, CONVD), bf16)]
    d_step, *front_parts = call(
        functools.partial(front_grads_kernel, n_ctx, r_in),
        (seqs,),
        [smem, seq_wide, seq_gp] + rims,
        all_of([sds((width, LANES))] + made),
        [sds((width, LANES))] + made,
        [pltpu.VMEM((width, FRONT), f32), pltpu.VMEM((length, FRONT), bf16)],
        cost=10,
        needs=[late_far] if fast else (),
    )(where, main(normed), main(gp), tail, rim)
    if fast:
        front_first = swap(front_parts[1], "dp", 2), swap(front_parts[2], "dp", 4)
    back_keep, back_send = leave_cores(back_mine, back_other, needs=[d_step])
    back_got = swap(back_send, "ctx", 1)

    def finish(kernel, arrays, more, dtype, needs, cost):
        block_s = pl.BlockSpec((1, piece, width), lambda j: (j, 0, 0))
        specs = [smem] + [block_s] * len(arrays) + all_of(more)
        made = sds((seqs, piece, width), dtype)
        return call(kernel, (seqs,), specs, block_s, made, (), cost, needs)(where, *arrays, *more)

    packed = once(
        functools.partial(pack_kernel, n_dp),
        [norm_sum, kw_sum, gain_sum, heads_sum, skip_sum, d_step, pick, pairs],
        sds((n_all, 16, LANES)),
        [pltpu.VMEM((8, XBC), f32), pltpu.VMEM((1, INNER), f32)],
        cost=8,
        needs=[back_send],
        placed=True,
    )
    packed_got = lax.all_to_all(packed, every, 0, 0)
    activations = finish(
        activations_kernel, [tokens], [out_keep, out_got], bf16, [packed], 8
    )
    if fast:
        front_second = join_of(front_parts[3], front_parts[4], *front_first, needs=[activations])
        front_last = sides_of_each(*front_second)
        late_keep, late_send = fold_of(late_near, late_got)
        late_got = swap(late_send, "ctx", 2)
    tokens_grad = finish(
        tokens_grad_kernel,
        [tokens, cotangent],
        [back_keep, back_got, norm_full],
        f32,
        [*front_second] if fast else (),
        8,
    )
    if fast:
        front_near, front_far = own_of(
            front_parts[0], *front_first, *front_last, needs=[tokens_grad]
        )
        front_keep, front_send = fold_of(front_near, swap(front_far, "ctx", 1))
        front_got = swap(front_send, "ctx", 2)
    sums = once(
        sums_kernel, [packed_got], sds((16, LANES)), needs=[front_send] if fast else (), cost=8
    )
    if fast:
        own, send, output_weight_grad = once(
            ends_grads_kernel,
            [front_keep, front_got, late_keep, late_got],
            [sds((r_in, CONVD + MINE), bf16)] * 2 + [sds((r_out, width))],
            needs=[sums],
        )
    else:
        d_gate, d_out = late_parts
        d_out = d_out.reshape(n_q, n_ctx, 2, r_out // 2, width)
        d_gate = d_gate.reshape(n_q, 2, n_ctx, r_in, MINE)
        halves = [
            jnp.concatenate([d_gate[:, which], d_out[:, :, which]], axis=2) for which in range(2)
        ]
        late = scatter_both(*halves, z, n_ctx, q, n_q)
        d_conv = front_parts[0].reshape(n_q, 2, n_ctx, r_in, CONVD)
        early = scatter_both(d_conv[:, 0], d_conv[:, 1], z, n_ctx, q, n_q)
        both_cores = jnp.concatenate([early, late[:, :r_in]], axis=2)
        own, send = choose(both_cores, core, 0), choose(both_cores, 1 - core, 0)
        output_weight_grad = late[:, r_in:].reshape(r_out, width).astype(f32)
    got = swap(send, "dp", 1)
    input_weight_grad = once(
        functools.partial(input_grad_kernel, n_dp),
        [own, got, sums],
        sds((r_in, INNER + XBC + HEADS)),
        placed=True,
    )
    head_sums = sums[7, : 3 * HEADS].reshape(3, HEADS)
    return (
        activations,
        tokens_grad,
        sums[6, :r_in],
        input_weight_grad,
        sums[:CONV, : XBC // n_all],
        sums[CONV, : XBC // n_all],
        head_sums[0],
        head_sums[1],
        head_sums[2],
        sums[5, : INNER // n_all],
        output_weight_grad,
    )


def solution(mesh):
    data, rows_spec, vector = P("dp", "ctx", None), P(("dp", "ctx"), None), P(("dp", "ctx"))
    taps = P(None, ("dp", "ctx"))
    return jax.shard_map(
        on_device,
        mesh=mesh,
        in_specs=(data, data, vector, rows_spec, taps, vector, P(), P(), P(), vector, rows_spec),
        out_specs=(data, data, vector, rows_spec, taps, vector, P(), P(), P(), vector, rows_spec),
        check_vma=False,
    )
```

```python
import functools

import jax
import jax.numpy as jnp
import ml_dtypes
import numpy as np
from jax import lax
from jax.experimental import pallas as pl
from jax.experimental.pallas import tpu as pltpu
from jax.sharding import PartitionSpec as P

HEADS = 32
HEAD = 64
STATE = 128
CONV = 4
INNER = 2048
XBC = 2304
BLOCK = 256
HALO = 16
LANES = 128
TILE = 128
DEEP = BLOCK // 8
AHEAD = 8 * (CONV - 1)
MINE = INNER // 2
PAIRS = MINE // LANES
CONVD = MINE + 2 * STATE
FRONT = CONVD + LANES

epsilon = 1e-05
bf16 = jnp.bfloat16
f32 = jnp.float32


def swap(value, axis, mask):
    count = lax.axis_size(axis)
    return lax.ppermute(value, axis, [(i, i ^ mask) for i in range(count)])


def hop(value, steps):
    count = lax.axis_size("ctx")
    pairs = [(i, i + steps) for i in range(count) if 0 <= i + steps < count]
    return lax.ppermute(value, "ctx", pairs)


def ordered(own, other, bit, place):
    first = bit == 0
    return jnp.stack([jnp.where(first, own, other), jnp.where(first, other, own)], axis=place)


def choose(value, index, place):
    return lax.dynamic_index_in_dim(value, index, place, keepdims=False)


def bits_of(count):
    return range(count.bit_length() - 1)


def gather_line(shard, z, n_ctx, least=0):
    grown = shard
    for place, bit in enumerate(reversed(range(least, n_ctx.bit_length() - 1))):
        grown = ordered(grown, swap(grown, "ctx", 1 << bit), (z >> bit) & 1, place)
    return grown.reshape((n_ctx >> least,) + shard.shape)


def gather_plane(first, second, q, n_q):
    bits = list(bits_of(n_q))
    shape = first.shape
    for step, bit in enumerate(bits):
        back = bits[len(bits) - 1 - step]
        other = swap(first, "dp", 2 << bit)
        other_second = swap(second, "dp", 2 << back)
        first = ordered(first, other, (q >> bit) & 1, 0)
        second = ordered(second, other_second, (q >> back) & 1, step)
    return first.reshape((n_q,) + shape), second.reshape((n_q,) + shape)


def fold(value, axis, mask, bit, place):
    got = swap(choose(value, 1 - bit, place), axis, mask)
    return (choose(value, bit, place).astype(f32) + got.astype(f32)).astype(bf16)


def scatter_plane(first, second, q, n_q):
    bits = list(bits_of(n_q))
    rest = first.shape[1:]
    left = n_q
    for step, bit in enumerate(bits):
        back = bits[len(bits) - 1 - step]
        left //= 2
        first = fold(
            first.reshape((2, left) + rest), "dp", 2 << back, (q >> back) & 1, 0
        )
        second = fold(
            second.reshape((left, 2) + rest), "dp", 2 << bit, (q >> bit) & 1, 1
        )
    return first.reshape(rest), second.reshape(rest)


def gather_rest(near, far, z, n_ctx, q, n_q):
    near_halves = gather_plane(near[:, 0], near[:, 1], q, n_q)
    far_halves = gather_plane(far[:, 0], far[:, 1], q, n_q)
    shape = (n_q, n_ctx) + near.shape[2:]
    return tuple(ordered(a, b, z & 1, 2).reshape(shape) for a, b in zip(near_halves, far_halves))


def scatter_both(first, second, z, n_ctx, q, n_q):
    shape = (n_q, n_ctx // 2, 2) + first.shape[2:]
    sums = []
    for which in (1 - (z & 1), z & 1):
        halves = (choose(value.reshape(shape), which, 2) for value in (first, second))
        sums.append(jnp.stack(scatter_plane(*halves, q, n_q), axis=1))
    got = swap(sums[0], "ctx", 1)
    total = (sums[1].astype(f32) + got.astype(f32)).astype(bf16)
    return scatter_line(total, z, n_ctx, 1)


def sides_of(value):
    return swap(value, "dp", 2), swap(value, "dp", 4)


def sides_of_each(along_x, along_y):
    return swap(along_x, "dp", 2), swap(along_y, "dp", 4)


def add(*values):
    return sum(value.astype(f32) for value in values).astype(bf16)


def after(value, *others):
    if not others:
        return value
    return pl.pallas_call(
        lambda *refs: None,
        in_specs=[pl.BlockSpec(memory_space=pl.ANY)] * (1 + len(others)),
        out_specs=pl.BlockSpec(memory_space=pl.ANY),
        out_shape=jax.ShapeDtypeStruct(value.shape, value.dtype),
        input_output_aliases={0: 0},
    )(value, *others)


def scatter_line(value, z, n_ctx, least=0):
    rest = value.shape[1:]
    left = n_ctx >> least
    for bit in range(least, n_ctx.bit_length() - 1):
        left //= 2
        value = fold(value.reshape((left, 2) + rest), "ctx", 1 << bit, (z >> bit) & 1, 1)
    return value.reshape(rest)


def dot(a, b):
    return jnp.dot(a, b, preferred_element_type=f32)


def dot_nt(a, b):
    return lax.dot_general(a, b, (((1,), (1,)), ((), ())), preferred_element_type=f32)


def dot_tn(a, b):
    return lax.dot_general(a, b, (((0,), (0,)), ((), ())), preferred_element_type=f32)


def split(value):
    high = value.astype(bf16)
    return high, (value - high.astype(f32)).astype(bf16)


def split3(value):
    high, low = split(value)
    least = (value - high.astype(f32) - low.astype(f32)).astype(bf16)
    return high, low, least


def halves_of(value):
    return jnp.concatenate(split(value), axis=1)


def spread(halves, ex, lanes):
    return dot(halves, ex[:, lanes])


def pool(value, ex):
    return dot_nt(value, ex[:LANES, :])


def sigmoid(value):
    return 0.5 + 0.5 * jnp.tanh(0.5 * value)


def tiles_of(first, last):
    for number in range(first, last):
        for row in range(0, BLOCK, TILE):
            yield slice(row, row + TILE), strip_of(number)


def strip_of(number, size=LANES):
    return slice(number * size, (number + 1) * size)


def token_of(row):
    return (row % 8) * DEEP + row // 8


def last_tokens(block, rows):
    picked = [block[BLOCK - AHEAD + 8 * k + 7 : BLOCK - AHEAD + 8 * k + 8] for k in range(CONV - 1)]
    empty = jnp.zeros((rows - CONV + 1, block.shape[1]), block.dtype)
    return jnp.concatenate([empty] + picked, axis=0)


def widen(rows, wide):
    values = rows[:, :CONVD].astype(f32)
    wide[AHEAD:, :] = values[HALO:]
    for k in range(CONV - 1):
        ahead = values[HALO - CONV + 1 + k : HALO - CONV + 2 + k]
        begin = HALO + BLOCK - AHEAD + 8 * k
        wide[8 * k : 8 * k + 8, :] = jnp.concatenate([ahead, values[begin : begin + 7]], axis=0)


def conv_tile(wide, kw, rows, lanes):
    taps = [wide[rows.start + 8 * k : rows.start + 8 * k + TILE, lanes] for k in range(CONV)]
    total = kw[CONV : CONV + 1, lanes]
    for k in range(CONV):
        total = total + kw[k : k + 1, lanes] * taps[k]
    return total, taps


def inverse_rms(rows):
    return lax.rsqrt(jnp.mean(rows * rows, axis=-1, keepdims=True) + epsilon)


def steps_of(raw, heads, pick):
    biased = dot(raw, pick[...]) + heads[0:1, :]
    rate = heads[1:2, :]
    step = jnp.maximum(biased, 0.0) + jnp.log1p(jnp.exp(-jnp.abs(biased)))
    return biased, step, -step * rate, rate


def features_kernel(mine, other, before, before_other, norm, front, kw, heads, pick, tri, ex,
                    normed_o, px_o, x_o, u_o, bc_o, cum_o, cumt_o, entry_o, factor_o, total_o,
                    decay_o, state, passed, wide, weighted, stepped, left):
    j, block = pl.program_id(0), pl.program_id(1)

    def rows_of(begin, count):
        begin = pl.multiple_of(begin, count)
        return jnp.where(j == 0, mine[pl.ds(begin, count), :], other[pl.ds(begin, count), :])

    ahead = jnp.where(j == 0, before[...], before_other[...])
    within = rows_of(jnp.maximum(block - 1, 0) * BLOCK, BLOCK)
    ahead = jnp.where(block == 0, ahead.astype(f32), last_tokens(within.astype(f32), HALO))
    residual = jnp.concatenate([ahead, rows_of(block * BLOCK, BLOCK).astype(f32)], axis=0)
    normed = (residual * inverse_rms(residual) * norm[...]).astype(bf16)
    normed_o[...] = normed[HALO:]
    rows = dot(normed, front[...]).astype(bf16)
    px_o[0] = rows
    widen(rows, wide)

    @pl.when(block == 0)
    def _():
        state[...] = jnp.zeros_like(state)
        passed[...] = jnp.ones_like(passed)

    _, step, log_decay, _ = steps_of(rows[HALO:, CONVD:], heads, pick)
    cum = sum(dot(tri[...], part) for part in split3(log_decay))
    last = cum[BLOCK - 1 : BLOCK, :]
    cum_o[...] = cum
    cumt_o[0] = cum.T
    step, remaining = halves_of(step), halves_of(jnp.exp(last - cum))
    whole = halves_of(jnp.broadcast_to(jnp.exp(last), (16, LANES)))
    entry_o[0] = state[...].astype(bf16)
    factor_o[0] = jnp.broadcast_to(passed[...], (8, MINE))
    for rows_t, lanes in tiles_of(PAIRS, PAIRS + 2):
        total, _ = conv_tile(wide, kw, rows_t, lanes)
        bc_o[rows_t, lanes.start - MINE : lanes.stop - MINE] = (total * sigmoid(total)).astype(bf16)
    stepped[...] = dot(step, ex[...])
    left[...] = dot(remaining, ex[...])
    for rows_t, lanes in tiles_of(0, PAIRS):
        total, _ = conv_tile(wide, kw, rows_t, lanes)
        x = total * sigmoid(total)
        x_o[rows_t, lanes] = x.astype(bf16)
        u = (x * stepped[rows_t, lanes]).astype(bf16)
        u_o[rows_t, lanes] = u
        weighted[rows_t, lanes] = (u.astype(f32) * left[rows_t, lanes]).astype(bf16)
    whole = spread(whole, ex, slice(0, MINE))[:1]
    state[...] = whole * state[...] + dot_tn(bc_o[:, :STATE], weighted[...])
    passed[...] = passed[...] * whole
    total_o[0] = state[...].astype(bf16)
    decay_o[0] = jnp.broadcast_to(passed[...], (8, MINE))


def within_kernel(u, bc, cum, cumt, y_o):
    rows = lax.broadcasted_iota(jnp.int32, (BLOCK, BLOCK), 0)
    columns = lax.broadcasted_iota(jnp.int32, (BLOCK, BLOCK), 1)
    products = jnp.where(token_of(rows) >= token_of(columns), dot_nt(bc[:, STATE:], bc[:, :STATE]), 0.0)
    lane = lax.broadcasted_iota(jnp.int32, (BLOCK, LANES), 1)
    for pair in range(PAIRS):
        values = u[:, pair * LANES : (pair + 1) * LANES]
        made = []
        for head in (2 * pair, 2 * pair + 1):
            decay = jnp.exp(jnp.minimum(cum[:, head : head + 1] - cumt[0, head : head + 1, :], 0.0))
            made.append(dot((products * decay).astype(bf16), values))
        made = jnp.where(lane < HEAD, made[0], made[1])
        y_o[:, pair * LANES : (pair + 1) * LANES] = made.astype(bf16)


def gate_kernel(normed, cot_mine, cot_other, wg, wo, y, x, bc, cum, entry, factor, incoming, skip,
                gain, ex, mix_o, z_o, ds_o, state_o, sums_o, squares, crossed):
    cot = jnp.where(pl.program_id(0) == 0, cot_mine[...], cot_other[...])
    grown = halves_of(jnp.exp(cum[...]))
    for chunk in range(PAIRS // 2):
        many = strip_of(chunk, 2 * LANES)
        z_all = dot(normed[...], wg[:, many]).astype(bf16)
        ds_all = dot_nt(cot, wo[many, :])
        entering = entry[0, :, many].astype(f32) + factor[0, :1, many] * incoming[0, :, many].astype(f32)
        entering = entering.astype(bf16)
        z_o[:, many] = z_all
        ds_o[:, many] = ds_all.astype(bf16)
        state_o[0, :, many] = entering
        mix_all = spread(grown, ex, many) * dot(bc[:, STATE:], entering)
        for half in range(2):
            part, lanes = strip_of(half), strip_of(2 * chunk + half)
            for begin in range(0, BLOCK, TILE):
                tile = slice(begin, begin + TILE)
                carried = mix_all[tile, part] + y[tile, lanes].astype(f32)
                mix_o[tile, lanes] = carried.astype(bf16)
                mix = carried + skip[:, lanes] * x[tile, lanes].astype(f32)
                z = z_all[tile, part].astype(f32)
                g = mix * (z * sigmoid(z))
                other = ds_all[tile, part] * gain[:, lanes] * g
                if chunk + half == 0:
                    squares[tile, :], crossed[tile, :] = g * g, other
                else:
                    squares[tile, :] += g * g
                    crossed[tile, :] += other
    ones = jnp.ones((8, 2 * LANES), bf16)
    which = lax.broadcasted_iota(jnp.int32, (8, BLOCK), 0)
    sums = dot_nt(ones, halves_of(squares[...])), dot_nt(ones, halves_of(crossed[...]))
    sums_o[...] = jnp.where(which < 4, *sums)


def mixture_kernel(mix_r, z_r, ds_r, x, bc, cum, sums, got, skip, gain, ex,
                   scaled_o, dy_o, dz_o, inner_o, exit_o, factor_o, send_o, gain_o, skip_o,
                   state, passed, weighted, pooled, grown, scales):
    j, i = pl.program_id(0), pl.program_id(1)

    @pl.when((j == 0) & (i == 0))
    def _():
        gain_o[...] = jnp.zeros_like(gain_o)
        skip_o[...] = jnp.zeros_like(skip_o)

    @pl.when(i == 0)
    def _():
        state[...] = jnp.zeros_like(state)
        passed[...] = jnp.ones_like(passed)

    summed = sums[...] + got[...]
    lane = lax.broadcasted_iota(jnp.int32, (8, 2 * LANES), 1)
    row = lax.broadcasted_iota(jnp.int32, (8, 2 * LANES), 0)
    turn = jnp.where(row == (lane // LANES) * 4, 1.0, 0.0).astype(bf16)
    summed = sum(dot_tn(part, turn) for part in split3(summed))
    scale = lax.rsqrt(summed[:, :LANES] / INNER + epsilon)
    back_scale = scale * scale * scale * (summed[:, LANES:] / INNER)
    scales[0], scales[1] = scale, back_scale
    grown[...] = dot(halves_of(jnp.exp(cum[...])), ex[...])
    for rows_t, lanes in tiles_of(0, PAIRS):
        carried = mix_r[rows_t, lanes].astype(f32)
        xs = x[rows_t, lanes].astype(f32)
        mix = carried + skip[:, lanes] * xs
        z = z_r[rows_t, lanes].astype(f32)
        ds = ds_r[rows_t, lanes].astype(f32)
        sig = sigmoid(z)
        silu = z * sig
        g = mix * silu
        normalized = g * scales[0, rows_t, :]
        scaled_o[rows_t, lanes] = (normalized * gain[:, lanes]).astype(bf16)
        gain_o[:, lanes] += jnp.sum(ds * normalized, axis=0, keepdims=True)
        dg = ds * (scales[0, rows_t, :] * gain[:, lanes]) - g * scales[1, rows_t, :]
        dmix = dg * silu
        dz_o[rows_t, lanes] = (dg * mix * (sig * (1.0 + z * (1.0 - sig)))).astype(bf16)
        skip_o[:, lanes] += jnp.sum(dmix * xs, axis=0, keepdims=True)
        dy = dmix.astype(bf16)
        dy_o[rows_t, lanes] = dy
        dyf = dy.astype(f32)
        pooled[rows_t, lanes] = (dyf * carried).astype(bf16)
        weighted[rows_t, lanes] = (dyf * grown[rows_t, lanes]).astype(bf16)
    inner_o[...] = pool(pooled[...], ex)
    last = cum[BLOCK - 1 : BLOCK, :]
    whole = halves_of(jnp.broadcast_to(jnp.exp(last), (16, LANES)))
    whole = spread(whole, ex, slice(0, MINE))[:1]
    exit_o[0] = state[...].astype(bf16)
    factor_o[0] = jnp.broadcast_to(passed[...], (8, MINE))
    state[...] = whole * state[...] + dot_tn(bc[:, STATE:], weighted[...])
    passed[...] = passed[...] * whole
    send_o[0] = state[...].astype(bf16)


def within_back(u, dy, bc, cum, cumt, du_o, dbc_o):
    rows = lax.broadcasted_iota(jnp.int32, (BLOCK, BLOCK), 0)
    columns = lax.broadcasted_iota(jnp.int32, (BLOCK, BLOCK), 1)
    causal = token_of(columns) >= token_of(rows)
    products = jnp.where(causal, dot_nt(bc[:, :STATE], bc[:, STATE:]), 0.0)
    lane = lax.broadcasted_iota(jnp.int32, (BLOCK, LANES), 1)
    total = jnp.zeros((BLOCK, BLOCK), f32)
    for pair in range(PAIRS):
        values = u[:, pair * LANES : (pair + 1) * LANES]
        grads = dy[:, pair * LANES : (pair + 1) * LANES]
        made = []
        for half in range(2):
            head = 2 * pair + half
            decay = jnp.exp(jnp.minimum(cumt[0, head : head + 1, :] - cum[:, head : head + 1], 0.0))
            made.append(dot((products * decay).astype(bf16), grads))
            own = jnp.where((lane < HEAD) == (half == 0), values, jnp.zeros_like(values))
            total = total + dot_nt(own, grads) * decay
        made = jnp.where(lane < HEAD, made[0], made[1])
        du_o[:, pair * LANES : (pair + 1) * LANES] = made.astype(bf16)
    total = jnp.where(causal, total, 0.0).astype(bf16)
    dbc_o[:, :STATE] = dot(total, bc[:, STATE:])
    dbc_o[:, STATE:] = dot_tn(total, bc[:, :STATE])


def features_back_kernel(px, kw, heads, pick, tri, ex, u, dy, du_r, dbc, inner, cum,
                         entering, exit_r, factor, incoming, skip,
                         gp_o, rim_o, tail_o, kw_o, heads_o, after, wide, dpre, raw, wides,
                         products):
    j, i = pl.program_id(0), pl.program_id(1)

    @pl.when((j == 0) & (i == 0))
    def _():
        kw_o[...] = jnp.zeros_like(kw_o)
        heads_o[...] = jnp.zeros_like(heads_o)

    @pl.when(i == 0)
    def _():
        after[...] = jnp.zeros_like(after)

    rows = px[0]
    widen(rows, wide)
    biased, step, log_decay, rate = steps_of(rows[HALO:, CONVD:], heads, pick)
    c = cum[...]
    last = c[BLOCK - 1 : BLOCK, :]
    leaving = exit_r[0].astype(f32) + factor[0][:1] * incoming[0].astype(f32)
    leaving16 = leaving.astype(bf16)
    crossing = jnp.sum(leaving * entering[0].astype(f32), axis=0, keepdims=True)
    crossing = jnp.broadcast_to(crossing, (16, MINE))
    crossing = sum(pool(part, ex) for part in split(crossing))[:1] * jnp.exp(last)
    for k, value in enumerate((jnp.exp(last - c), jnp.exp(c), step)):
        wides[k] = dot(halves_of(value), ex[...])
    for rows_t, lanes in tiles_of(PAIRS, PAIRS + 1):
        total, _ = conv_tile(wide, kw, rows_t, lanes)
        products[0, rows_t, :LANES] = (total * sigmoid(total)).astype(bf16)
    raw[...] = dot(products[0, :, :LANES], leaving16)

    def finish(dact, total, sig, taps, rows_t, lanes):
        value = dact * (sig * (1.0 + total * (1.0 - sig)))
        kw_o[CONV : CONV + 1, lanes] += jnp.sum(value, axis=0, keepdims=True)
        for k in range(CONV):
            kw_o[k : k + 1, lanes] += jnp.sum(value * taps[k], axis=0, keepdims=True)
        dpre[rows_t, lanes] = value

    for rows_t, lanes in tiles_of(0, PAIRS):
        total, taps = conv_tile(wide, kw, rows_t, lanes)
        sig = sigmoid(total)
        uf = u[rows_t, lanes].astype(f32)
        dyf = dy[rows_t, lanes].astype(f32)
        left = wides[0, rows_t, lanes]
        du_state = left * raw[rows_t, lanes]
        du_in = du_r[rows_t, lanes].astype(f32)
        products[0, rows_t, lanes] = (uf * left).astype(bf16)
        products[1, rows_t, lanes] = (dyf * wides[1, rows_t, lanes]).astype(bf16)
        products[2, rows_t, lanes] = (uf * du_state).astype(bf16)
        products[3, rows_t, lanes] = (uf * du_in).astype(bf16)
        du = du_in + du_state
        products[4, rows_t, lanes] = (du * (total * sig)).astype(bf16)
        dx = du * wides[2, rows_t, lanes] + skip[:, lanes] * dyf
        finish(dx, total, sig, taps, rows_t, lanes)
    held, flow = pool(products[2], ex), inner[...] - pool(products[3], ex)
    dstep = pool(products[4], ex)
    raw[:, :STATE] = dbc[:, :STATE] + dot_nt(products[0], leaving16)
    raw[:, STATE : 2 * STATE] = dbc[:, STATE:] + dot_nt(products[1], entering[0])
    for rows_t, lanes in tiles_of(PAIRS, PAIRS + 2):
        total, taps = conv_tile(wide, kw, rows_t, lanes)
        dact = raw[rows_t, lanes.start - MINE : lanes.stop - MINE]
        finish(dact, total, sigmoid(total), taps, rows_t, lanes)
    for k in range(CONV - 1):
        begin = 8 * k + 1
        behind = jnp.concatenate([dpre[begin : begin + 7, :], after[k : k + 1, :]], axis=0)
        dpre[BLOCK + 8 * k : BLOCK + 8 * k + 8, :] = behind
    for rows_t, lanes in tiles_of(0, PAIRS + 2):
        begin = rows_t.start + 8 * (CONV - 1)
        din = sum(
            kw[k : k + 1, lanes] * dpre[begin - 8 * k : begin - 8 * k + TILE, lanes]
            for k in range(CONV)
        )
        gp_o[0, rows_t, lanes] = din.astype(bf16)
        if rows_t.stop == BLOCK:

            @pl.when(i == 0)
            def _(din=din, lanes=lanes):
                tail_o[0, :, lanes] = din[TILE - 32 :]

    first = [dpre[8 * k : 8 * k + 1, :] for k in range(CONV - 1)]
    first = jnp.concatenate(first + [jnp.zeros((8 - CONV + 1, CONVD), f32)], axis=0)
    after[...] = first
    dlog = crossing + sum(dot_tn(tri[...], part) for part in split3(flow))
    dlog = dlog + sum(dot(tri[...], part) for part in split3(held)) - held
    draw = (dstep - dlog * rate) * jax.nn.sigmoid(biased)
    gp_o[0, :, CONVD:] = dot_nt(draw.astype(bf16), pick[...]).astype(bf16)
    heads_o[0:1, :] += jnp.sum(draw, axis=0, keepdims=True)
    heads_o[1:2, :] += jnp.sum(dlog * log_decay, axis=0, keepdims=True)
    early = jnp.concatenate([jnp.zeros((8, CONVD), f32), first], axis=0)
    rim_o[0] = sum(kw[k : k + 1, :] * early[CONV - 1 - k : CONV - 1 - k + 8] for k in range(CONV))


def write_parts(j, mine_o, other_o, value):
    @pl.when(j == 0)
    def _():
        mine_o[...] = value

    @pl.when(j > 0)
    def _():
        other_o[...] = value


def added(*refs):
    return sum(ref.astype(f32) for ref in refs).astype(bf16)


def send_piece_kernel(place, value, out):
    out[...] = jnp.where(place[2] % 2 == 0, value[1], value[0])


def both_pieces_kernel(place, value, got, turn, out):
    side = place[2] % 2
    kept = jnp.where(side == 0, value[0], value[1])
    piece = jnp.where(pl.program_id(0) == side, kept, got[...])
    out[0] = dot(turn[...], piece).astype(bf16)


def ends_kernel(value, out):
    out[...] = last_tokens(value[...].astype(f32), HALO).astype(bf16)


def shard_kernel(own, got, out_weight, front_o, late_o):
    r_in, half = own.shape[0], out_weight.shape[0] // 2
    for k, source in enumerate((own, got)):
        front_o[k] = source[:, :FRONT]
        late_o[k, :r_in] = source[:, FRONT:]
        late_o[k, r_in:] = out_weight[k * half : (k + 1) * half]


def pair_kernel(first, second, out):
    count = first.shape[1]
    out[:, :count] = first[...]
    out[:, count:] = second[...]


def halves_kernel(along_x, along_y, x_o, y_o):
    x_o[...] = along_x[0]
    y_o[...] = along_y[0]


def ends_grads_kernel(front, front_got, late, late_got, own_o, send_o, out_o):
    r_in = front.shape[1]
    for k, out in enumerate((own_o, send_o)):
        out[:, :CONVD] = added(front[k], front_got[k])
        out[:, CONVD:] = added(late[k, :r_in], late_got[k, :r_in])
        half = late.shape[1] - r_in
        out_o[k * half : (k + 1) * half] = late[k, r_in:].astype(f32) + late_got[k, r_in:].astype(f32)


def input_grad_kernel(n_dp, place, own, got, sums, out):
    run, first = INNER // n_dp, place[1] == 0
    part = own.shape[0] // 4
    for k in range(n_dp // 2):
        for source, target in ((0, INNER), (CONVD, 0)):
            mine = own[:, source + k * run : source + (k + 1) * run].astype(f32)
            others = got[:, source + k * run : source + (k + 1) * run].astype(f32)
            at = target + 2 * k * run
            out[:, at : at + run] = jnp.where(first, mine, others)
            out[:, at + run : at + 2 * run] = jnp.where(first, others, mine)
    both = own[:, MINE:CONVD].astype(f32) + got[:, MINE:CONVD].astype(f32)
    out[:, 2 * INNER : INNER + XBC] = both
    for k in range(4):
        out[k * part : (k + 1) * part, INNER + XBC :] = sums[8 : 8 + part, k * HEADS : (k + 1) * HEADS]


def sums_kernel(parts, out):
    out[...] = jnp.sum(parts[...], axis=0)


def activations_kernel(place, tokens, keep, got, turn, out):
    value = jnp.where(pl.program_id(0) == place[2] % 2, keep[...], got[...])
    value = dot_tn(turn[...], value)
    out[0] = (tokens[0].astype(f32) + value).astype(bf16)


def tokens_grad_kernel(place, tokens, cot, keep, got, norm, turn, out):
    value = jnp.where(pl.program_id(0) == place[2] % 2, keep[...], got[...])
    value = dot_tn(turn[...], value)
    residual = tokens[0].astype(f32)
    inverse = inverse_rms(residual)
    weighted = value * norm[...]
    along = jnp.mean(weighted * residual, axis=-1, keepdims=True)
    out[0] = (
        cot[0].astype(f32) + inverse * weighted - residual * (inverse * inverse * inverse * along)
    )


def relative(place, n_ctx, groups):
    for group in range(2):
        for slot in range(n_ctx // 2):
            z = place[2] ^ group ^ (2 * slot)
            at = slot if groups == 2 else group * (n_ctx // 2) + slot
            first = 5 * group if groups == 2 else 0
            for half in range(2):
                for chip in range(3):
                    yield first + chip, (half, at), place[0] ^ chip, z, half
                yield first + 3 + half, (at,), place[0] ^ 3, z, half


def relative_back(place, n_ctx, groups):
    spots = {(0, 0): (0, 0), (0, 1): (0, 1), (1, 1): (1, 1), (2, 0): (2, 1), (1, 0): (3, None),
             (2, 1): (4, None), (3, 1): (1, 0), (3, 0): (2, 0)}
    for group in range(2):
        for slot in range(n_ctx // 2):
            z = place[2] ^ group ^ (2 * slot)
            at = slot if groups == 2 else group * (n_ctx // 2) + slot
            first = 5 * group if groups == 2 else 0
            for (chip, half), (piece, lead) in spots.items():
                index = (at,) if lead is None else (lead, at)
                yield first + piece, index, place[0] ^ chip, z, half


def front_rows(place, n_ctx, chip, z, half, count):
    return pl.multiple_of(((chip * 2 + (place[1] ^ half)) * n_ctx + z) * count, count)


def out_rows(n_ctx, chip, z, half, count):
    return pl.multiple_of(((chip * n_ctx + z) * 2 + half) * count, count)


def front_weights_kernel(n_dp, n_ctx, r_in, place, heads_in, ex, *refs):
    pieces, refs = refs[:-10], refs[-10:]
    front, wide = refs[0], refs[7]
    if len(pieces) == 1:
        front[...] = pieces[0][...]
    else:
        for piece, index, chip, z, half in relative(place, n_ctx, 2):
            begin = front_rows(place, n_ctx, chip, z, half, r_in)
            front[pl.ds(begin, r_in), :] = pieces[piece][index]
    wide[...] = front[:, CONVD:].astype(f32)
    spread_small(n_dp, r_in, place[1], wide, heads_in, ex, *refs[1:7], *refs[8:])


def late_weights_kernel(n_ctx, r_in, place, *refs):
    pieces, gate, out = refs[:-2], refs[-2], refs[-1]
    r_out = pieces[0].shape[2] - r_in
    for piece, index, chip, z, half in relative(place, n_ctx, 1):
        block = pieces[piece][index]
        gate[pl.ds(front_rows(place, n_ctx, chip, z, half, r_in), r_in), :] = block[:r_in]
        out[pl.ds(out_rows(n_ctx, chip, z, half, r_out), r_out), :] = block[r_in:]


def middle_kernel(n_ctx, r_in, place, normed, dz, scaled, cot_mine, cot_other, wo, u, dy, bc, cum, cumt, *refs):
    mine_o, other_o, du_o, dbc_o = refs[:4]
    outputs, (gate, out) = refs[4:-2], refs[-2:]
    j, i = pl.program_id(0), pl.program_id(1)
    within_back(u, dy, bc, cum, cumt, du_o, dbc_o)
    step = j * pl.num_programs(1) + i
    cot = jnp.where(j == 0, cot_mine[...], cot_other[...])
    write_parts(j, mine_o, other_o, dot(scaled[...], wo[...]).astype(bf16))
    gate_part, out_part = dot_tn(normed[...], dz[...]), dot_tn(scaled[...], cot)

    @pl.when(step == 0)
    def _():
        gate[...] = gate_part
        out[...] = out_part

    @pl.when(step > 0)
    def _():
        gate[...] += gate_part
        out[...] += out_part

    @pl.when(step == pl.num_programs(0) * pl.num_programs(1) - 1)
    def _():
        if len(outputs) == 2:
            outputs[0][...] = gate[...].astype(bf16)
            outputs[1][...] = out[...].astype(bf16)
            return
        r_out = outputs[0].shape[2] - r_in
        for piece, index, chip, z, half in relative_back(place, n_ctx, 1):
            begin = front_rows(place, n_ctx, chip, z, half, r_in)
            outputs[piece][index + (slice(0, r_in),)] = gate[pl.ds(begin, r_in), :].astype(bf16)
            begin = out_rows(n_ctx, chip, z, half, r_out)
            outputs[piece][index + (slice(r_in, r_in + r_out),)] = out[
                pl.ds(begin, r_out), :
            ].astype(bf16)


def with_rim(gp, tail, rim, whole):
    whole[...] = gp[0]
    late = tail[0]
    row = lax.broadcasted_iota(jnp.int32, late.shape, 0)
    for k in range(CONV - 1):
        here = row == 32 - AHEAD + 8 * k + 7
        late = late + jnp.where(here, rim[0, 8 - CONV + 1 + k : 8 - CONV + 2 + k, :], 0.0)
    whole[whole.shape[0] - 32 :, :CONVD] = late.astype(bf16)


def front_grads_kernel(n_ctx, r_in, place, normed, gp, tail, rim, step_o, *refs):
    outputs, (total, whole) = refs[:-2], refs[-2:]
    j = pl.program_id(0)
    with_rim(gp, tail, rim, whole)
    part = dot_tn(normed[...], whole[...])

    @pl.when(j == 0)
    def _():
        total[...] = part

    @pl.when(j > 0)
    def _():
        total[...] += part

    @pl.when(j == pl.num_programs(0) - 1)
    def _():
        step_o[...] = total[:, CONVD:]
        if len(outputs) == 1:
            outputs[0][...] = total[:, :CONVD].astype(bf16)
            return
        for piece, index, chip, z, half in relative_back(place, n_ctx, 1):
            begin = front_rows(place, n_ctx, chip, z, half, r_in)
            outputs[piece][index] = total[pl.ds(begin, r_in), :CONVD].astype(bf16)


def normed_grads_kernel(mine, other, dz, wg, gp, tail, rim, front, mine_o, other_o, norm_o, whole):
    j = pl.program_id(0)
    with_rim(gp, tail, rim, whole)
    back = dot_nt(dz[...], wg[...]) + dot_nt(whole[...], front[...])
    write_parts(j, mine_o, other_o, back.astype(bf16))
    residual = jnp.where(j == 0, mine[...], other[...]).astype(f32)

    @pl.when(j == 0)
    def _():
        norm_o[...] = jnp.zeros_like(norm_o)

    norm_o[...] += jnp.sum(back * (residual * inverse_rms(residual)), axis=0, keepdims=True)


def small_place(n, k, r_in, n_all):
    rows = min(r_in, 8)
    span = (LANES - HEADS) // -(-7 // rows)
    width = (XBC // n_all,) * 5 + (INNER // n_all, r_in)
    return n * r_in + k % rows, HEADS + (k // rows) * span, width[k]


def prepare_kernel(n_dp, n_all, place, weight, vectors, own_o, other_o):
    r_in, run, first = weight.shape[0], INNER // n_dp, place[1] == 0
    for k in range(n_dp // 2):
        for source, target in ((INNER, 0), (0, FRONT)):
            low = weight[:, source + 2 * k * run : source + (2 * k + 1) * run]
            high = weight[:, source + (2 * k + 1) * run : source + (2 * k + 2) * run]
            at = target + k * run
            own_o[:, at : at + run] = jnp.where(first, low, high)
            other_o[:, at : at + run] = jnp.where(first, high, low)
    row = lax.broadcasted_iota(jnp.int32, (r_in, LANES), 0)
    small = jnp.concatenate(
        [weight[:, INNER + XBC :].astype(f32), jnp.zeros((r_in, LANES - HEADS), f32)], axis=1
    )
    at = 0
    for k in range(7):
        line, lane, count = small_place(0, k, r_in, n_all)
        piece = vectors[:, at : at + count].astype(f32)
        parts = [jnp.zeros((1, lane), f32), piece, jnp.zeros((1, LANES - lane - count), f32)]
        small = small + jnp.where(row == line, jnp.concatenate(parts, axis=1), 0.0)
        at += count
    for out in (own_o, other_o):
        out[:, MINE:CONVD] = weight[:, 2 * INNER : INNER + XBC]
        out[:, CONVD:FRONT] = small.astype(bf16)


def spread_small(n_dp, r_in, core, wide, heads_in, ex, kw_o, gain_o, norm_o, heads_o, skip_o, pick_o,
                 full, gains):
    n_all = wide.shape[0] // r_in
    run, heads_run, first = INNER // n_dp, HEADS // n_dp, core == 0
    full[...] = jnp.zeros_like(full)
    for n in range(n_all):
        for k in range(7):
            row, lane, count = small_place(n, k, r_in, n_all)
            target, at = ((full, k), (gains, 0), (norm_o, 0))[max(k - CONV, 0)]
            target[at : at + 1, n * count : (n + 1) * count] = wide[row : row + 1, lane : lane + count]
    for k in range(n_dp // 2):
        low, high = 2 * k * run, (2 * k + 1) * run
        kw_o[:, k * run : (k + 1) * run] = jnp.where(
            first, full[:, low : low + run], full[:, high : high + run]
        )
        gain_o[:, k * run : (k + 1) * run] = jnp.where(
            first, gains[:, low : low + run], gains[:, high : high + run]
        )
    kw_o[:, MINE:] = full[:, INNER:]
    source = lax.broadcasted_iota(jnp.int32, (LANES, LANES), 0)
    local = lax.broadcasted_iota(jnp.int32, (LANES, LANES), 1)
    position = ((local // heads_run) * 2 + core) * heads_run + local % heads_run
    chosen = (source == position) & (local < HEADS // 2)
    pick = jnp.where(chosen, 1.0, 0.0).astype(bf16)
    pick_o[...] = pick
    heads = dot(heads_in[...].astype(bf16), pick)
    row = lax.broadcasted_iota(jnp.int32, (8, LANES), 0)
    lane = lax.broadcasted_iota(jnp.int32, (8, LANES), 1)
    rate = jnp.where(lane < HEADS // 2, jnp.exp(heads), 0.0)
    heads_o[...] = jnp.where(row == 1, rate, heads)
    skip_o[...] = dot(heads.astype(bf16), ex[:LANES, :])[2:3]


def pack_kernel(n_dp, place, norm_sum, kw_sum, gain_sum, heads_sum, skip_sum, step_sum, pick, ex,
                packed_o, full, gains):
    n_all = packed_o.shape[0]
    taps_n, gain_n, norm_n = XBC // n_all, INNER // n_all, norm_sum.shape[1] // n_all
    part, run = norm_n // 4, INNER // n_dp
    keep = [jnp.where(place[1] == which, 1.0, 0.0) for which in range(2)]
    for k in range(n_dp // 2):
        for which in range(2):
            begin = (2 * k + which) * run
            full[:, begin : begin + run] = kw_sum[:, k * run : (k + 1) * run] * keep[which]
            gains[:, begin : begin + run] = gain_sum[:, k * run : (k + 1) * run] * keep[which]
    full[:, INNER:] = kw_sum[:, MINE:]
    skips = jnp.broadcast_to(skip_sum[...], (16, MINE))
    skips = sum(pool(part, ex) for part in split(skips))[:8]
    row = lax.broadcasted_iota(jnp.int32, (8, LANES), 0)
    heads = jnp.where(row == 2, skips, heads_sum[...])
    heads = sum(dot_nt(piece, pick[...]) for piece in split3(heads))
    packed_o[...] = jnp.zeros_like(packed_o)
    for n in range(n_all):
        packed_o[n, 0:5, :taps_n] = full[0:5, n * taps_n : (n + 1) * taps_n]
        packed_o[n, 5:6, :gain_n] = gains[:, n * gain_n : (n + 1) * gain_n]
        packed_o[n, 6:7, :norm_n] = norm_sum[:, n * norm_n : (n + 1) * norm_n]
        for k in range(3):
            packed_o[n, 7:8, k * HEADS : (k + 1) * HEADS] = heads[k : k + 1, :HEADS]
        for k in range(4):
            begin = n * norm_n + k * part
            packed_o[n, 8 : 8 + part, k * HEADS : (k + 1) * HEADS] = step_sum[
                begin : begin + part, :HEADS
            ]


def call(kernel, grid, in_specs, out_specs, out_shape, scratch=(), cost=0, needs=(), vmem=20):
    count = len(in_specs)

    def body(*refs):
        kernel(*refs[:count], *refs[count + len(needs) :])

    made = pl.pallas_call(
        body,
        grid=grid,
        in_specs=list(in_specs) + [pl.BlockSpec(memory_space=pl.ANY)] * len(needs),
        out_specs=out_specs,
        out_shape=out_shape,
        scratch_shapes=scratch,
        cost_estimate=pl.CostEstimate(
            flops=int(1 + cost * 1e9), transcendentals=0, bytes_accessed=int(1 + cost * 3.5e6)
        ),
        compiler_params=pltpu.CompilerParams(
            vmem_limit_bytes=vmem << 20, dimension_semantics=("arbitrary",) * len(grid)
        ),
    )
    return lambda *arrays: made(*arrays, *needs)


def sds(shape, dtype=f32):
    return jax.ShapeDtypeStruct(shape, dtype)


def main(value):
    return pltpu.with_memory_space_constraint(value, pltpu.HBM)


def on_device(
    tokens,
    cotangent,
    norm_weight,
    input_weight,
    kernel_weight,
    kernel_bias,
    step_bias,
    decay_log,
    skip_gain,
    gate_norm_weight,
    output_weight,
):
    n_dp, n_ctx = lax.axis_size("dp"), lax.axis_size("ctx")
    n_q, n_all = n_dp // 2, n_dp * n_ctx
    place, z = lax.axis_index("dp"), lax.axis_index("ctx")
    q, core = place >> 1, place & 1
    seqs, piece, width = tokens.shape
    length = 2 * piece
    blocks = length // BLOCK
    rows = seqs * length
    r_in, r_out = input_weight.shape[0], output_weight.shape[0]
    every = ("dp", "ctx")
    fast = n_q == 4 and n_ctx == 4 and r_in % 16 == 0
    where = jnp.stack([q, core, z]).astype(jnp.int32)
    smem = pl.BlockSpec(memory_space=pltpu.SMEM)

    def lanes(value, count, wide=LANES):
        return jnp.pad(value, ((0, count - value.shape[0]), (0, wide - value.shape[1])))

    def all_of(arrays):
        return [pl.BlockSpec(v.shape, lambda *_, n=len(v.shape): (0,) * n) for v in arrays]

    def once(kernel, arrays, made, scratch=(), cost=0, needs=(), placed=False):
        specs = ([smem] if placed else []) + all_of(arrays)
        single = not isinstance(made, list)
        outs = all_of([made])[0] if single else all_of(made)
        run = call(kernel, (1,), specs, outs, made, scratch, cost, needs)
        return run(*([where] if placed else []), *arrays)

    order = token_of(np.arange(BLOCK))
    turn = (order[:, None] == np.arange(BLOCK)[None]).astype(ml_dtypes.bfloat16)
    turn = jnp.asarray(turn)
    cuts = 2
    cut_s = pl.BlockSpec((piece // cuts, width), lambda i: (i, 0))
    both_cut_s = pl.BlockSpec((2, piece // cuts, width), lambda i: (0, i, 0))

    def piece_to_send(value, needs=()):
        made = sds((piece, width), bf16)
        run = call(send_piece_kernel, (cuts,), [smem, both_cut_s], cut_s, made, needs=needs)
        return run(where, value)

    def enter_line(value, send, needs=(), cost=0):
        made, got = sds((2, piece, width), bf16), swap(send, "ctx", 1)
        specs = [smem] + all_of([value, got, turn])
        out_s = pl.BlockSpec((1, piece, width), lambda i: (i, 0, 0))
        run = call(both_pieces_kernel, (2,), specs, out_s, made, (), cost, needs)
        return run(where, value, got, turn).reshape(length, width)

    def ends_of(value):
        end_s = pl.BlockSpec((BLOCK, width), lambda i: (length // BLOCK - 1, 0))
        made = sds((HALO, width), bf16)
        return call(ends_kernel, (1,), [end_s], all_of([made])[0], made)(value)

    def leave_cores(mine, other, needs=()):
        total = add(after(mine, *needs), swap(other, "dp", 1)).reshape(2, piece, width)
        return choose(total, z & 1, 0), choose(total, 1 - (z & 1), 0)


    tokens_send = piece_to_send(tokens)
    vectors = jnp.concatenate([kernel_weight.reshape(-1), kernel_bias, gate_norm_weight, norm_weight])
    own_columns, other_columns = once(
        functools.partial(prepare_kernel, n_dp, n_all),
        [input_weight, vectors[None]],
        [sds((r_in, FRONT + MINE), bf16)] * 2,
        cost=8,
        needs=[tokens_send],
        placed=True,
    )
    got = swap(other_columns, "dp", 1)
    half = r_in + r_out // 2
    if fast:
        front_shard, late_shard = once(
            shard_kernel,
            [own_columns, got, output_weight],
            [sds((2, r_in, FRONT), bf16), sds((2, half, width), bf16)],
        )

        def pair(first, second, needs=(), cost=0):
            first, second = (v.reshape((2, -1) + v.shape[-2:]) for v in (first, second))
            count = first.shape[1] + second.shape[1]
            made = sds((2, count) + first.shape[2:], bf16)
            specs = [
                pl.BlockSpec((1,) + v.shape[1:], lambda k: (k, 0, 0, 0)) for v in (first, second, made)
            ]
            run = call(pair_kernel, (2,), specs[:2], specs[2], made, (), cost, needs)
            return run(first, second)

        def across_parts(along_x, along_y, needs=()):
            made = [sds(along_x.shape[1:], bf16)] * 2
            block = (1, 1) + along_x.shape[2:]
            specs = [
                pl.BlockSpec(block, lambda i, half=half: (half, i, 0, 0)) for half in range(2)
            ]
            outs = [pl.BlockSpec(block[1:], lambda i: (i, 0, 0))] * 2
            run = call(halves_kernel, along_x.shape[1:2], specs, outs, made, (), 0, needs)
            return run(along_x, along_y)

        def across_of(send_y, send_x):
            return swap(send_y, "dp", 4), swap(send_x, "dp", 2)

        first_got = swap(front_shard, "ctx", 2)
        inside = enter_line(tokens, tokens_send, needs=[front_shard], cost=8)
        other = swap(inside, "dp", 1)
        ends = ends_of(inside)
        before = hop(ends, 2)
        near = pair(front_shard, first_got, needs=[ends])
        sides = sides_of(near)
        far = swap(near, "ctx", 1)
        late_shard = after(late_shard, near)
        late_got = swap(late_shard, "ctx", 2)
        across = across_of(*across_parts(*sides))
        far = after(far, *across)
        far_sides = sides_of(far)
        late_near = pair(late_shard, late_got, needs=[far, before], cost=8)
        far_across_send = across_parts(*far_sides, needs=[late_near])
        far_across = across_of(*far_across_send)
        late_far = swap(late_near, "ctx", 1)
        before_other = swap(before, "dp", 1)
        late_own = after(pair(late_near, late_far, needs=far_across_send, cost=8), *far_across)
        front_pieces = [near, *sides, *across, far, *far_sides, *far_across]
    else:
        shard = ordered(own_columns, got, core, 0)
        near = gather_line(shard[:, :, :FRONT], z, n_ctx, 1)
        far = swap(near, "ctx", 1)
        halves = gather_rest(near, far, z, n_ctx, q, n_q)
        front_pieces = [jnp.stack(halves, axis=1).reshape(width, FRONT)]
        inside = enter_line(tokens, tokens_send)
        other = swap(inside, "dp", 1)
        before = hop(ends_of(inside), 2)
        before_other = swap(before, "dp", 1)
        out_halves = output_weight.reshape(2, r_out // 2, width)
        late_shard = jnp.concatenate([shard[:, :, FRONT:], out_halves], axis=1)
        late_near = gather_line(late_shard, z, n_ctx, 1)
        late_far = swap(late_near, "ctx", 1)
        first, second = gather_rest(late_near, late_far, z, n_ctx, q, n_q)
        w_gate = jnp.stack([first[:, :, :r_in], second[:, :, :r_in]], axis=1).reshape(width, MINE)
        w_out = jnp.stack([first[:, :, r_in:], second[:, :, r_in:]], axis=2).reshape(MINE, width)

    ex = np.arange(LANES)[:, None] == (np.arange(MINE)[None] // HEAD)
    ex = ex.astype(ml_dtypes.bfloat16)
    ex = jnp.asarray(np.concatenate([ex, ex], axis=0))
    tri = order[:, None] >= order[None]
    tri = jnp.asarray(tri.astype(ml_dtypes.bfloat16))
    heads_in = lanes(jnp.stack([step_bias, decay_log, skip_gain]).astype(f32), 8)
    w_front, kw, gain, norm_full, heads, skip, pick = once(
        functools.partial(front_weights_kernel, n_dp, n_ctx, r_in),
        [heads_in, ex, *map(main, front_pieces)],
        [pltpu.HBM((width, FRONT), bf16), sds((8, CONVD)), sds((1, MINE)), sds((1, width)),
         sds((8, LANES)), sds((1, MINE)), sds((LANES, LANES), bf16)],
        [pltpu.VMEM((width, LANES), f32), pltpu.VMEM((8, XBC), f32), pltpu.VMEM((1, INNER), f32)],
        cost=8,
        needs=[late_own, before_other] if fast else (),
        placed=True,
    )
    if fast:
        late_sides = sides_of(late_own)
    cot_send = piece_to_send(cotangent, needs=[w_front])

    grid = (seqs, blocks)

    def here(shape, back=False):
        lead = len(shape)
        if back:
            return pl.BlockSpec(shape, lambda j, i: (j * blocks + blocks - 1 - i,) + (0,) * (lead - 1))
        return pl.BlockSpec(shape, lambda j, i: (j * blocks + i,) + (0,) * (lead - 1))

    def per_seq(shape):
        return pl.BlockSpec(shape, lambda j, i: (j,) + (0,) * (len(shape) - 1))

    def fixed(shape):
        return pl.BlockSpec(shape, lambda j, i: (0,) * len(shape))

    mine_s = pl.BlockSpec((BLOCK, width), lambda j, i: (i * (1 - j) + (blocks - 1) * j, 0))
    other_s = pl.BlockSpec((BLOCK, width), lambda j, i: (i * j, 0))
    part_s = sds((length, width), bf16)
    steps_n = seqs * blocks
    wide, heads_s, both = (BLOCK, MINE), (BLOCK, LANES), (BLOCK, 2 * STATE)
    state_s, row8 = (1, STATE, MINE), (1, 8, MINE)
    conv_specs = [
        fixed((8, CONVD)),
        fixed((8, LANES)),
        fixed((LANES, LANES)),
        fixed((BLOCK, BLOCK)),
        fixed((2 * LANES, MINE)),
    ]
    conv_args = (kw, heads, pick, tri, ex)
    ext_front = (1, BLOCK + HALO, FRONT)
    front_s = fixed((width, FRONT))
    whole_s, halo_s = fixed((length, width)), fixed((HALO, width))
    normed, px, x, u, bc, cum, cumt, entry, entry_factor, state_total, state_decay = call(
        features_kernel,
        grid,
        [whole_s, whole_s, halo_s, halo_s, fixed((1, width)), front_s] + conv_specs,
        [here((BLOCK, width)), here(ext_front), here(wide), here(wide), here(both), here(heads_s),
         here((1, LANES, BLOCK)), here(state_s), here(row8), per_seq(state_s), per_seq(row8)],
        [pltpu.HBM((rows, width), bf16), pltpu.HBM((steps_n, BLOCK + HALO, FRONT), bf16),
         pltpu.HBM((rows, MINE), bf16), pltpu.HBM((rows, MINE), bf16),
         pltpu.HBM((rows, 2 * STATE), bf16), pltpu.HBM((rows, LANES)  , f32),
         pltpu.HBM((steps_n, LANES, BLOCK), f32), pltpu.HBM((steps_n, STATE, MINE), bf16), sds((steps_n, 8, MINE)),
         sds((seqs, STATE, MINE), bf16), sds((seqs, 8, MINE))],
        [pltpu.VMEM((STATE, MINE), f32), pltpu.VMEM((1, MINE), f32),
         pltpu.VMEM((BLOCK + AHEAD, CONVD), f32), pltpu.VMEM((BLOCK, MINE), bf16),
         pltpu.VMEM((BLOCK, MINE), f32), pltpu.VMEM((BLOCK, MINE), f32)],
        cost=16,
        needs=[cot_send],
    )(main(inside), main(other), before, before_other, norm_full, main(w_front), *conv_args)

    cot = enter_line(cotangent, cot_send, needs=[state_total])
    cot_other = swap(cot, "dp", 1)

    def relay(local, decay, steps):
        received = hop(local, steps)
        for _ in range(n_ctx // 2 - 2):
            received = hop((decay[:, :1] * received.astype(f32) + local.astype(f32)).astype(bf16), steps)
        return received

    incoming = relay(state_total, state_decay, 2)
    late_across_send = across_parts(*late_sides, needs=[cot]) if fast else ()
    y = call(
        within_kernel,
        grid,
        [here(wide), here(both), here(heads_s), here((1, LANES, BLOCK))],
        here(wide),
        sds((rows, MINE), bf16),
        cost=8,
        needs=late_across_send,
    )(u, bc, cum, cumt)

    if fast:
        late_across = across_of(*late_across_send)
        w_gate, w_out = once(
            functools.partial(late_weights_kernel, n_ctx, r_in),
            [*map(main, (late_own, *late_sides, *late_across))],
            [sds((width, MINE), bf16), sds((MINE, width), bf16)],
            placed=True,
            needs=[y],
        )

    mix, gate_raw, ds, entering, sums = call(
        gate_kernel,
        grid,
        [here((BLOCK, width)), mine_s, other_s, fixed((width, MINE)),
         fixed((MINE, width)), here(wide), here(wide), here(both), here(heads_s),
         here(state_s), here(row8), per_seq(state_s), fixed((1, MINE)), fixed((1, MINE)),
         fixed((2 * LANES, MINE))],
        [here(wide), here(wide), here(wide), here(state_s),
         pl.BlockSpec((8, BLOCK), lambda j, i: (0, j * blocks + i))],
        [pltpu.HBM((rows, MINE), bf16)] * 3
        + [pltpu.HBM((steps_n, STATE, MINE), bf16), sds((8, rows))],
        [pltpu.VMEM((BLOCK, LANES), f32)] * 2,
        cost=16,
    )(normed, cot, cot_other, w_gate, w_out, y, x, bc, cum, entry, entry_factor, incoming, skip, gain, ex)
    sums_got = swap(sums, "dp", 1)

    scaled, dy, dz, inner, leaving, leave_factor, grad_send, gain_sum, skip_sum = call(
        mixture_kernel,
        grid,
        [here(wide, True)] * 4
        + [here(both, True), here(heads_s, True)]
        + [pl.BlockSpec((8, BLOCK), lambda j, i: (0, j * blocks + blocks - 1 - i)),
           pl.BlockSpec((8, BLOCK), lambda j, i: (0, (1 - j) * blocks + blocks - 1 - i))]
        + [fixed((1, MINE)), fixed((1, MINE)), fixed((2 * LANES, MINE))],
        [here(wide, True)] * 3
        + [here(heads_s, True), here(state_s, True), here(row8, True), per_seq(state_s),
           fixed((1, MINE)), fixed((1, MINE))],
        [sds((rows, MINE), bf16)] * 3
        + [sds((rows, LANES)), sds((steps_n, STATE, MINE), bf16), sds((steps_n, 8, MINE)),
           sds((seqs, STATE, MINE), bf16), sds((1, MINE)), sds((1, MINE))],
        [pltpu.VMEM((STATE, MINE), f32), pltpu.VMEM((1, MINE), f32), pltpu.VMEM((BLOCK, MINE), bf16),
         pltpu.VMEM((BLOCK, MINE), bf16), pltpu.VMEM((BLOCK, MINE), f32), pltpu.VMEM((2, BLOCK, LANES), f32)],
        cost=12,
    )(*map(main, (mix, gate_raw, ds, x, bc, cum)), sums, sums_got, skip, gain, ex)
    grad_incoming = relay(grad_send, state_decay, -2)

    def parts_of(rows_n, columns):
        wide_part, narrow = (2, n_ctx, rows_n, columns), (n_ctx, rows_n, columns)
        return [sds(shape, bf16) for shape in [wide_part] * 3 + [narrow] * 2]

    made = parts_of(half, width) if fast else [sds((width, MINE), bf16), sds((MINE, width), bf16)]
    out_mine, out_other, du, dbc, *late_parts = call(
        functools.partial(middle_kernel, n_ctx, r_in),
        grid,
        [smem, here((BLOCK, width)), here(wide), here(wide), mine_s, other_s, fixed((MINE, width)),
         here(wide), here(wide), here(both), here(heads_s), here((1, LANES, BLOCK))],
        [mine_s, other_s, here(wide), here(both)] + all_of(made),
        [part_s, part_s, sds((rows, MINE), bf16), sds((rows, 2 * STATE))] + made,
        [pltpu.VMEM((width, MINE), f32), pltpu.VMEM((MINE, width), f32)],
        cost=24,
    )(where, normed, dz, scaled, cot, cot_other, w_out, u, dy, bc, cum, cumt)

    def join_of(along_x, along_y, got_x, got_y, needs=()):
        return add(after(along_x, *needs), got_y[0]), add(along_y, got_x[0])

    def own_of(own, got_x, got_y, last_x, last_y, needs=()):
        own = after(own, *needs)
        far_n = n_ctx // 2
        return [
            jnp.stack(
                [
                    add(own[0, part], got_y[1, part], last_x[part]),
                    add(own[1, part], got_x[1, part], last_y[part]),
                ]
            )
            for part in (slice(0, far_n), slice(far_n, n_ctx))
        ]

    def fold_of(near_part, got):
        return [add(near_part[:, slot], got[:, slot]) for slot in range(2)]

    if fast:
        late_first = swap(late_parts[1], "dp", 2), swap(late_parts[2], "dp", 4)

    gp, rim, tail, kw_sum, heads_sum = call(
        features_back_kernel,
        grid,
        [here(ext_front, True)]
        + conv_specs
        + [here(wide, True), here(wide, True), here(wide, True), here(both, True),
           here(heads_s, True), here(heads_s, True), here(state_s, True), here(state_s, True),
           here(row8, True), per_seq(state_s), fixed((1, MINE))],
        [pl.BlockSpec((1, BLOCK, FRONT), lambda j, i: (j, blocks - 1 - i, 0)),
         per_seq((1, 8, CONVD)), per_seq((1, 32, CONVD)), fixed((8, CONVD)), fixed((8, LANES))],
        [pltpu.HBM((seqs, length, FRONT), bf16), sds((seqs, 8, CONVD)),
         sds((seqs, 32, CONVD)), sds((8, CONVD)), sds((8, LANES))],
        [pltpu.VMEM((8, CONVD), f32), pltpu.VMEM((BLOCK + AHEAD, CONVD), f32),
         pltpu.VMEM((BLOCK + AHEAD, CONVD), f32), pltpu.VMEM((BLOCK, MINE), f32),
         pltpu.VMEM((3, BLOCK, MINE), f32), pltpu.VMEM((5, BLOCK, MINE), bf16)],
        cost=24,
    )(px, *conv_args, u, dy, du, dbc, inner, cum, entering, leaving, leave_factor, grad_incoming, skip)

    out_keep, out_send = leave_cores(out_mine, out_other, needs=[gp])
    out_got = swap(out_send, "ctx", 1)
    rim = hop(rim, -2)
    if fast:
        late_second = join_of(late_parts[3], late_parts[4], *late_first, needs=[gp])
        late_last = sides_of_each(*late_second)
    seq_wide = pl.BlockSpec((length, MINE), lambda j: (j, 0))
    seq_gp = pl.BlockSpec((1, length, FRONT), lambda j: (j, 0, 0))
    rims = [pl.BlockSpec((1, n, CONVD), lambda j: (j, 0, 0)) for n in (32, 8)]
    back_mine, back_other, norm_sum = call(
        normed_grads_kernel,
        (seqs,),
        all_of([inside, other]) + [seq_wide] + all_of([w_gate]) + [seq_gp] + rims + all_of([w_front]),
        all_of([part_s, part_s, sds((1, width))]),
        [part_s, part_s, sds((1, width))],
        [pltpu.VMEM((length, FRONT), bf16)],
        cost=12,
        needs=[*late_second, out_send] if fast else (),
    )(*map(main, (inside, other, dz, w_gate, gp)), tail, rim, main(w_front))
    if fast:
        late_near, late_far = own_of(late_parts[0], *late_first, *late_last, needs=[back_mine])
        late_got = swap(late_far, "ctx", 1)
    made = parts_of(r_in, CONVD) if fast else [sds((width, CONVD), bf16)]
    d_step, *front_parts = call(
        functools.partial(front_grads_kernel, n_ctx, r_in),
        (seqs,),
        [smem, seq_wide, seq_gp] + rims,
        all_of([sds((width, LANES))] + made),
        [sds((width, LANES))] + made,
        [pltpu.VMEM((width, FRONT), f32), pltpu.VMEM((length, FRONT), bf16)],
        cost=10,
        needs=[late_far] if fast else (),
    )(where, main(normed), main(gp), tail, rim)
    if fast:
        front_first = swap(front_parts[1], "dp", 2), swap(front_parts[2], "dp", 4)
    back_keep, back_send = leave_cores(back_mine, back_other, needs=[d_step])
    back_got = swap(back_send, "ctx", 1)

    def finish(kernel, arrays, more, dtype, needs, cost):
        block_s = pl.BlockSpec((1, piece, width), lambda j: (j, 0, 0))
        specs = [smem] + [block_s] * len(arrays) + all_of(more)
        made = sds((seqs, piece, width), dtype)
        return call(kernel, (seqs,), specs, block_s, made, (), cost, needs)(where, *arrays, *more)

    if fast:
        late_keep, late_send = fold_of(late_near, late_got)
        late_got = swap(late_send, "ctx", 2)
    packed = once(
        functools.partial(pack_kernel, n_dp),
        [norm_sum, kw_sum, gain_sum, heads_sum, skip_sum, d_step, pick, ex],
        sds((n_all, 16, LANES)),
        [pltpu.VMEM((8, XBC), f32), pltpu.VMEM((1, INNER), f32)],
        cost=8,
        needs=[back_send, late_send] if fast else (),
        placed=True,
    )
    packed_got = lax.all_to_all(packed, every, 0, 0)
    activations = finish(
        activations_kernel, [tokens], [out_keep, out_got, turn], bf16, [packed], 8
    )
    if fast:
        front_second = join_of(front_parts[3], front_parts[4], *front_first, needs=[activations])
        front_last = sides_of_each(*front_second)
    tokens_grad = finish(
        tokens_grad_kernel,
        [tokens, cotangent],
        [back_keep, back_got, norm_full, turn],
        f32,
        [*front_second, late_got] if fast else (),
        8,
    )
    if fast:
        front_near, front_far = own_of(
            front_parts[0], *front_first, *front_last, needs=[tokens_grad, packed_got]
        )
        front_keep, front_send = fold_of(front_near, swap(front_far, "ctx", 1))
        front_got = swap(front_send, "ctx", 2)
    sums = once(
        sums_kernel, [packed_got], sds((16, LANES)), needs=[front_send] if fast else (), cost=8
    )
    if fast:
        own, send, output_weight_grad = once(
            ends_grads_kernel,
            [front_keep, front_got, late_keep, late_got],
            [sds((r_in, CONVD + MINE), bf16)] * 2 + [sds((r_out, width))],
            needs=[sums],
        )
    else:
        d_gate, d_out = late_parts
        d_out = d_out.reshape(n_q, n_ctx, 2, r_out // 2, width)
        d_gate = d_gate.reshape(n_q, 2, n_ctx, r_in, MINE)
        halves = [
            jnp.concatenate([d_gate[:, which], d_out[:, :, which]], axis=2) for which in range(2)
        ]
        late = scatter_both(*halves, z, n_ctx, q, n_q)
        d_conv = front_parts[0].reshape(n_q, 2, n_ctx, r_in, CONVD)
        early = scatter_both(d_conv[:, 0], d_conv[:, 1], z, n_ctx, q, n_q)
        both_cores = jnp.concatenate([early, late[:, :r_in]], axis=2)
        own, send = choose(both_cores, core, 0), choose(both_cores, 1 - core, 0)
        output_weight_grad = late[:, r_in:].reshape(r_out, width).astype(f32)
    got = swap(send, "dp", 1)
    input_weight_grad = once(
        functools.partial(input_grad_kernel, n_dp),
        [own, got, sums],
        sds((r_in, INNER + XBC + HEADS)),
        placed=True,
    )
    head_sums = sums[7, : 3 * HEADS].reshape(3, HEADS)
    return (
        activations,
        tokens_grad,
        sums[6, :r_in],
        input_weight_grad,
        sums[:CONV, : XBC // n_all],
        sums[CONV, : XBC // n_all],
        head_sums[0],
        head_sums[1],
        head_sums[2],
        sums[5, : INNER // n_all],
        output_weight_grad,
    )


def solution(mesh):
    data, rows_spec, vector = P("dp", "ctx", None), P(("dp", "ctx"), None), P(("dp", "ctx"))
    taps = P(None, ("dp", "ctx"))
    return jax.shard_map(
        on_device,
        mesh=mesh,
        in_specs=(data, data, vector, rows_spec, taps, vector, P(), P(), P(), vector, rows_spec),
        out_specs=(data, data, vector, rows_spec, taps, vector, P(), P(), P(), vector, rows_spec),
        check_vma=False,
    )
```

```python
import functools

import jax
import jax.numpy as jnp
import ml_dtypes
import numpy as np
from jax import lax
from jax.experimental import pallas as pl
from jax.experimental.pallas import tpu as pltpu
from jax.sharding import PartitionSpec as P

HEADS = 32
HEAD = 64
STATE = 128
CONV = 4
INNER = 2048
XBC = 2304
BLOCK = 256
HALO = 16
LANES = 128
TILE = 128
DEEP = BLOCK // 8
AHEAD = 8 * (CONV - 1)
MINE = INNER // 2
PAIRS = MINE // LANES
CONVD = MINE + 2 * STATE
FRONT = CONVD + LANES

epsilon = 1e-05
bf16 = jnp.bfloat16
f32 = jnp.float32


def swap(value, axis, mask):
    count = lax.axis_size(axis)
    return lax.ppermute(value, axis, [(i, i ^ mask) for i in range(count)])


def hop(value, steps):
    count = lax.axis_size("ctx")
    pairs = [(i, i + steps) for i in range(count) if 0 <= i + steps < count]
    return lax.ppermute(value, "ctx", pairs)


def ordered(own, other, bit, place):
    first = bit == 0
    return jnp.stack([jnp.where(first, own, other), jnp.where(first, other, own)], axis=place)


def choose(value, index, place):
    return lax.dynamic_index_in_dim(value, index, place, keepdims=False)


def bits_of(count):
    return range(count.bit_length() - 1)


def gather_line(shard, z, n_ctx, least=0):
    grown = shard
    for place, bit in enumerate(reversed(range(least, n_ctx.bit_length() - 1))):
        grown = ordered(grown, swap(grown, "ctx", 1 << bit), (z >> bit) & 1, place)
    return grown.reshape((n_ctx >> least,) + shard.shape)


def gather_plane(first, second, q, n_q):
    bits = list(bits_of(n_q))
    shape = first.shape
    for step, bit in enumerate(bits):
        back = bits[len(bits) - 1 - step]
        other = swap(first, "dp", 2 << bit)
        other_second = swap(second, "dp", 2 << back)
        first = ordered(first, other, (q >> bit) & 1, 0)
        second = ordered(second, other_second, (q >> back) & 1, step)
    return first.reshape((n_q,) + shape), second.reshape((n_q,) + shape)


def fold(value, axis, mask, bit, place):
    got = swap(choose(value, 1 - bit, place), axis, mask)
    return (choose(value, bit, place).astype(f32) + got.astype(f32)).astype(bf16)


def scatter_plane(first, second, q, n_q):
    bits = list(bits_of(n_q))
    rest = first.shape[1:]
    left = n_q
    for step, bit in enumerate(bits):
        back = bits[len(bits) - 1 - step]
        left //= 2
        first = fold(
            first.reshape((2, left) + rest), "dp", 2 << back, (q >> back) & 1, 0
        )
        second = fold(
            second.reshape((left, 2) + rest), "dp", 2 << bit, (q >> bit) & 1, 1
        )
    return first.reshape(rest), second.reshape(rest)


def gather_rest(near, far, z, n_ctx, q, n_q):
    near_halves = gather_plane(near[:, 0], near[:, 1], q, n_q)
    far_halves = gather_plane(far[:, 0], far[:, 1], q, n_q)
    shape = (n_q, n_ctx) + near.shape[2:]
    return tuple(ordered(a, b, z & 1, 2).reshape(shape) for a, b in zip(near_halves, far_halves))


def scatter_both(first, second, z, n_ctx, q, n_q):
    shape = (n_q, n_ctx // 2, 2) + first.shape[2:]
    sums = []
    for which in (1 - (z & 1), z & 1):
        halves = (choose(value.reshape(shape), which, 2) for value in (first, second))
        sums.append(jnp.stack(scatter_plane(*halves, q, n_q), axis=1))
    got = swap(sums[0], "ctx", 1)
    total = (sums[1].astype(f32) + got.astype(f32)).astype(bf16)
    return scatter_line(total, z, n_ctx, 1)


def sides_of(value):
    return swap(value, "dp", 2), swap(value, "dp", 4)


def sides_of_each(along_x, along_y):
    return swap(along_x, "dp", 2), swap(along_y, "dp", 4)


def add(*values):
    return sum(value.astype(f32) for value in values).astype(bf16)


def after(value, *others):
    if not others:
        return value
    return pl.pallas_call(
        lambda *refs: None,
        in_specs=[pl.BlockSpec(memory_space=pl.ANY)] * (1 + len(others)),
        out_specs=pl.BlockSpec(memory_space=pl.ANY),
        out_shape=jax.ShapeDtypeStruct(value.shape, value.dtype),
        input_output_aliases={0: 0},
        compiler_params=pltpu.CompilerParams(vmem_limit_bytes=1 << 20),
    )(value, *others)


def scatter_line(value, z, n_ctx, least=0):
    rest = value.shape[1:]
    left = n_ctx >> least
    for bit in range(least, n_ctx.bit_length() - 1):
        left //= 2
        value = fold(value.reshape((left, 2) + rest), "ctx", 1 << bit, (z >> bit) & 1, 1)
    return value.reshape(rest)


def dot(a, b):
    return jnp.dot(a, b, preferred_element_type=f32)


def dot_nt(a, b):
    return lax.dot_general(a, b, (((1,), (1,)), ((), ())), preferred_element_type=f32)


def dot_tn(a, b):
    return lax.dot_general(a, b, (((0,), (0,)), ((), ())), preferred_element_type=f32)


def split(value):
    high = value.astype(bf16)
    return high, (value - high.astype(f32)).astype(bf16)


def split3(value):
    high, low = split(value)
    least = (value - high.astype(f32) - low.astype(f32)).astype(bf16)
    return high, low, least


def halves_of(value):
    return jnp.concatenate(split(value), axis=1)


def spread(halves, ex, lanes):
    return dot(halves, ex[:, lanes])


def pool(value, ex):
    return dot_nt(value, ex[:LANES, :])


def sigmoid(value):
    return 0.5 + 0.5 * jnp.tanh(0.5 * value)


def tiles_of(first, last):
    for number in range(first, last):
        for row in range(0, BLOCK, TILE):
            yield slice(row, row + TILE), strip_of(number)


def strip_of(number, size=LANES):
    return slice(number * size, (number + 1) * size)


def token_of(row):
    return (row % 8) * DEEP + row // 8


def last_tokens(block, rows):
    picked = [block[BLOCK - AHEAD + 8 * k + 7 : BLOCK - AHEAD + 8 * k + 8] for k in range(CONV - 1)]
    empty = jnp.zeros((rows - CONV + 1, block.shape[1]), block.dtype)
    return jnp.concatenate([empty] + picked, axis=0)


def widen(rows, wide):
    values = rows[:, :CONVD].astype(f32)
    wide[AHEAD:, :] = values[HALO:]
    for k in range(CONV - 1):
        ahead = values[HALO - CONV + 1 + k : HALO - CONV + 2 + k]
        begin = HALO + BLOCK - AHEAD + 8 * k
        wide[8 * k : 8 * k + 8, :] = jnp.concatenate([ahead, values[begin : begin + 7]], axis=0)


def conv_tile(wide, kw, rows, lanes):
    taps = [wide[rows.start + 8 * k : rows.start + 8 * k + TILE, lanes] for k in range(CONV)]
    total = kw[CONV : CONV + 1, lanes]
    for k in range(CONV):
        total = total + kw[k : k + 1, lanes] * taps[k]
    return total, taps


def inverse_rms(rows):
    return lax.rsqrt(jnp.mean(rows * rows, axis=-1, keepdims=True) + epsilon)


def steps_of(raw, heads, pick):
    biased = dot(raw, pick[...]) + heads[0:1, :]
    rate = heads[1:2, :]
    step = jnp.maximum(biased, 0.0) + jnp.log1p(jnp.exp(-jnp.abs(biased)))
    return biased, step, -step * rate, rate


def features_kernel(mine, other, before, before_other, norm, front, kw, heads, pick, tri, ex,
                    normed_o, px_o, x_o, u_o, bc_o, cum_o, cumt_o, entry_o, factor_o, total_o,
                    decay_o, state, passed, wide, weighted, stepped, left):
    j, block = pl.program_id(0), pl.program_id(1)

    def rows_of(begin, count):
        begin = pl.multiple_of(begin, count)
        return jnp.where(j == 0, mine[pl.ds(begin, count), :], other[pl.ds(begin, count), :])

    ahead = jnp.where(j == 0, before[...], before_other[...])
    within = rows_of(jnp.maximum(block - 1, 0) * BLOCK, BLOCK)
    ahead = jnp.where(block == 0, ahead.astype(f32), last_tokens(within.astype(f32), HALO))
    residual = jnp.concatenate([ahead, rows_of(block * BLOCK, BLOCK).astype(f32)], axis=0)
    normed = (residual * inverse_rms(residual) * norm[...]).astype(bf16)
    normed_o[...] = normed[HALO:]
    rows = dot(normed, front[...]).astype(bf16)
    px_o[0] = rows
    widen(rows, wide)

    @pl.when(block == 0)
    def _():
        state[...] = jnp.zeros_like(state)
        passed[...] = jnp.ones_like(passed)

    _, step, log_decay, _ = steps_of(rows[HALO:, CONVD:], heads, pick)
    cum = sum(dot(tri[...], part) for part in split3(log_decay))
    last = cum[BLOCK - 1 : BLOCK, :]
    cum_o[...] = cum
    cumt_o[0] = cum.T
    step, remaining = halves_of(step), halves_of(jnp.exp(last - cum))
    whole = halves_of(jnp.broadcast_to(jnp.exp(last), (16, LANES)))
    entry_o[0] = state[...].astype(bf16)
    factor_o[0] = jnp.broadcast_to(passed[...], (8, MINE))
    for rows_t, lanes in tiles_of(PAIRS, PAIRS + 2):
        total, _ = conv_tile(wide, kw, rows_t, lanes)
        bc_o[rows_t, lanes.start - MINE : lanes.stop - MINE] = (total * sigmoid(total)).astype(bf16)
    stepped[...] = dot(step, ex[...])
    left[...] = dot(remaining, ex[...])
    for rows_t, lanes in tiles_of(0, PAIRS):
        total, _ = conv_tile(wide, kw, rows_t, lanes)
        x = total * sigmoid(total)
        x_o[rows_t, lanes] = x.astype(bf16)
        u = (x * stepped[rows_t, lanes]).astype(bf16)
        u_o[rows_t, lanes] = u
        weighted[rows_t, lanes] = (u.astype(f32) * left[rows_t, lanes]).astype(bf16)
    whole = spread(whole, ex, slice(0, MINE))[:1]
    state[...] = whole * state[...] + dot_tn(bc_o[:, :STATE], weighted[...])
    passed[...] = passed[...] * whole
    total_o[0] = state[...].astype(bf16)
    decay_o[0] = jnp.broadcast_to(passed[...], (8, MINE))


def within_kernel(u, bc, cum, cumt, y_o):
    rows = lax.broadcasted_iota(jnp.int32, (BLOCK, BLOCK), 0)
    columns = lax.broadcasted_iota(jnp.int32, (BLOCK, BLOCK), 1)
    products = jnp.where(token_of(rows) >= token_of(columns), dot_nt(bc[:, STATE:], bc[:, :STATE]), 0.0)
    lane = lax.broadcasted_iota(jnp.int32, (BLOCK, LANES), 1)
    for pair in range(PAIRS):
        values = u[:, pair * LANES : (pair + 1) * LANES]
        made = []
        for head in (2 * pair, 2 * pair + 1):
            decay = jnp.exp(jnp.minimum(cum[:, head : head + 1] - cumt[0, head : head + 1, :], 0.0))
            made.append(dot((products * decay).astype(bf16), values))
        made = jnp.where(lane < HEAD, made[0], made[1])
        y_o[:, pair * LANES : (pair + 1) * LANES] = made.astype(bf16)


def gate_kernel(normed, cot_mine, cot_other, wg, wo, y, x, bc, cum, entry, factor, incoming, skip,
                gain, ex, mix_o, z_o, ds_o, state_o, sums_o, squares, crossed):
    cot = jnp.where(pl.program_id(0) == 0, cot_mine[...], cot_other[...])
    grown = halves_of(jnp.exp(cum[...]))
    for chunk in range(PAIRS // 2):
        many = strip_of(chunk, 2 * LANES)
        z_all = dot(normed[...], wg[:, many]).astype(bf16)
        ds_all = dot_nt(cot, wo[many, :])
        entering = entry[0, :, many].astype(f32) + factor[0, :1, many] * incoming[0, :, many].astype(f32)
        entering = entering.astype(bf16)
        z_o[:, many] = z_all
        ds_o[:, many] = ds_all.astype(bf16)
        state_o[0, :, many] = entering
        mix_all = spread(grown, ex, many) * dot(bc[:, STATE:], entering)
        for half in range(2):
            part, lanes = strip_of(half), strip_of(2 * chunk + half)
            for begin in range(0, BLOCK, TILE):
                tile = slice(begin, begin + TILE)
                carried = mix_all[tile, part] + y[tile, lanes].astype(f32)
                mix_o[tile, lanes] = carried.astype(bf16)
                mix = carried + skip[:, lanes] * x[tile, lanes].astype(f32)
                z = z_all[tile, part].astype(f32)
                g = mix * (z * sigmoid(z))
                other = ds_all[tile, part] * gain[:, lanes] * g
                if chunk + half == 0:
                    squares[tile, :], crossed[tile, :] = g * g, other
                else:
                    squares[tile, :] += g * g
                    crossed[tile, :] += other
    ones = jnp.ones((8, 2 * LANES), bf16)
    which = lax.broadcasted_iota(jnp.int32, (8, BLOCK), 0)
    sums = dot_nt(ones, halves_of(squares[...])), dot_nt(ones, halves_of(crossed[...]))
    sums_o[...] = jnp.where(which < 4, *sums)


def mixture_kernel(mix_r, z_r, ds_r, x, bc, cum, sums, got, skip, gain, ex,
                   scaled_o, dy_o, dz_o, inner_o, exit_o, factor_o, send_o, gain_o, skip_o,
                   state, passed, weighted, pooled, grown, scales):
    j, i = pl.program_id(0), pl.program_id(1)

    @pl.when((j == 0) & (i == 0))
    def _():
        gain_o[...] = jnp.zeros_like(gain_o)
        skip_o[...] = jnp.zeros_like(skip_o)

    @pl.when(i == 0)
    def _():
        state[...] = jnp.zeros_like(state)
        passed[...] = jnp.ones_like(passed)

    summed = sums[...] + got[...]
    lane = lax.broadcasted_iota(jnp.int32, (8, 2 * LANES), 1)
    row = lax.broadcasted_iota(jnp.int32, (8, 2 * LANES), 0)
    turn = jnp.where(row == (lane // LANES) * 4, 1.0, 0.0).astype(bf16)
    summed = sum(dot_tn(part, turn) for part in split3(summed))
    scale = lax.rsqrt(summed[:, :LANES] / INNER + epsilon)
    back_scale = scale * scale * scale * (summed[:, LANES:] / INNER)
    scales[0], scales[1] = scale, back_scale
    grown[...] = dot(halves_of(jnp.exp(cum[...])), ex[...])
    for rows_t, lanes in tiles_of(0, PAIRS):
        carried = mix_r[rows_t, lanes].astype(f32)
        xs = x[rows_t, lanes].astype(f32)
        mix = carried + skip[:, lanes] * xs
        z = z_r[rows_t, lanes].astype(f32)
        ds = ds_r[rows_t, lanes].astype(f32)
        sig = sigmoid(z)
        silu = z * sig
        g = mix * silu
        normalized = g * scales[0, rows_t, :]
        scaled_o[rows_t, lanes] = (normalized * gain[:, lanes]).astype(bf16)
        gain_o[:, lanes] += jnp.sum(ds * normalized, axis=0, keepdims=True)
        dg = ds * (scales[0, rows_t, :] * gain[:, lanes]) - g * scales[1, rows_t, :]
        dmix = dg * silu
        dz_o[rows_t, lanes] = (dg * mix * (sig * (1.0 + z * (1.0 - sig)))).astype(bf16)
        skip_o[:, lanes] += jnp.sum(dmix * xs, axis=0, keepdims=True)
        dy = dmix.astype(bf16)
        dy_o[rows_t, lanes] = dy
        dyf = dy.astype(f32)
        pooled[rows_t, lanes] = (dyf * carried).astype(bf16)
        weighted[rows_t, lanes] = (dyf * grown[rows_t, lanes]).astype(bf16)
    inner_o[...] = pool(pooled[...], ex)
    last = cum[BLOCK - 1 : BLOCK, :]
    whole = halves_of(jnp.broadcast_to(jnp.exp(last), (16, LANES)))
    whole = spread(whole, ex, slice(0, MINE))[:1]
    exit_o[0] = state[...].astype(bf16)
    factor_o[0] = jnp.broadcast_to(passed[...], (8, MINE))
    state[...] = whole * state[...] + dot_tn(bc[:, STATE:], weighted[...])
    passed[...] = passed[...] * whole
    send_o[0] = state[...].astype(bf16)


def within_back(u, dy, bc, cum, cumt, du_o, dbc_o):
    rows = lax.broadcasted_iota(jnp.int32, (BLOCK, BLOCK), 0)
    columns = lax.broadcasted_iota(jnp.int32, (BLOCK, BLOCK), 1)
    causal = token_of(columns) >= token_of(rows)
    products = jnp.where(causal, dot_nt(bc[:, :STATE], bc[:, STATE:]), 0.0)
    lane = lax.broadcasted_iota(jnp.int32, (BLOCK, LANES), 1)
    total = jnp.zeros((BLOCK, BLOCK), f32)
    for pair in range(PAIRS):
        values = u[:, pair * LANES : (pair + 1) * LANES]
        grads = dy[:, pair * LANES : (pair + 1) * LANES]
        made = []
        for half in range(2):
            head = 2 * pair + half
            decay = jnp.exp(jnp.minimum(cumt[0, head : head + 1, :] - cum[:, head : head + 1], 0.0))
            made.append(dot((products * decay).astype(bf16), grads))
            own = jnp.where((lane < HEAD) == (half == 0), values, jnp.zeros_like(values))
            total = total + dot_nt(own, grads) * decay
        made = jnp.where(lane < HEAD, made[0], made[1])
        du_o[:, pair * LANES : (pair + 1) * LANES] = made.astype(bf16)
    total = jnp.where(causal, total, 0.0).astype(bf16)
    dbc_o[:, :STATE] = dot(total, bc[:, STATE:])
    dbc_o[:, STATE:] = dot_tn(total, bc[:, :STATE])


def features_back_kernel(px, kw, heads, pick, tri, ex, u, dy, du_r, dbc, inner, cum,
                         entering, exit_r, factor, incoming, skip,
                         gp_o, rim_o, tail_o, kw_o, heads_o, after, wide, dpre, raw, wides,
                         products):
    j, i = pl.program_id(0), pl.program_id(1)

    @pl.when((j == 0) & (i == 0))
    def _():
        kw_o[...] = jnp.zeros_like(kw_o)
        heads_o[...] = jnp.zeros_like(heads_o)

    @pl.when(i == 0)
    def _():
        after[...] = jnp.zeros_like(after)

    rows = px[0]
    widen(rows, wide)
    biased, step, log_decay, rate = steps_of(rows[HALO:, CONVD:], heads, pick)
    c = cum[...]
    last = c[BLOCK - 1 : BLOCK, :]
    leaving = exit_r[0].astype(f32) + factor[0][:1] * incoming[0].astype(f32)
    leaving16 = leaving.astype(bf16)
    crossing = jnp.sum(leaving * entering[0].astype(f32), axis=0, keepdims=True)
    crossing = jnp.broadcast_to(crossing, (16, MINE))
    crossing = sum(pool(part, ex) for part in split(crossing))[:1] * jnp.exp(last)
    for k, value in enumerate((jnp.exp(last - c), jnp.exp(c), step)):
        wides[k] = dot(halves_of(value), ex[...])
    for rows_t, lanes in tiles_of(PAIRS, PAIRS + 1):
        total, _ = conv_tile(wide, kw, rows_t, lanes)
        products[0, rows_t, :LANES] = (total * sigmoid(total)).astype(bf16)
    raw[...] = dot(products[0, :, :LANES], leaving16)

    def finish(dact, total, sig, taps, rows_t, lanes):
        value = dact * (sig * (1.0 + total * (1.0 - sig)))
        kw_o[CONV : CONV + 1, lanes] += jnp.sum(value, axis=0, keepdims=True)
        for k in range(CONV):
            kw_o[k : k + 1, lanes] += jnp.sum(value * taps[k], axis=0, keepdims=True)
        dpre[rows_t, lanes] = value

    for rows_t, lanes in tiles_of(0, PAIRS):
        total, taps = conv_tile(wide, kw, rows_t, lanes)
        sig = sigmoid(total)
        uf = u[rows_t, lanes].astype(f32)
        dyf = dy[rows_t, lanes].astype(f32)
        left = wides[0, rows_t, lanes]
        du_state = left * raw[rows_t, lanes]
        du_in = du_r[rows_t, lanes].astype(f32)
        products[0, rows_t, lanes] = (uf * left).astype(bf16)
        products[1, rows_t, lanes] = (dyf * wides[1, rows_t, lanes]).astype(bf16)
        products[2, rows_t, lanes] = (uf * du_state).astype(bf16)
        products[3, rows_t, lanes] = (uf * du_in).astype(bf16)
        du = du_in + du_state
        products[4, rows_t, lanes] = (du * (total * sig)).astype(bf16)
        dx = du * wides[2, rows_t, lanes] + skip[:, lanes] * dyf
        finish(dx, total, sig, taps, rows_t, lanes)
    held, flow = pool(products[2], ex), inner[...] - pool(products[3], ex)
    dstep = pool(products[4], ex)
    raw[:, :STATE] = dbc[:, :STATE] + dot_nt(products[0], leaving16)
    raw[:, STATE : 2 * STATE] = dbc[:, STATE:] + dot_nt(products[1], entering[0])
    for rows_t, lanes in tiles_of(PAIRS, PAIRS + 2):
        total, taps = conv_tile(wide, kw, rows_t, lanes)
        dact = raw[rows_t, lanes.start - MINE : lanes.stop - MINE]
        finish(dact, total, sigmoid(total), taps, rows_t, lanes)
    for k in range(CONV - 1):
        begin = 8 * k + 1
        behind = jnp.concatenate([dpre[begin : begin + 7, :], after[k : k + 1, :]], axis=0)
        dpre[BLOCK + 8 * k : BLOCK + 8 * k + 8, :] = behind
    for rows_t, lanes in tiles_of(0, PAIRS + 2):
        begin = rows_t.start + 8 * (CONV - 1)
        din = sum(
            kw[k : k + 1, lanes] * dpre[begin - 8 * k : begin - 8 * k + TILE, lanes]
            for k in range(CONV)
        )
        gp_o[0, rows_t, lanes] = din.astype(bf16)
        if rows_t.stop == BLOCK:

            @pl.when(i == 0)
            def _(din=din, lanes=lanes):
                tail_o[0, :, lanes] = din[TILE - 32 :]

    first = [dpre[8 * k : 8 * k + 1, :] for k in range(CONV - 1)]
    first = jnp.concatenate(first + [jnp.zeros((8 - CONV + 1, CONVD), f32)], axis=0)
    after[...] = first
    dlog = crossing + sum(dot_tn(tri[...], part) for part in split3(flow))
    dlog = dlog + sum(dot(tri[...], part) for part in split3(held)) - held
    draw = (dstep - dlog * rate) * jax.nn.sigmoid(biased)
    gp_o[0, :, CONVD:] = dot_nt(draw.astype(bf16), pick[...]).astype(bf16)
    heads_o[0:1, :] += jnp.sum(draw, axis=0, keepdims=True)
    heads_o[1:2, :] += jnp.sum(dlog * log_decay, axis=0, keepdims=True)
    early = jnp.concatenate([jnp.zeros((8, CONVD), f32), first], axis=0)
    rim_o[0] = sum(kw[k : k + 1, :] * early[CONV - 1 - k : CONV - 1 - k + 8] for k in range(CONV))


def write_parts(j, mine_o, other_o, value):
    @pl.when(j == 0)
    def _():
        mine_o[...] = value

    @pl.when(j > 0)
    def _():
        other_o[...] = value


def added(*refs):
    return sum(ref.astype(f32) for ref in refs).astype(bf16)


def send_piece_kernel(place, value, out):
    out[...] = jnp.where(place[2] % 2 == 0, value[1], value[0])


def both_pieces_kernel(place, value, got, turn, out):
    side = place[2] % 2
    kept = jnp.where(side == 0, value[0], value[1])
    piece = jnp.where(pl.program_id(0) == side, kept, got[...])
    out[0] = dot(turn[...], piece).astype(bf16)


def ends_kernel(value, out):
    out[...] = last_tokens(value[...].astype(f32), HALO).astype(bf16)


def shard_kernel(own, got, out_weight, front_o, late_o):
    r_in, half = own.shape[0], out_weight.shape[0] // 2
    for k, source in enumerate((own, got)):
        front_o[k] = source[:, :FRONT]
        late_o[k, :r_in] = source[:, FRONT:]
        late_o[k, r_in:] = out_weight[k * half : (k + 1) * half]


def pair_kernel(first, second, out):
    count = first.shape[1]
    out[:, :count] = first[...]
    out[:, count:] = second[...]


def halves_kernel(along_x, along_y, x_o, y_o):
    x_o[...] = along_x[0]
    y_o[...] = along_y[0]


def ends_grads_kernel(front, front_got, late, late_got, own_o, send_o, out_o):
    r_in = front.shape[1]
    for k, out in enumerate((own_o, send_o)):
        out[:, :CONVD] = added(front[k], front_got[k])
        out[:, CONVD:] = added(late[k, :r_in], late_got[k, :r_in])
        half = late.shape[1] - r_in
        out_o[k * half : (k + 1) * half] = late[k, r_in:].astype(f32) + late_got[k, r_in:].astype(f32)


def input_grad_kernel(n_dp, place, own, got, sums, out):
    run, first = INNER // n_dp, place[1] == 0
    part = own.shape[0] // 4
    for k in range(n_dp // 2):
        for source, target in ((0, INNER), (CONVD, 0)):
            mine = own[:, source + k * run : source + (k + 1) * run].astype(f32)
            others = got[:, source + k * run : source + (k + 1) * run].astype(f32)
            at = target + 2 * k * run
            out[:, at : at + run] = jnp.where(first, mine, others)
            out[:, at + run : at + 2 * run] = jnp.where(first, others, mine)
    both = own[:, MINE:CONVD].astype(f32) + got[:, MINE:CONVD].astype(f32)
    out[:, 2 * INNER : INNER + XBC] = both
    for k in range(4):
        out[k * part : (k + 1) * part, INNER + XBC :] = sums[8 : 8 + part, k * HEADS : (k + 1) * HEADS]


def sums_kernel(parts, out):
    out[...] = jnp.sum(parts[...], axis=0)


def activations_kernel(place, tokens, keep, got, turn, out):
    value = jnp.where(pl.program_id(0) == place[2] % 2, keep[...], got[...])
    value = dot_tn(turn[...], value)
    out[0] = (tokens[0].astype(f32) + value).astype(bf16)


def tokens_grad_kernel(place, tokens, cot, keep, got, norm, turn, out):
    value = jnp.where(pl.program_id(0) == place[2] % 2, keep[...], got[...])
    value = dot_tn(turn[...], value)
    residual = tokens[0].astype(f32)
    inverse = inverse_rms(residual)
    weighted = value * norm[...]
    along = jnp.mean(weighted * residual, axis=-1, keepdims=True)
    out[0] = (
        cot[0].astype(f32) + inverse * weighted - residual * (inverse * inverse * inverse * along)
    )


def relative(place, n_ctx, groups):
    for group in range(2):
        for slot in range(n_ctx // 2):
            z = place[2] ^ group ^ (2 * slot)
            at = slot if groups == 2 else group * (n_ctx // 2) + slot
            first = 5 * group if groups == 2 else 0
            for half in range(2):
                for chip in range(3):
                    yield first + chip, (half, at), place[0] ^ chip, z, half
                yield first + 3 + half, (at,), place[0] ^ 3, z, half


def relative_back(place, n_ctx, groups):
    spots = {(0, 0): (0, 0), (0, 1): (0, 1), (1, 1): (1, 1), (2, 0): (2, 1), (1, 0): (3, None),
             (2, 1): (4, None), (3, 1): (1, 0), (3, 0): (2, 0)}
    for group in range(2):
        for slot in range(n_ctx // 2):
            z = place[2] ^ group ^ (2 * slot)
            at = slot if groups == 2 else group * (n_ctx // 2) + slot
            first = 5 * group if groups == 2 else 0
            for (chip, half), (piece, lead) in spots.items():
                index = (at,) if lead is None else (lead, at)
                yield first + piece, index, place[0] ^ chip, z, half


def front_rows(place, n_ctx, chip, z, half, count):
    return pl.multiple_of(((chip * 2 + (place[1] ^ half)) * n_ctx + z) * count, count)


def out_rows(n_ctx, chip, z, half, count):
    return pl.multiple_of(((chip * n_ctx + z) * 2 + half) * count, count)


def front_weights_kernel(n_dp, n_ctx, r_in, place, heads_in, ex, *refs):
    pieces, refs = refs[:-10], refs[-10:]
    front, wide = refs[0], refs[7]
    if len(pieces) == 1:
        front[...] = pieces[0][...]
    else:
        for piece, index, chip, z, half in relative(place, n_ctx, 2):
            begin = front_rows(place, n_ctx, chip, z, half, r_in)
            front[pl.ds(begin, r_in), :] = pieces[piece][index]
    wide[...] = front[:, CONVD:].astype(f32)
    spread_small(n_dp, r_in, place[1], wide, heads_in, ex, *refs[1:7], *refs[8:])


def late_weights_kernel(n_ctx, r_in, place, *refs):
    pieces, gate, out = refs[:-2], refs[-2], refs[-1]
    r_out = pieces[0].shape[2] - r_in
    for piece, index, chip, z, half in relative(place, n_ctx, 1):
        block = pieces[piece][index]
        gate[pl.ds(front_rows(place, n_ctx, chip, z, half, r_in), r_in), :] = block[:r_in]
        out[pl.ds(out_rows(n_ctx, chip, z, half, r_out), r_out), :] = block[r_in:]


def middle_kernel(n_ctx, r_in, place, normed, dz, scaled, cot_mine, cot_other, wo, u, dy, bc, cum, cumt, *refs):
    mine_o, other_o, du_o, dbc_o = refs[:4]
    outputs, (gate, out) = refs[4:-2], refs[-2:]
    j, i = pl.program_id(0), pl.program_id(1)
    within_back(u, dy, bc, cum, cumt, du_o, dbc_o)
    step = j * pl.num_programs(1) + i
    cot = jnp.where(j == 0, cot_mine[...], cot_other[...])
    write_parts(j, mine_o, other_o, dot(scaled[...], wo[...]).astype(bf16))
    gate_part, out_part = dot_tn(normed[...], dz[...]), dot_tn(scaled[...], cot)

    @pl.when(step == 0)
    def _():
        gate[...] = gate_part
        out[...] = out_part

    @pl.when(step > 0)
    def _():
        gate[...] += gate_part
        out[...] += out_part

    @pl.when(step == pl.num_programs(0) * pl.num_programs(1) - 1)
    def _():
        if len(outputs) == 2:
            outputs[0][...] = gate[...].astype(bf16)
            outputs[1][...] = out[...].astype(bf16)
            return
        r_out = outputs[0].shape[2] - r_in
        for piece, index, chip, z, half in relative_back(place, n_ctx, 1):
            begin = front_rows(place, n_ctx, chip, z, half, r_in)
            outputs[piece][index + (slice(0, r_in),)] = gate[pl.ds(begin, r_in), :].astype(bf16)
            begin = out_rows(n_ctx, chip, z, half, r_out)
            outputs[piece][index + (slice(r_in, r_in + r_out),)] = out[
                pl.ds(begin, r_out), :
            ].astype(bf16)


def with_rim(gp, tail, rim, whole):
    whole[...] = gp[0]
    late = tail[0]
    row = lax.broadcasted_iota(jnp.int32, late.shape, 0)
    for k in range(CONV - 1):
        here = row == 32 - AHEAD + 8 * k + 7
        late = late + jnp.where(here, rim[0, 8 - CONV + 1 + k : 8 - CONV + 2 + k, :], 0.0)
    whole[whole.shape[0] - 32 :, :CONVD] = late.astype(bf16)


def front_grads_kernel(n_ctx, r_in, place, normed, gp, tail, rim, step_o, *refs):
    outputs, (total, whole) = refs[:-2], refs[-2:]
    j = pl.program_id(0)
    with_rim(gp, tail, rim, whole)
    part = dot_tn(normed[...], whole[...])

    @pl.when(j == 0)
    def _():
        total[...] = part

    @pl.when(j > 0)
    def _():
        total[...] += part

    @pl.when(j == pl.num_programs(0) - 1)
    def _():
        step_o[...] = total[:, CONVD:]
        if len(outputs) == 1:
            outputs[0][...] = total[:, :CONVD].astype(bf16)
            return
        for piece, index, chip, z, half in relative_back(place, n_ctx, 1):
            begin = front_rows(place, n_ctx, chip, z, half, r_in)
            outputs[piece][index] = total[pl.ds(begin, r_in), :CONVD].astype(bf16)


def normed_grads_kernel(mine, other, dz, wg, gp, tail, rim, front, mine_o, other_o, norm_o, whole):
    j = pl.program_id(0)
    with_rim(gp, tail, rim, whole)
    back = dot_nt(dz[...], wg[...]) + dot_nt(whole[...], front[...])
    write_parts(j, mine_o, other_o, back.astype(bf16))
    residual = jnp.where(j == 0, mine[...], other[...]).astype(f32)

    @pl.when(j == 0)
    def _():
        norm_o[...] = jnp.zeros_like(norm_o)

    norm_o[...] += jnp.sum(back * (residual * inverse_rms(residual)), axis=0, keepdims=True)


def small_place(n, k, r_in, n_all):
    rows = min(r_in, 8)
    span = (LANES - HEADS) // -(-7 // rows)
    width = (XBC // n_all,) * 5 + (INNER // n_all, r_in)
    return n * r_in + k % rows, HEADS + (k // rows) * span, width[k]


def prepare_kernel(n_dp, n_all, place, weight, vectors, own_o, other_o):
    r_in, run, first = weight.shape[0], INNER // n_dp, place[1] == 0
    for k in range(n_dp // 2):
        for source, target in ((INNER, 0), (0, FRONT)):
            low = weight[:, source + 2 * k * run : source + (2 * k + 1) * run]
            high = weight[:, source + (2 * k + 1) * run : source + (2 * k + 2) * run]
            at = target + k * run
            own_o[:, at : at + run] = jnp.where(first, low, high)
            other_o[:, at : at + run] = jnp.where(first, high, low)
    row = lax.broadcasted_iota(jnp.int32, (r_in, LANES), 0)
    small = jnp.concatenate(
        [weight[:, INNER + XBC :].astype(f32), jnp.zeros((r_in, LANES - HEADS), f32)], axis=1
    )
    at = 0
    for k in range(7):
        line, lane, count = small_place(0, k, r_in, n_all)
        piece = vectors[:, at : at + count].astype(f32)
        parts = [jnp.zeros((1, lane), f32), piece, jnp.zeros((1, LANES - lane - count), f32)]
        small = small + jnp.where(row == line, jnp.concatenate(parts, axis=1), 0.0)
        at += count
    for out in (own_o, other_o):
        out[:, MINE:CONVD] = weight[:, 2 * INNER : INNER + XBC]
        out[:, CONVD:FRONT] = small.astype(bf16)


def spread_small(n_dp, r_in, core, wide, heads_in, ex, kw_o, gain_o, norm_o, heads_o, skip_o, pick_o,
                 full, gains):
    n_all = wide.shape[0] // r_in
    run, heads_run, first = INNER // n_dp, HEADS // n_dp, core == 0
    full[...] = jnp.zeros_like(full)
    for n in range(n_all):
        for k in range(7):
            row, lane, count = small_place(n, k, r_in, n_all)
            target, at = ((full, k), (gains, 0), (norm_o, 0))[max(k - CONV, 0)]
            target[at : at + 1, n * count : (n + 1) * count] = wide[row : row + 1, lane : lane + count]
    for k in range(n_dp // 2):
        low, high = 2 * k * run, (2 * k + 1) * run
        kw_o[:, k * run : (k + 1) * run] = jnp.where(
            first, full[:, low : low + run], full[:, high : high + run]
        )
        gain_o[:, k * run : (k + 1) * run] = jnp.where(
            first, gains[:, low : low + run], gains[:, high : high + run]
        )
    kw_o[:, MINE:] = full[:, INNER:]
    source = lax.broadcasted_iota(jnp.int32, (LANES, LANES), 0)
    local = lax.broadcasted_iota(jnp.int32, (LANES, LANES), 1)
    position = ((local // heads_run) * 2 + core) * heads_run + local % heads_run
    chosen = (source == position) & (local < HEADS // 2)
    pick = jnp.where(chosen, 1.0, 0.0).astype(bf16)
    pick_o[...] = pick
    heads = dot(heads_in[...].astype(bf16), pick)
    row = lax.broadcasted_iota(jnp.int32, (8, LANES), 0)
    lane = lax.broadcasted_iota(jnp.int32, (8, LANES), 1)
    rate = jnp.where(lane < HEADS // 2, jnp.exp(heads), 0.0)
    heads_o[...] = jnp.where(row == 1, rate, heads)
    skip_o[...] = dot(heads.astype(bf16), ex[:LANES, :])[2:3]


def pack_kernel(n_dp, place, norm_sum, kw_sum, gain_sum, heads_sum, skip_sum, step_sum, pick, ex,
                packed_o, full, gains):
    n_all = packed_o.shape[0]
    taps_n, gain_n, norm_n = XBC // n_all, INNER // n_all, norm_sum.shape[1] // n_all
    part, run = norm_n // 4, INNER // n_dp
    keep = [jnp.where(place[1] == which, 1.0, 0.0) for which in range(2)]
    for k in range(n_dp // 2):
        for which in range(2):
            begin = (2 * k + which) * run
            full[:, begin : begin + run] = kw_sum[:, k * run : (k + 1) * run] * keep[which]
            gains[:, begin : begin + run] = gain_sum[:, k * run : (k + 1) * run] * keep[which]
    full[:, INNER:] = kw_sum[:, MINE:]
    skips = jnp.broadcast_to(skip_sum[...], (16, MINE))
    skips = sum(pool(part, ex) for part in split(skips))[:8]
    row = lax.broadcasted_iota(jnp.int32, (8, LANES), 0)
    heads = jnp.where(row == 2, skips, heads_sum[...])
    heads = sum(dot_nt(piece, pick[...]) for piece in split3(heads))
    packed_o[...] = jnp.zeros_like(packed_o)
    for n in range(n_all):
        packed_o[n, 0:5, :taps_n] = full[0:5, n * taps_n : (n + 1) * taps_n]
        packed_o[n, 5:6, :gain_n] = gains[:, n * gain_n : (n + 1) * gain_n]
        packed_o[n, 6:7, :norm_n] = norm_sum[:, n * norm_n : (n + 1) * norm_n]
        for k in range(3):
            packed_o[n, 7:8, k * HEADS : (k + 1) * HEADS] = heads[k : k + 1, :HEADS]
        for k in range(4):
            begin = n * norm_n + k * part
            packed_o[n, 8 : 8 + part, k * HEADS : (k + 1) * HEADS] = step_sum[
                begin : begin + part, :HEADS
            ]


def call(kernel, grid, in_specs, out_specs, out_shape, scratch=(), cost=0, needs=(), vmem=20):
    count = len(in_specs)

    def body(*refs):
        kernel(*refs[:count], *refs[count + len(needs) :])

    made = pl.pallas_call(
        body,
        grid=grid,
        in_specs=list(in_specs) + [pl.BlockSpec(memory_space=pl.ANY)] * len(needs),
        out_specs=out_specs,
        out_shape=out_shape,
        scratch_shapes=scratch,
        cost_estimate=pl.CostEstimate(
            flops=int(1 + cost * 1e9), transcendentals=0, bytes_accessed=int(1 + cost * 3.5e6)
        ),
        compiler_params=pltpu.CompilerParams(
            vmem_limit_bytes=vmem << 20, dimension_semantics=("arbitrary",) * len(grid)
        ),
    )
    return lambda *arrays: made(*arrays, *needs)


def sds(shape, dtype=f32):
    return jax.ShapeDtypeStruct(shape, dtype)


def main(value):
    return pltpu.with_memory_space_constraint(value, pltpu.HBM)


def on_device(
    tokens,
    cotangent,
    norm_weight,
    input_weight,
    kernel_weight,
    kernel_bias,
    step_bias,
    decay_log,
    skip_gain,
    gate_norm_weight,
    output_weight,
):
    n_dp, n_ctx = lax.axis_size("dp"), lax.axis_size("ctx")
    n_q, n_all = n_dp // 2, n_dp * n_ctx
    place, z = lax.axis_index("dp"), lax.axis_index("ctx")
    q, core = place >> 1, place & 1
    seqs, piece, width = tokens.shape
    length = 2 * piece
    blocks = length // BLOCK
    rows = seqs * length
    r_in, r_out = input_weight.shape[0], output_weight.shape[0]
    every = ("dp", "ctx")
    fast = n_q == 4 and n_ctx == 4 and r_in % 16 == 0
    where = jnp.stack([q, core, z]).astype(jnp.int32)
    smem = pl.BlockSpec(memory_space=pltpu.SMEM)

    def lanes(value, count, wide=LANES):
        return jnp.pad(value, ((0, count - value.shape[0]), (0, wide - value.shape[1])))

    def all_of(arrays):
        return [pl.BlockSpec(v.shape, lambda *_, n=len(v.shape): (0,) * n) for v in arrays]

    def once(kernel, arrays, made, scratch=(), cost=0, needs=(), placed=False):
        specs = ([smem] if placed else []) + all_of(arrays)
        single = not isinstance(made, list)
        outs = all_of([made])[0] if single else all_of(made)
        run = call(kernel, (1,), specs, outs, made, scratch, cost, needs)
        return run(*([where] if placed else []), *arrays)

    order = token_of(np.arange(BLOCK))
    turn = (order[:, None] == np.arange(BLOCK)[None]).astype(ml_dtypes.bfloat16)
    turn = jnp.asarray(turn)
    cuts = 2
    cut_s = pl.BlockSpec((piece // cuts, width), lambda i: (i, 0))
    both_cut_s = pl.BlockSpec((2, piece // cuts, width), lambda i: (0, i, 0))

    def piece_to_send(value, needs=()):
        made = sds((piece, width), bf16)
        run = call(send_piece_kernel, (cuts,), [smem, both_cut_s], cut_s, made, needs=needs)
        return run(where, value)

    def enter_line(value, send, needs=(), cost=0):
        made, got = sds((2, piece, width), bf16), swap(send, "ctx", 1)
        specs = [smem] + all_of([value, got, turn])
        out_s = pl.BlockSpec((1, piece, width), lambda i: (i, 0, 0))
        run = call(both_pieces_kernel, (2,), specs, out_s, made, (), cost, needs)
        return run(where, value, got, turn).reshape(length, width)

    def ends_of(value):
        end_s = pl.BlockSpec((BLOCK, width), lambda i: (length // BLOCK - 1, 0))
        made = sds((HALO, width), bf16)
        return call(ends_kernel, (1,), [end_s], all_of([made])[0], made)(value)

    def leave_cores(mine, other, needs=()):
        total = add(after(mine, *needs), swap(other, "dp", 1)).reshape(2, piece, width)
        return choose(total, z & 1, 0), choose(total, 1 - (z & 1), 0)


    tokens_send = piece_to_send(tokens)
    vectors = jnp.concatenate([kernel_weight.reshape(-1), kernel_bias, gate_norm_weight, norm_weight])
    own_columns, other_columns = once(
        functools.partial(prepare_kernel, n_dp, n_all),
        [input_weight, vectors[None]],
        [sds((r_in, FRONT + MINE), bf16)] * 2,
        cost=8,
        needs=[tokens_send],
        placed=True,
    )
    got = swap(other_columns, "dp", 1)
    half = r_in + r_out // 2
    if fast:
        front_shard, late_shard = once(
            shard_kernel,
            [own_columns, got, output_weight],
            [sds((2, r_in, FRONT), bf16), sds((2, half, width), bf16)],
        )

        def pair(first, second, needs=(), cost=0):
            first, second = (v.reshape((2, -1) + v.shape[-2:]) for v in (first, second))
            count = first.shape[1] + second.shape[1]
            made = sds((2, count) + first.shape[2:], bf16)
            specs = [
                pl.BlockSpec((1,) + v.shape[1:], lambda k: (k, 0, 0, 0)) for v in (first, second, made)
            ]
            run = call(pair_kernel, (2,), specs[:2], specs[2], made, (), cost, needs)
            return run(first, second)

        def across_parts(along_x, along_y, needs=()):
            made = [sds(along_x.shape[1:], bf16)] * 2
            block = (1, 1) + along_x.shape[2:]
            specs = [
                pl.BlockSpec(block, lambda i, half=half: (half, i, 0, 0)) for half in range(2)
            ]
            outs = [pl.BlockSpec(block[1:], lambda i: (i, 0, 0))] * 2
            run = call(halves_kernel, along_x.shape[1:2], specs, outs, made, (), 0, needs)
            return run(along_x, along_y)

        def across_of(send_y, send_x):
            return swap(send_y, "dp", 4), swap(send_x, "dp", 2)

        first_got = swap(front_shard, "ctx", 2)
        inside = enter_line(tokens, tokens_send, needs=[front_shard], cost=8)
        other = swap(inside, "dp", 1)
        ends = ends_of(inside)
        before = hop(ends, 2)
        near = pair(front_shard, first_got, needs=[ends])
        sides = sides_of(near)
        far = swap(near, "ctx", 1)
        late_shard = after(late_shard, near)
        late_got = swap(late_shard, "ctx", 2)
        across = across_of(*across_parts(*sides))
        far = after(far, *across)
        far_sides = sides_of(far)
        late_near = pair(late_shard, late_got, needs=[far, before], cost=8)
        far_across_send = across_parts(*far_sides, needs=[late_near])
        far_across = across_of(*far_across_send)
        late_far = swap(late_near, "ctx", 1)
        before_other = swap(before, "dp", 1)
        late_own = after(pair(late_near, late_far, needs=far_across_send, cost=8), *far_across)
        front_pieces = [near, *sides, *across, far, *far_sides, *far_across]
    else:
        shard = ordered(own_columns, got, core, 0)
        near = gather_line(shard[:, :, :FRONT], z, n_ctx, 1)
        far = swap(near, "ctx", 1)
        halves = gather_rest(near, far, z, n_ctx, q, n_q)
        front_pieces = [jnp.stack(halves, axis=1).reshape(width, FRONT)]
        inside = enter_line(tokens, tokens_send)
        other = swap(inside, "dp", 1)
        before = hop(ends_of(inside), 2)
        before_other = swap(before, "dp", 1)
        out_halves = output_weight.reshape(2, r_out // 2, width)
        late_shard = jnp.concatenate([shard[:, :, FRONT:], out_halves], axis=1)
        late_near = gather_line(late_shard, z, n_ctx, 1)
        late_far = swap(late_near, "ctx", 1)
        first, second = gather_rest(late_near, late_far, z, n_ctx, q, n_q)
        w_gate = jnp.stack([first[:, :, :r_in], second[:, :, :r_in]], axis=1).reshape(width, MINE)
        w_out = jnp.stack([first[:, :, r_in:], second[:, :, r_in:]], axis=2).reshape(MINE, width)

    ex = np.arange(LANES)[:, None] == (np.arange(MINE)[None] // HEAD)
    ex = ex.astype(ml_dtypes.bfloat16)
    ex = jnp.asarray(np.concatenate([ex, ex], axis=0))
    tri = order[:, None] >= order[None]
    tri = jnp.asarray(tri.astype(ml_dtypes.bfloat16))
    heads_in = lanes(jnp.stack([step_bias, decay_log, skip_gain]).astype(f32), 8)
    w_front, kw, gain, norm_full, heads, skip, pick = once(
        functools.partial(front_weights_kernel, n_dp, n_ctx, r_in),
        [heads_in, ex, *front_pieces],
        [sds((width, FRONT), bf16), sds((8, CONVD)), sds((1, MINE)), sds((1, width)),
         sds((8, LANES)), sds((1, MINE)), sds((LANES, LANES), bf16)],
        [pltpu.VMEM((width, LANES), f32), pltpu.VMEM((8, XBC), f32), pltpu.VMEM((1, INNER), f32)],
        cost=8,
        needs=[late_own, before_other] if fast else (),
        placed=True,
    )
    if fast:
        late_sides = sides_of(late_own)
    cot_send = piece_to_send(cotangent, needs=[w_front])

    grid = (seqs, blocks)

    def here(shape, back=False):
        lead = len(shape)
        if back:
            return pl.BlockSpec(shape, lambda j, i: (j * blocks + blocks - 1 - i,) + (0,) * (lead - 1))
        return pl.BlockSpec(shape, lambda j, i: (j * blocks + i,) + (0,) * (lead - 1))

    def per_seq(shape):
        return pl.BlockSpec(shape, lambda j, i: (j,) + (0,) * (len(shape) - 1))

    def fixed(shape):
        return pl.BlockSpec(shape, lambda j, i: (0,) * len(shape))

    mine_s = pl.BlockSpec((BLOCK, width), lambda j, i: (i * (1 - j) + (blocks - 1) * j, 0))
    other_s = pl.BlockSpec((BLOCK, width), lambda j, i: (i * j, 0))
    part_s = sds((length, width), bf16)
    steps_n = seqs * blocks
    wide, heads_s, both = (BLOCK, MINE), (BLOCK, LANES), (BLOCK, 2 * STATE)
    state_s, row8 = (1, STATE, MINE), (1, 8, MINE)
    conv_specs = [
        fixed((8, CONVD)),
        fixed((8, LANES)),
        fixed((LANES, LANES)),
        fixed((BLOCK, BLOCK)),
        fixed((2 * LANES, MINE)),
    ]
    conv_args = (kw, heads, pick, tri, ex)
    ext_front = (1, BLOCK + HALO, FRONT)
    front_s = fixed((width, FRONT))
    whole_s, halo_s = fixed((length, width)), fixed((HALO, width))
    normed, px, x, u, bc, cum, cumt, entry, entry_factor, state_total, state_decay = call(
        features_kernel,
        grid,
        [whole_s, whole_s, halo_s, halo_s, fixed((1, width)), front_s] + conv_specs,
        [here((BLOCK, width)), here(ext_front), here(wide), here(wide), here(both), here(heads_s),
         here((1, LANES, BLOCK)), here(state_s), here(row8), per_seq(state_s), per_seq(row8)],
        [pltpu.HBM((rows, width), bf16), pltpu.HBM((steps_n, BLOCK + HALO, FRONT), bf16),
         pltpu.HBM((rows, MINE), bf16), pltpu.HBM((rows, MINE), bf16),
         pltpu.HBM((rows, 2 * STATE), bf16), pltpu.HBM((rows, LANES)  , f32),
         pltpu.HBM((steps_n, LANES, BLOCK), f32), pltpu.HBM((steps_n, STATE, MINE), bf16), sds((steps_n, 8, MINE)),
         sds((seqs, STATE, MINE), bf16), sds((seqs, 8, MINE))],
        [pltpu.VMEM((STATE, MINE), f32), pltpu.VMEM((1, MINE), f32),
         pltpu.VMEM((BLOCK + AHEAD, CONVD), f32), pltpu.VMEM((BLOCK, MINE), bf16),
         pltpu.VMEM((BLOCK, MINE), f32), pltpu.VMEM((BLOCK, MINE), f32)],
        cost=16,
        needs=[cot_send],
    )(inside, other, before, before_other, norm_full, w_front, *conv_args)

    cot = enter_line(cotangent, cot_send, needs=[state_total])
    cot_other = swap(cot, "dp", 1)

    def relay(local, decay, steps):
        received = hop(local, steps)
        for _ in range(n_ctx // 2 - 2):
            received = hop((decay[:, :1] * received.astype(f32) + local.astype(f32)).astype(bf16), steps)
        return received

    incoming = relay(state_total, state_decay, 2)
    late_across_send = across_parts(*late_sides, needs=[cot]) if fast else ()
    y = call(
        within_kernel,
        grid,
        [here(wide), here(both), here(heads_s), here((1, LANES, BLOCK))],
        here(wide),
        sds((rows, MINE), bf16),
        cost=8,
        needs=late_across_send,
    )(u, bc, cum, cumt)

    if fast:
        late_across = across_of(*late_across_send)
        w_gate, w_out = once(
            functools.partial(late_weights_kernel, n_ctx, r_in),
            [late_own, *late_sides, *late_across],
            [sds((width, MINE), bf16), sds((MINE, width), bf16)],
            placed=True,
            needs=[y],
        )

    mix, gate_raw, ds, entering, sums = call(
        gate_kernel,
        grid,
        [here((BLOCK, width)), mine_s, other_s, fixed((width, MINE)),
         fixed((MINE, width)), here(wide), here(wide), here(both), here(heads_s),
         here(state_s), here(row8), per_seq(state_s), fixed((1, MINE)), fixed((1, MINE)),
         fixed((2 * LANES, MINE))],
        [here(wide), here(wide), here(wide), here(state_s),
         pl.BlockSpec((8, BLOCK), lambda j, i: (0, j * blocks + i))],
        [pltpu.HBM((rows, MINE), bf16)] * 3
        + [pltpu.HBM((steps_n, STATE, MINE), bf16), sds((8, rows))],
        [pltpu.VMEM((BLOCK, LANES), f32)] * 2,
        cost=16,
    )(normed, cot, cot_other, w_gate, w_out, y, x, bc, cum, entry, entry_factor, incoming, skip, gain, ex)
    sums_got = swap(sums, "dp", 1)

    scaled, dy, dz, inner, leaving, leave_factor, grad_send, gain_sum, skip_sum = call(
        mixture_kernel,
        grid,
        [here(wide, True)] * 4
        + [here(both, True), here(heads_s, True)]
        + [pl.BlockSpec((8, BLOCK), lambda j, i: (0, j * blocks + blocks - 1 - i)),
           pl.BlockSpec((8, BLOCK), lambda j, i: (0, (1 - j) * blocks + blocks - 1 - i))]
        + [fixed((1, MINE)), fixed((1, MINE)), fixed((2 * LANES, MINE))],
        [here(wide, True)] * 3
        + [here(heads_s, True), here(state_s, True), here(row8, True), per_seq(state_s),
           fixed((1, MINE)), fixed((1, MINE))],
        [sds((rows, MINE), bf16)] * 3
        + [sds((rows, LANES)), sds((steps_n, STATE, MINE), bf16), sds((steps_n, 8, MINE)),
           sds((seqs, STATE, MINE), bf16), sds((1, MINE)), sds((1, MINE))],
        [pltpu.VMEM((STATE, MINE), f32), pltpu.VMEM((1, MINE), f32), pltpu.VMEM((BLOCK, MINE), bf16),
         pltpu.VMEM((BLOCK, MINE), bf16), pltpu.VMEM((BLOCK, MINE), f32), pltpu.VMEM((2, BLOCK, LANES), f32)],
        cost=12,
    )(*map(main, (mix, gate_raw, ds, x, bc, cum)), sums, sums_got, skip, gain, ex)
    grad_incoming = relay(grad_send, state_decay, -2)

    def parts_of(rows_n, columns):
        wide_part, narrow = (2, n_ctx, rows_n, columns), (n_ctx, rows_n, columns)
        return [sds(shape, bf16) for shape in [wide_part] * 3 + [narrow] * 2]

    made = parts_of(half, width) if fast else [sds((width, MINE), bf16), sds((MINE, width), bf16)]
    out_mine, out_other, du, dbc, *late_parts = call(
        functools.partial(middle_kernel, n_ctx, r_in),
        grid,
        [smem, here((BLOCK, width)), here(wide), here(wide), mine_s, other_s, fixed((MINE, width)),
         here(wide), here(wide), here(both), here(heads_s), here((1, LANES, BLOCK))],
        [mine_s, other_s, here(wide), here(both)] + all_of(made),
        [part_s, part_s, sds((rows, MINE), bf16), sds((rows, 2 * STATE))] + made,
        [pltpu.VMEM((width, MINE), f32), pltpu.VMEM((MINE, width), f32)],
        cost=24,
    )(where, normed, dz, scaled, cot, cot_other, w_out, u, dy, bc, cum, cumt)

    def join_of(along_x, along_y, got_x, got_y, needs=()):
        return add(after(along_x, *needs), got_y[0]), add(along_y, got_x[0])

    def own_of(own, got_x, got_y, last_x, last_y, needs=()):
        own = after(own, *needs)
        far_n = n_ctx // 2
        return [
            jnp.stack(
                [
                    add(own[0, part], got_y[1, part], last_x[part]),
                    add(own[1, part], got_x[1, part], last_y[part]),
                ]
            )
            for part in (slice(0, far_n), slice(far_n, n_ctx))
        ]

    def fold_of(near_part, got):
        return [add(near_part[:, slot], got[:, slot]) for slot in range(2)]

    if fast:
        late_first = swap(late_parts[1], "dp", 2), swap(late_parts[2], "dp", 4)

    gp, rim, tail, kw_sum, heads_sum = call(
        features_back_kernel,
        grid,
        [here(ext_front, True)]
        + conv_specs
        + [here(wide, True), here(wide, True), here(wide, True), here(both, True),
           here(heads_s, True), here(heads_s, True), here(state_s, True), here(state_s, True),
           here(row8, True), per_seq(state_s), fixed((1, MINE))],
        [pl.BlockSpec((1, BLOCK, FRONT), lambda j, i: (j, blocks - 1 - i, 0)),
         per_seq((1, 8, CONVD)), per_seq((1, 32, CONVD)), fixed((8, CONVD)), fixed((8, LANES))],
        [sds((seqs, length, FRONT), bf16), sds((seqs, 8, CONVD)),
         sds((seqs, 32, CONVD)), sds((8, CONVD)), sds((8, LANES))],
        [pltpu.VMEM((8, CONVD), f32), pltpu.VMEM((BLOCK + AHEAD, CONVD), f32),
         pltpu.VMEM((BLOCK + AHEAD, CONVD), f32), pltpu.VMEM((BLOCK, MINE), f32),
         pltpu.VMEM((3, BLOCK, MINE), f32), pltpu.VMEM((5, BLOCK, MINE), bf16)],
        cost=24,
    )(px, *conv_args, u, dy, du, dbc, inner, cum, entering, leaving, leave_factor, grad_incoming, skip)

    out_keep, out_send = leave_cores(out_mine, out_other, needs=[gp])
    out_got = swap(out_send, "ctx", 1)
    rim = hop(rim, -2)
    if fast:
        late_second = join_of(late_parts[3], late_parts[4], *late_first, needs=[gp])
        late_last = sides_of_each(*late_second)
    seq_wide = pl.BlockSpec((length, MINE), lambda j: (j, 0))
    seq_gp = pl.BlockSpec((1, length, FRONT), lambda j: (j, 0, 0))
    rims = [pl.BlockSpec((1, n, CONVD), lambda j: (j, 0, 0)) for n in (32, 8)]
    back_mine, back_other, norm_sum = call(
        normed_grads_kernel,
        (seqs,),
        all_of([inside, other]) + [seq_wide] + all_of([w_gate]) + [seq_gp] + rims + all_of([w_front]),
        all_of([part_s, part_s, sds((1, width))]),
        [part_s, part_s, sds((1, width))],
        [pltpu.VMEM((length, FRONT), bf16)],
        cost=12,
        needs=[*late_second, out_send] if fast else (),
    )(inside, other, dz, w_gate, gp, tail, rim, w_front)
    if fast:
        late_near, late_far = own_of(late_parts[0], *late_first, *late_last, needs=[back_mine])
        late_got = swap(late_far, "ctx", 1)
    made = parts_of(r_in, CONVD) if fast else [sds((width, CONVD), bf16)]
    d_step, *front_parts = call(
        functools.partial(front_grads_kernel, n_ctx, r_in),
        (seqs,),
        [smem, seq_wide, seq_gp] + rims,
        all_of([sds((width, LANES))] + made),
        [sds((width, LANES))] + made,
        [pltpu.VMEM((width, FRONT), f32), pltpu.VMEM((length, FRONT), bf16)],
        cost=10,
        needs=[late_far] if fast else (),
    )(where, normed, gp, tail, rim)
    if fast:
        front_first = swap(front_parts[1], "dp", 2), swap(front_parts[2], "dp", 4)
    back_keep, back_send = leave_cores(back_mine, back_other, needs=[d_step])
    back_got = swap(back_send, "ctx", 1)

    def finish(kernel, arrays, more, dtype, needs, cost):
        block_s = pl.BlockSpec((1, piece, width), lambda j: (j, 0, 0))
        specs = [smem] + [block_s] * len(arrays) + all_of(more)
        made = sds((seqs, piece, width), dtype)
        return call(kernel, (seqs,), specs, block_s, made, (), cost, needs)(where, *arrays, *more)

    if fast:
        late_keep, late_send = fold_of(late_near, late_got)
        late_got = swap(late_send, "ctx", 2)
    packed = once(
        functools.partial(pack_kernel, n_dp),
        [norm_sum, kw_sum, gain_sum, heads_sum, skip_sum, d_step, pick, ex],
        sds((n_all, 16, LANES)),
        [pltpu.VMEM((8, XBC), f32), pltpu.VMEM((1, INNER), f32)],
        cost=8,
        needs=[back_send, late_send] if fast else (),
        placed=True,
    )
    packed_got = lax.all_to_all(packed, every, 0, 0)
    activations = finish(
        activations_kernel, [tokens], [out_keep, out_got, turn], bf16, [packed], 8
    )
    if fast:
        front_second = join_of(front_parts[3], front_parts[4], *front_first, needs=[activations])
        front_last = sides_of_each(*front_second)
    tokens_grad = finish(
        tokens_grad_kernel,
        [tokens, cotangent],
        [back_keep, back_got, norm_full, turn],
        f32,
        [*front_second, late_got] if fast else (),
        8,
    )
    if fast:
        front_near, front_far = own_of(
            front_parts[0], *front_first, *front_last, needs=[tokens_grad, packed_got]
        )
        front_keep, front_send = fold_of(front_near, swap(front_far, "ctx", 1))
        front_got = swap(front_send, "ctx", 2)
    sums = once(
        sums_kernel, [packed_got], sds((16, LANES)), needs=[front_send] if fast else (), cost=8
    )
    if fast:
        own, send, output_weight_grad = once(
            ends_grads_kernel,
            [front_keep, front_got, late_keep, late_got],
            [sds((r_in, CONVD + MINE), bf16)] * 2 + [sds((r_out, width))],
            needs=[sums],
        )
    else:
        d_gate, d_out = late_parts
        d_out = d_out.reshape(n_q, n_ctx, 2, r_out // 2, width)
        d_gate = d_gate.reshape(n_q, 2, n_ctx, r_in, MINE)
        halves = [
            jnp.concatenate([d_gate[:, which], d_out[:, :, which]], axis=2) for which in range(2)
        ]
        late = scatter_both(*halves, z, n_ctx, q, n_q)
        d_conv = front_parts[0].reshape(n_q, 2, n_ctx, r_in, CONVD)
        early = scatter_both(d_conv[:, 0], d_conv[:, 1], z, n_ctx, q, n_q)
        both_cores = jnp.concatenate([early, late[:, :r_in]], axis=2)
        own, send = choose(both_cores, core, 0), choose(both_cores, 1 - core, 0)
        output_weight_grad = late[:, r_in:].reshape(r_out, width).astype(f32)
    got = swap(send, "dp", 1)
    input_weight_grad = once(
        functools.partial(input_grad_kernel, n_dp),
        [own, got, sums],
        sds((r_in, INNER + XBC + HEADS)),
        placed=True,
    )
    head_sums = sums[7, : 3 * HEADS].reshape(3, HEADS)
    return (
        activations,
        tokens_grad,
        sums[6, :r_in],
        input_weight_grad,
        sums[:CONV, : XBC // n_all],
        sums[CONV, : XBC // n_all],
        head_sums[0],
        head_sums[1],
        head_sums[2],
        sums[5, : INNER // n_all],
        output_weight_grad,
    )


def solution(mesh):
    data, rows_spec, vector = P("dp", "ctx", None), P(("dp", "ctx"), None), P(("dp", "ctx"))
    taps = P(None, ("dp", "ctx"))
    return jax.shard_map(
        on_device,
        mesh=mesh,
        in_specs=(data, data, vector, rows_spec, taps, vector, P(), P(), P(), vector, rows_spec),
        out_specs=(data, data, vector, rows_spec, taps, vector, P(), P(), P(), vector, rows_spec),
        check_vma=False,
    )
```

```python
import functools

import jax
import jax.numpy as jnp
import ml_dtypes
import numpy as np
from jax import lax
from jax.experimental import pallas as pl
from jax.experimental.pallas import tpu as pltpu
from jax.sharding import PartitionSpec as P

HEADS = 32
HEAD = 64
STATE = 128
CONV = 4
INNER = 2048
XBC = 2304
BLOCK = 256
HALO = 16
LANES = 128
TILE = 128
DEEP = BLOCK // 8
AHEAD = 8 * (CONV - 1)
MINE = INNER // 2
PAIRS = MINE // LANES
CONVD = MINE + 2 * STATE
FRONT = CONVD + LANES

epsilon = 1e-05
bf16 = jnp.bfloat16
f32 = jnp.float32


def swap(value, axis, mask):
    count = lax.axis_size(axis)
    return lax.ppermute(value, axis, [(i, i ^ mask) for i in range(count)])


def hop(value, steps):
    count = lax.axis_size("ctx")
    pairs = [(i, i + steps) for i in range(count) if 0 <= i + steps < count]
    return lax.ppermute(value, "ctx", pairs)


def ordered(own, other, bit, place):
    first = bit == 0
    return jnp.stack([jnp.where(first, own, other), jnp.where(first, other, own)], axis=place)


def choose(value, index, place):
    return lax.dynamic_index_in_dim(value, index, place, keepdims=False)


def bits_of(count):
    return range(count.bit_length() - 1)


def gather_line(shard, z, n_ctx, least=0):
    grown = shard
    for place, bit in enumerate(reversed(range(least, n_ctx.bit_length() - 1))):
        grown = ordered(grown, swap(grown, "ctx", 1 << bit), (z >> bit) & 1, place)
    return grown.reshape((n_ctx >> least,) + shard.shape)


def gather_plane(first, second, q, n_q):
    bits = list(bits_of(n_q))
    shape = first.shape
    for step, bit in enumerate(bits):
        back = bits[len(bits) - 1 - step]
        other = swap(first, "dp", 2 << bit)
        other_second = swap(second, "dp", 2 << back)
        first = ordered(first, other, (q >> bit) & 1, 0)
        second = ordered(second, other_second, (q >> back) & 1, step)
    return first.reshape((n_q,) + shape), second.reshape((n_q,) + shape)


def fold(value, axis, mask, bit, place):
    got = swap(choose(value, 1 - bit, place), axis, mask)
    return (choose(value, bit, place).astype(f32) + got.astype(f32)).astype(bf16)


def scatter_plane(first, second, q, n_q):
    bits = list(bits_of(n_q))
    rest = first.shape[1:]
    left = n_q
    for step, bit in enumerate(bits):
        back = bits[len(bits) - 1 - step]
        left //= 2
        first = fold(
            first.reshape((2, left) + rest), "dp", 2 << back, (q >> back) & 1, 0
        )
        second = fold(
            second.reshape((left, 2) + rest), "dp", 2 << bit, (q >> bit) & 1, 1
        )
    return first.reshape(rest), second.reshape(rest)


def gather_rest(near, far, z, n_ctx, q, n_q):
    near_halves = gather_plane(near[:, 0], near[:, 1], q, n_q)
    far_halves = gather_plane(far[:, 0], far[:, 1], q, n_q)
    shape = (n_q, n_ctx) + near.shape[2:]
    return tuple(ordered(a, b, z & 1, 2).reshape(shape) for a, b in zip(near_halves, far_halves))


def scatter_both(first, second, z, n_ctx, q, n_q):
    shape = (n_q, n_ctx // 2, 2) + first.shape[2:]
    sums = []
    for which in (1 - (z & 1), z & 1):
        halves = (choose(value.reshape(shape), which, 2) for value in (first, second))
        sums.append(jnp.stack(scatter_plane(*halves, q, n_q), axis=1))
    got = swap(sums[0], "ctx", 1)
    total = (sums[1].astype(f32) + got.astype(f32)).astype(bf16)
    return scatter_line(total, z, n_ctx, 1)


def sides_of(value):
    return swap(value, "dp", 2), swap(value, "dp", 4)


def sides_of_each(along_x, along_y):
    return swap(along_x, "dp", 2), swap(along_y, "dp", 4)


def add(*values):
    return sum(value.astype(f32) for value in values).astype(bf16)


def after(value, *others):
    if not others:
        return value
    return pl.pallas_call(
        lambda *refs: None,
        in_specs=[pl.BlockSpec(memory_space=pl.ANY)] * (1 + len(others)),
        out_specs=pl.BlockSpec(memory_space=pl.ANY),
        out_shape=jax.ShapeDtypeStruct(value.shape, value.dtype),
        input_output_aliases={0: 0},
        compiler_params=pltpu.CompilerParams(vmem_limit_bytes=1 << 20),
    )(value, *others)


def scatter_line(value, z, n_ctx, least=0):
    rest = value.shape[1:]
    left = n_ctx >> least
    for bit in range(least, n_ctx.bit_length() - 1):
        left //= 2
        value = fold(value.reshape((left, 2) + rest), "ctx", 1 << bit, (z >> bit) & 1, 1)
    return value.reshape(rest)


def dot(a, b):
    return jnp.dot(a, b, preferred_element_type=f32)


def dot_nt(a, b):
    return lax.dot_general(a, b, (((1,), (1,)), ((), ())), preferred_element_type=f32)


def dot_tn(a, b):
    return lax.dot_general(a, b, (((0,), (0,)), ((), ())), preferred_element_type=f32)


def split(value):
    high = value.astype(bf16)
    return high, (value - high.astype(f32)).astype(bf16)


def split3(value):
    high, low = split(value)
    least = (value - high.astype(f32) - low.astype(f32)).astype(bf16)
    return high, low, least


def halves_of(value):
    return jnp.concatenate(split(value), axis=1)


def spread(halves, ex, lanes):
    return dot(halves, ex[:, lanes])


def pool(value, ex):
    return dot_nt(value, ex[:LANES, :])


def sigmoid(value):
    return 0.5 + 0.5 * jnp.tanh(0.5 * value)


def tiles_of(first, last):
    for number in range(first, last):
        for row in range(0, BLOCK, TILE):
            yield slice(row, row + TILE), strip_of(number)


def strip_of(number, size=LANES):
    return slice(number * size, (number + 1) * size)


def token_of(row):
    return (row % 8) * DEEP + row // 8


def last_tokens(block, rows):
    picked = [block[BLOCK - AHEAD + 8 * k + 7 : BLOCK - AHEAD + 8 * k + 8] for k in range(CONV - 1)]
    empty = jnp.zeros((rows - CONV + 1, block.shape[1]), block.dtype)
    return jnp.concatenate([empty] + picked, axis=0)


def widen(rows, wide):
    values = rows[:, :CONVD].astype(f32)
    wide[AHEAD:, :] = values[HALO:]
    for k in range(CONV - 1):
        ahead = values[HALO - CONV + 1 + k : HALO - CONV + 2 + k]
        begin = HALO + BLOCK - AHEAD + 8 * k
        wide[8 * k : 8 * k + 8, :] = jnp.concatenate([ahead, values[begin : begin + 7]], axis=0)


def conv_tile(wide, kw, rows, lanes):
    taps = [wide[rows.start + 8 * k : rows.start + 8 * k + TILE, lanes] for k in range(CONV)]
    total = kw[CONV : CONV + 1, lanes]
    for k in range(CONV):
        total = total + kw[k : k + 1, lanes] * taps[k]
    return total, taps


def inverse_rms(rows):
    return lax.rsqrt(jnp.mean(rows * rows, axis=-1, keepdims=True) + epsilon)


def steps_of(raw, heads, pick):
    biased = dot(raw, pick[...]) + heads[0:1, :]
    rate = heads[1:2, :]
    step = jnp.maximum(biased, 0.0) + jnp.log1p(jnp.exp(-jnp.abs(biased)))
    return biased, step, -step * rate, rate


def features_kernel(mine, other, before, before_other, norm, front, kw, heads, pick, tri, ex,
                    normed_o, px_o, x_o, u_o, bc_o, cum_o, cumt_o, entry_o, factor_o, total_o,
                    decay_o, state, passed, wide, weighted, stepped, left):
    j, block = pl.program_id(0), pl.program_id(1)

    def rows_of(begin, count):
        begin = pl.multiple_of(begin, count)
        return jnp.where(j == 0, mine[pl.ds(begin, count), :], other[pl.ds(begin, count), :])

    ahead = jnp.where(j == 0, before[...], before_other[...])
    within = rows_of(jnp.maximum(block - 1, 0) * BLOCK, BLOCK)
    ahead = jnp.where(block == 0, ahead.astype(f32), last_tokens(within.astype(f32), HALO))
    residual = jnp.concatenate([ahead, rows_of(block * BLOCK, BLOCK).astype(f32)], axis=0)
    normed = (residual * inverse_rms(residual) * norm[...]).astype(bf16)
    normed_o[...] = normed[HALO:]
    rows = dot(normed, front[...]).astype(bf16)
    px_o[0] = rows
    widen(rows, wide)

    @pl.when(block == 0)
    def _():
        state[...] = jnp.zeros_like(state)
        passed[...] = jnp.ones_like(passed)

    _, step, log_decay, _ = steps_of(rows[HALO:, CONVD:], heads, pick)
    cum = sum(dot(tri[...], part) for part in split3(log_decay))
    last = cum[BLOCK - 1 : BLOCK, :]
    cum_o[...] = cum
    cumt_o[0] = cum.T
    step, remaining = halves_of(step), halves_of(jnp.exp(last - cum))
    whole = halves_of(jnp.broadcast_to(jnp.exp(last), (16, LANES)))
    entry_o[0] = state[...].astype(bf16)
    factor_o[0] = jnp.broadcast_to(passed[...], (8, MINE))
    for rows_t, lanes in tiles_of(PAIRS, PAIRS + 2):
        total, _ = conv_tile(wide, kw, rows_t, lanes)
        bc_o[rows_t, lanes.start - MINE : lanes.stop - MINE] = (total * sigmoid(total)).astype(bf16)
    stepped[...] = dot(step, ex[...])
    left[...] = dot(remaining, ex[...])
    for rows_t, lanes in tiles_of(0, PAIRS):
        total, _ = conv_tile(wide, kw, rows_t, lanes)
        x = total * sigmoid(total)
        x_o[rows_t, lanes] = x.astype(bf16)
        u = (x * stepped[rows_t, lanes]).astype(bf16)
        u_o[rows_t, lanes] = u
        weighted[rows_t, lanes] = (u.astype(f32) * left[rows_t, lanes]).astype(bf16)
    whole = spread(whole, ex, slice(0, MINE))[:1]
    state[...] = whole * state[...] + dot_tn(bc_o[:, :STATE], weighted[...])
    passed[...] = passed[...] * whole
    total_o[0] = state[...].astype(bf16)
    decay_o[0] = jnp.broadcast_to(passed[...], (8, MINE))


def within_kernel(u, bc, cum, cumt, y_o):
    rows = lax.broadcasted_iota(jnp.int32, (BLOCK, BLOCK), 0)
    columns = lax.broadcasted_iota(jnp.int32, (BLOCK, BLOCK), 1)
    products = jnp.where(token_of(rows) >= token_of(columns), dot_nt(bc[:, STATE:], bc[:, :STATE]), 0.0)
    lane = lax.broadcasted_iota(jnp.int32, (BLOCK, LANES), 1)
    for pair in range(PAIRS):
        values = u[:, pair * LANES : (pair + 1) * LANES]
        made = []
        for head in (2 * pair, 2 * pair + 1):
            decay = jnp.exp(jnp.minimum(cum[:, head : head + 1] - cumt[0, head : head + 1, :], 0.0))
            made.append(dot((products * decay).astype(bf16), values))
        made = jnp.where(lane < HEAD, made[0], made[1])
        y_o[:, pair * LANES : (pair + 1) * LANES] = made.astype(bf16)


def gate_kernel(normed, cot_mine, cot_other, wg, wo, y, x, bc, cum, entry, factor, incoming, skip,
                gain, ex, mix_o, z_o, ds_o, state_o, sums_o, squares, crossed):
    cot = jnp.where(pl.program_id(0) == 0, cot_mine[...], cot_other[...])
    grown = halves_of(jnp.exp(cum[...]))
    for chunk in range(PAIRS // 2):
        many = strip_of(chunk, 2 * LANES)
        z_all = dot(normed[...], wg[:, many]).astype(bf16)
        ds_all = dot_nt(cot, wo[many, :])
        entering = entry[0, :, many].astype(f32) + factor[0, :1, many] * incoming[0, :, many].astype(f32)
        entering = entering.astype(bf16)
        z_o[:, many] = z_all
        ds_o[:, many] = ds_all.astype(bf16)
        state_o[0, :, many] = entering
        mix_all = spread(grown, ex, many) * dot(bc[:, STATE:], entering)
        for half in range(2):
            part, lanes = strip_of(half), strip_of(2 * chunk + half)
            for begin in range(0, BLOCK, TILE):
                tile = slice(begin, begin + TILE)
                carried = mix_all[tile, part] + y[tile, lanes].astype(f32)
                mix_o[tile, lanes] = carried.astype(bf16)
                mix = carried + skip[:, lanes] * x[tile, lanes].astype(f32)
                z = z_all[tile, part].astype(f32)
                g = mix * (z * sigmoid(z))
                other = ds_all[tile, part] * gain[:, lanes] * g
                if chunk + half == 0:
                    squares[tile, :], crossed[tile, :] = g * g, other
                else:
                    squares[tile, :] += g * g
                    crossed[tile, :] += other
    ones = jnp.ones((8, 2 * LANES), bf16)
    which = lax.broadcasted_iota(jnp.int32, (8, BLOCK), 0)
    sums = dot_nt(ones, halves_of(squares[...])), dot_nt(ones, halves_of(crossed[...]))
    sums_o[...] = jnp.where(which < 4, *sums)


def mixture_kernel(mix_r, z_r, ds_r, x, bc, cum, sums, got, skip, gain, ex,
                   scaled_o, dy_o, dz_o, inner_o, exit_o, factor_o, send_o, gain_o, skip_o,
                   state, passed, weighted, pooled, grown, scales):
    j, i = pl.program_id(0), pl.program_id(1)

    @pl.when((j == 0) & (i == 0))
    def _():
        gain_o[...] = jnp.zeros_like(gain_o)
        skip_o[...] = jnp.zeros_like(skip_o)

    @pl.when(i == 0)
    def _():
        state[...] = jnp.zeros_like(state)
        passed[...] = jnp.ones_like(passed)

    summed = sums[...] + got[...]
    lane = lax.broadcasted_iota(jnp.int32, (8, 2 * LANES), 1)
    row = lax.broadcasted_iota(jnp.int32, (8, 2 * LANES), 0)
    turn = jnp.where(row == (lane // LANES) * 4, 1.0, 0.0).astype(bf16)
    summed = sum(dot_tn(part, turn) for part in split3(summed))
    scale = lax.rsqrt(summed[:, :LANES] / INNER + epsilon)
    back_scale = scale * scale * scale * (summed[:, LANES:] / INNER)
    scales[0], scales[1] = scale, back_scale
    grown[...] = dot(halves_of(jnp.exp(cum[...])), ex[...])
    for rows_t, lanes in tiles_of(0, PAIRS):
        carried = mix_r[rows_t, lanes].astype(f32)
        xs = x[rows_t, lanes].astype(f32)
        mix = carried + skip[:, lanes] * xs
        z = z_r[rows_t, lanes].astype(f32)
        ds = ds_r[rows_t, lanes].astype(f32)
        sig = sigmoid(z)
        silu = z * sig
        g = mix * silu
        normalized = g * scales[0, rows_t, :]
        scaled_o[rows_t, lanes] = (normalized * gain[:, lanes]).astype(bf16)
        gain_o[:, lanes] += jnp.sum(ds * normalized, axis=0, keepdims=True)
        dg = ds * (scales[0, rows_t, :] * gain[:, lanes]) - g * scales[1, rows_t, :]
        dmix = dg * silu
        dz_o[rows_t, lanes] = (dg * mix * (sig * (1.0 + z * (1.0 - sig)))).astype(bf16)
        skip_o[:, lanes] += jnp.sum(dmix * xs, axis=0, keepdims=True)
        dy = dmix.astype(bf16)
        dy_o[rows_t, lanes] = dy
        dyf = dy.astype(f32)
        pooled[rows_t, lanes] = (dyf * carried).astype(bf16)
        weighted[rows_t, lanes] = (dyf * grown[rows_t, lanes]).astype(bf16)
    inner_o[...] = pool(pooled[...], ex)
    last = cum[BLOCK - 1 : BLOCK, :]
    whole = halves_of(jnp.broadcast_to(jnp.exp(last), (16, LANES)))
    whole = spread(whole, ex, slice(0, MINE))[:1]
    exit_o[0] = state[...].astype(bf16)
    factor_o[0] = jnp.broadcast_to(passed[...], (8, MINE))
    state[...] = whole * state[...] + dot_tn(bc[:, STATE:], weighted[...])
    passed[...] = passed[...] * whole
    send_o[0] = state[...].astype(bf16)


def within_back(u, dy, bc, cum, cumt, du_o, dbc_o):
    rows = lax.broadcasted_iota(jnp.int32, (BLOCK, BLOCK), 0)
    columns = lax.broadcasted_iota(jnp.int32, (BLOCK, BLOCK), 1)
    causal = token_of(columns) >= token_of(rows)
    products = jnp.where(causal, dot_nt(bc[:, :STATE], bc[:, STATE:]), 0.0)
    lane = lax.broadcasted_iota(jnp.int32, (BLOCK, LANES), 1)
    total = jnp.zeros((BLOCK, BLOCK), f32)
    for pair in range(PAIRS):
        values = u[:, pair * LANES : (pair + 1) * LANES]
        grads = dy[:, pair * LANES : (pair + 1) * LANES]
        made = []
        for half in range(2):
            head = 2 * pair + half
            decay = jnp.exp(jnp.minimum(cumt[0, head : head + 1, :] - cum[:, head : head + 1], 0.0))
            made.append(dot((products * decay).astype(bf16), grads))
            own = jnp.where((lane < HEAD) == (half == 0), values, jnp.zeros_like(values))
            total = total + dot_nt(own, grads) * decay
        made = jnp.where(lane < HEAD, made[0], made[1])
        du_o[:, pair * LANES : (pair + 1) * LANES] = made.astype(bf16)
    total = jnp.where(causal, total, 0.0).astype(bf16)
    dbc_o[:, :STATE] = dot(total, bc[:, STATE:])
    dbc_o[:, STATE:] = dot_tn(total, bc[:, :STATE])


def features_back_kernel(px, kw, heads, pick, tri, ex, u, dy, du_r, dbc, inner, cum,
                         entering, exit_r, factor, incoming, skip,
                         gp_o, rim_o, tail_o, kw_o, heads_o, after, wide, dpre, raw, wides,
                         products):
    j, i = pl.program_id(0), pl.program_id(1)

    @pl.when((j == 0) & (i == 0))
    def _():
        kw_o[...] = jnp.zeros_like(kw_o)
        heads_o[...] = jnp.zeros_like(heads_o)

    @pl.when(i == 0)
    def _():
        after[...] = jnp.zeros_like(after)

    rows = px[0]
    widen(rows, wide)
    biased, step, log_decay, rate = steps_of(rows[HALO:, CONVD:], heads, pick)
    c = cum[...]
    last = c[BLOCK - 1 : BLOCK, :]
    leaving = exit_r[0].astype(f32) + factor[0][:1] * incoming[0].astype(f32)
    leaving16 = leaving.astype(bf16)
    crossing = jnp.sum(leaving * entering[0].astype(f32), axis=0, keepdims=True)
    crossing = jnp.broadcast_to(crossing, (16, MINE))
    crossing = sum(pool(part, ex) for part in split(crossing))[:1] * jnp.exp(last)
    for k, value in enumerate((jnp.exp(last - c), jnp.exp(c), step)):
        wides[k] = dot(halves_of(value), ex[...])
    for rows_t, lanes in tiles_of(PAIRS, PAIRS + 1):
        total, _ = conv_tile(wide, kw, rows_t, lanes)
        products[0, rows_t, :LANES] = (total * sigmoid(total)).astype(bf16)
    raw[...] = dot(products[0, :, :LANES], leaving16)

    def finish(dact, total, sig, taps, rows_t, lanes):
        value = dact * (sig * (1.0 + total * (1.0 - sig)))
        kw_o[CONV : CONV + 1, lanes] += jnp.sum(value, axis=0, keepdims=True)
        for k in range(CONV):
            kw_o[k : k + 1, lanes] += jnp.sum(value * taps[k], axis=0, keepdims=True)
        dpre[rows_t, lanes] = value

    for rows_t, lanes in tiles_of(0, PAIRS):
        total, taps = conv_tile(wide, kw, rows_t, lanes)
        sig = sigmoid(total)
        uf = u[rows_t, lanes].astype(f32)
        dyf = dy[rows_t, lanes].astype(f32)
        left = wides[0, rows_t, lanes]
        du_state = left * raw[rows_t, lanes]
        du_in = du_r[rows_t, lanes].astype(f32)
        products[0, rows_t, lanes] = (uf * left).astype(bf16)
        products[1, rows_t, lanes] = (dyf * wides[1, rows_t, lanes]).astype(bf16)
        products[2, rows_t, lanes] = (uf * du_state).astype(bf16)
        products[3, rows_t, lanes] = (uf * du_in).astype(bf16)
        du = du_in + du_state
        products[4, rows_t, lanes] = (du * (total * sig)).astype(bf16)
        dx = du * wides[2, rows_t, lanes] + skip[:, lanes] * dyf
        finish(dx, total, sig, taps, rows_t, lanes)
    held, flow = pool(products[2], ex), inner[...] - pool(products[3], ex)
    dstep = pool(products[4], ex)
    raw[:, :STATE] = dbc[:, :STATE] + dot_nt(products[0], leaving16)
    raw[:, STATE : 2 * STATE] = dbc[:, STATE:] + dot_nt(products[1], entering[0])
    for rows_t, lanes in tiles_of(PAIRS, PAIRS + 2):
        total, taps = conv_tile(wide, kw, rows_t, lanes)
        dact = raw[rows_t, lanes.start - MINE : lanes.stop - MINE]
        finish(dact, total, sigmoid(total), taps, rows_t, lanes)
    for k in range(CONV - 1):
        begin = 8 * k + 1
        behind = jnp.concatenate([dpre[begin : begin + 7, :], after[k : k + 1, :]], axis=0)
        dpre[BLOCK + 8 * k : BLOCK + 8 * k + 8, :] = behind
    for rows_t, lanes in tiles_of(0, PAIRS + 2):
        begin = rows_t.start + 8 * (CONV - 1)
        din = sum(
            kw[k : k + 1, lanes] * dpre[begin - 8 * k : begin - 8 * k + TILE, lanes]
            for k in range(CONV)
        )
        gp_o[0, rows_t, lanes] = din.astype(bf16)
        if rows_t.stop == BLOCK:

            @pl.when(i == 0)
            def _(din=din, lanes=lanes):
                tail_o[0, :, lanes] = din[TILE - 32 :]

    first = [dpre[8 * k : 8 * k + 1, :] for k in range(CONV - 1)]
    first = jnp.concatenate(first + [jnp.zeros((8 - CONV + 1, CONVD), f32)], axis=0)
    after[...] = first
    dlog = crossing + sum(dot_tn(tri[...], part) for part in split3(flow))
    dlog = dlog + sum(dot(tri[...], part) for part in split3(held)) - held
    draw = (dstep - dlog * rate) * jax.nn.sigmoid(biased)
    gp_o[0, :, CONVD:] = dot_nt(draw.astype(bf16), pick[...]).astype(bf16)
    heads_o[0:1, :] += jnp.sum(draw, axis=0, keepdims=True)
    heads_o[1:2, :] += jnp.sum(dlog * log_decay, axis=0, keepdims=True)
    early = jnp.concatenate([jnp.zeros((8, CONVD), f32), first], axis=0)
    rim_o[0] = sum(kw[k : k + 1, :] * early[CONV - 1 - k : CONV - 1 - k + 8] for k in range(CONV))


def write_parts(j, mine_o, other_o, value):
    @pl.when(j == 0)
    def _():
        mine_o[...] = value

    @pl.when(j > 0)
    def _():
        other_o[...] = value


def added(*refs):
    return sum(ref.astype(f32) for ref in refs).astype(bf16)


def send_piece_kernel(place, value, out):
    out[...] = jnp.where(place[2] % 2 == 0, value[1], value[0])


def both_pieces_kernel(place, value, got, turn, out):
    side = place[2] % 2
    kept = jnp.where(side == 0, value[0], value[1])
    piece = jnp.where(pl.program_id(0) == side, kept, got[...])
    out[0] = dot(turn[...], piece).astype(bf16)


def ends_kernel(value, out):
    out[...] = last_tokens(value[...].astype(f32), HALO).astype(bf16)


def shard_kernel(own, got, out_weight, front_o, late_o):
    r_in, half = own.shape[0], out_weight.shape[0] // 2
    for k, source in enumerate((own, got)):
        front_o[k] = source[:, :FRONT]
        late_o[k, :r_in] = source[:, FRONT:]
        late_o[k, r_in:] = out_weight[k * half : (k + 1) * half]


def pair_kernel(first, second, out):
    count = first.shape[1]
    out[:, :count] = first[...]
    out[:, count:] = second[...]


def halves_kernel(along_x, along_y, x_o, y_o):
    x_o[...] = along_x[0]
    y_o[...] = along_y[0]


def ends_grads_kernel(front, front_got, late, late_got, own_o, send_o, out_o):
    r_in = front.shape[1]
    for k, out in enumerate((own_o, send_o)):
        out[:, :CONVD] = added(front[k], front_got[k])
        out[:, CONVD:] = added(late[k, :r_in], late_got[k, :r_in])
        half = late.shape[1] - r_in
        out_o[k * half : (k + 1) * half] = late[k, r_in:].astype(f32) + late_got[k, r_in:].astype(f32)


def input_grad_kernel(n_dp, place, own, got, sums, out):
    run, first = INNER // n_dp, place[1] == 0
    part = own.shape[0] // 4
    for k in range(n_dp // 2):
        for source, target in ((0, INNER), (CONVD, 0)):
            mine = own[:, source + k * run : source + (k + 1) * run].astype(f32)
            others = got[:, source + k * run : source + (k + 1) * run].astype(f32)
            at = target + 2 * k * run
            out[:, at : at + run] = jnp.where(first, mine, others)
            out[:, at + run : at + 2 * run] = jnp.where(first, others, mine)
    both = own[:, MINE:CONVD].astype(f32) + got[:, MINE:CONVD].astype(f32)
    out[:, 2 * INNER : INNER + XBC] = both
    for k in range(4):
        out[k * part : (k + 1) * part, INNER + XBC :] = sums[8 : 8 + part, k * HEADS : (k + 1) * HEADS]


def sums_kernel(parts, out):
    out[...] = jnp.sum(parts[...], axis=0)


def activations_kernel(place, tokens, keep, got, turn, out):
    value = jnp.where(pl.program_id(0) == place[2] % 2, keep[...], got[...])
    value = dot_tn(turn[...], value)
    out[0] = (tokens[0].astype(f32) + value).astype(bf16)


def tokens_grad_kernel(place, tokens, cot, keep, got, norm, turn, out):
    value = jnp.where(pl.program_id(0) == place[2] % 2, keep[...], got[...])
    value = dot_tn(turn[...], value)
    residual = tokens[0].astype(f32)
    inverse = inverse_rms(residual)
    weighted = value * norm[...]
    along = jnp.mean(weighted * residual, axis=-1, keepdims=True)
    out[0] = (
        cot[0].astype(f32) + inverse * weighted - residual * (inverse * inverse * inverse * along)
    )


def relative(place, n_ctx, groups):
    for group in range(2):
        for slot in range(n_ctx // 2):
            z = place[2] ^ group ^ (2 * slot)
            at = slot if groups == 2 else group * (n_ctx // 2) + slot
            first = 5 * group if groups == 2 else 0
            for half in range(2):
                for chip in range(3):
                    yield first + chip, (half, at), place[0] ^ chip, z, half
                yield first + 3 + half, (at,), place[0] ^ 3, z, half


def relative_back(place, n_ctx, groups):
    spots = {(0, 0): (0, 0), (0, 1): (0, 1), (1, 1): (1, 1), (2, 0): (2, 1), (1, 0): (3, None),
             (2, 1): (4, None), (3, 1): (1, 0), (3, 0): (2, 0)}
    for group in range(2):
        for slot in range(n_ctx // 2):
            z = place[2] ^ group ^ (2 * slot)
            at = slot if groups == 2 else group * (n_ctx // 2) + slot
            first = 5 * group if groups == 2 else 0
            for (chip, half), (piece, lead) in spots.items():
                index = (at,) if lead is None else (lead, at)
                yield first + piece, index, place[0] ^ chip, z, half


def front_rows(place, n_ctx, chip, z, half, count):
    return pl.multiple_of(((chip * 2 + (place[1] ^ half)) * n_ctx + z) * count, count)


def out_rows(n_ctx, chip, z, half, count):
    return pl.multiple_of(((chip * n_ctx + z) * 2 + half) * count, count)


def front_weights_kernel(n_dp, n_ctx, r_in, place, heads_in, ex, *refs):
    pieces, refs = refs[:-10], refs[-10:]
    front, wide = refs[0], refs[7]
    if len(pieces) == 1:
        front[...] = pieces[0][...]
    else:
        for piece, index, chip, z, half in relative(place, n_ctx, 2):
            begin = front_rows(place, n_ctx, chip, z, half, r_in)
            front[pl.ds(begin, r_in), :] = pieces[piece][index]
    wide[...] = front[:, CONVD:].astype(f32)
    spread_small(n_dp, r_in, place[1], wide, heads_in, ex, *refs[1:7], *refs[8:])


def late_weights_kernel(n_ctx, r_in, place, *refs):
    pieces, gate, out = refs[:-2], refs[-2], refs[-1]
    r_out = pieces[0].shape[2] - r_in
    for piece, index, chip, z, half in relative(place, n_ctx, 1):
        block = pieces[piece][index]
        gate[pl.ds(front_rows(place, n_ctx, chip, z, half, r_in), r_in), :] = block[:r_in]
        out[pl.ds(out_rows(n_ctx, chip, z, half, r_out), r_out), :] = block[r_in:]


def middle_kernel(n_ctx, r_in, place, normed, dz, scaled, cot_mine, cot_other, wo, u, dy, bc, cum, cumt, *refs):
    mine_o, other_o, du_o, dbc_o = refs[:4]
    outputs, (gate, out) = refs[4:-2], refs[-2:]
    j, i = pl.program_id(0), pl.program_id(1)
    within_back(u, dy, bc, cum, cumt, du_o, dbc_o)
    step = j * pl.num_programs(1) + i
    cot = jnp.where(j == 0, cot_mine[...], cot_other[...])
    write_parts(j, mine_o, other_o, dot(scaled[...], wo[...]).astype(bf16))
    gate_part, out_part = dot_tn(normed[...], dz[...]), dot_tn(scaled[...], cot)

    @pl.when(step == 0)
    def _():
        gate[...] = gate_part
        out[...] = out_part

    @pl.when(step > 0)
    def _():
        gate[...] += gate_part
        out[...] += out_part

    @pl.when(step == pl.num_programs(0) * pl.num_programs(1) - 1)
    def _():
        if len(outputs) == 2:
            outputs[0][...] = gate[...].astype(bf16)
            outputs[1][...] = out[...].astype(bf16)
            return
        r_out = outputs[0].shape[2] - r_in
        for piece, index, chip, z, half in relative_back(place, n_ctx, 1):
            begin = front_rows(place, n_ctx, chip, z, half, r_in)
            outputs[piece][index + (slice(0, r_in),)] = gate[pl.ds(begin, r_in), :].astype(bf16)
            begin = out_rows(n_ctx, chip, z, half, r_out)
            outputs[piece][index + (slice(r_in, r_in + r_out),)] = out[
                pl.ds(begin, r_out), :
            ].astype(bf16)


def with_rim(gp, tail, rim, whole):
    whole[...] = gp[0]
    late = tail[0]
    row = lax.broadcasted_iota(jnp.int32, late.shape, 0)
    for k in range(CONV - 1):
        here = row == 32 - AHEAD + 8 * k + 7
        late = late + jnp.where(here, rim[0, 8 - CONV + 1 + k : 8 - CONV + 2 + k, :], 0.0)
    whole[whole.shape[0] - 32 :, :CONVD] = late.astype(bf16)


def front_grads_kernel(n_ctx, r_in, place, normed, gp, tail, rim, step_o, *refs):
    outputs, (total, whole) = refs[:-2], refs[-2:]
    j = pl.program_id(0)
    with_rim(gp, tail, rim, whole)
    part = dot_tn(normed[...], whole[...])

    @pl.when(j == 0)
    def _():
        total[...] = part

    @pl.when(j > 0)
    def _():
        total[...] += part

    @pl.when(j == pl.num_programs(0) - 1)
    def _():
        step_o[...] = total[:, CONVD:]
        if len(outputs) == 1:
            outputs[0][...] = total[:, :CONVD].astype(bf16)
            return
        for piece, index, chip, z, half in relative_back(place, n_ctx, 1):
            begin = front_rows(place, n_ctx, chip, z, half, r_in)
            outputs[piece][index] = total[pl.ds(begin, r_in), :CONVD].astype(bf16)


def normed_grads_kernel(mine, other, dz, wg, gp, tail, rim, front, mine_o, other_o, norm_o, whole):
    j = pl.program_id(0)
    with_rim(gp, tail, rim, whole)
    back = dot_nt(dz[...], wg[...]) + dot_nt(whole[...], front[...])
    write_parts(j, mine_o, other_o, back.astype(bf16))
    residual = jnp.where(j == 0, mine[...], other[...]).astype(f32)

    @pl.when(j == 0)
    def _():
        norm_o[...] = jnp.zeros_like(norm_o)

    norm_o[...] += jnp.sum(back * (residual * inverse_rms(residual)), axis=0, keepdims=True)


def small_place(n, k, r_in, n_all):
    rows = min(r_in, 8)
    span = (LANES - HEADS) // -(-7 // rows)
    width = (XBC // n_all,) * 5 + (INNER // n_all, r_in)
    return n * r_in + k % rows, HEADS + (k // rows) * span, width[k]


def prepare_kernel(n_dp, n_all, place, weight, vectors, own_o, other_o):
    r_in, run, first = weight.shape[0], INNER // n_dp, place[1] == 0
    for k in range(n_dp // 2):
        for source, target in ((INNER, 0), (0, FRONT)):
            low = weight[:, source + 2 * k * run : source + (2 * k + 1) * run]
            high = weight[:, source + (2 * k + 1) * run : source + (2 * k + 2) * run]
            at = target + k * run
            own_o[:, at : at + run] = jnp.where(first, low, high)
            other_o[:, at : at + run] = jnp.where(first, high, low)
    row = lax.broadcasted_iota(jnp.int32, (r_in, LANES), 0)
    small = jnp.concatenate(
        [weight[:, INNER + XBC :].astype(f32), jnp.zeros((r_in, LANES - HEADS), f32)], axis=1
    )
    at = 0
    for k in range(7):
        line, lane, count = small_place(0, k, r_in, n_all)
        piece = vectors[:, at : at + count].astype(f32)
        parts = [jnp.zeros((1, lane), f32), piece, jnp.zeros((1, LANES - lane - count), f32)]
        small = small + jnp.where(row == line, jnp.concatenate(parts, axis=1), 0.0)
        at += count
    for out in (own_o, other_o):
        out[:, MINE:CONVD] = weight[:, 2 * INNER : INNER + XBC]
        out[:, CONVD:FRONT] = small.astype(bf16)


def spread_small(n_dp, r_in, core, wide, heads_in, ex, kw_o, gain_o, norm_o, heads_o, skip_o, pick_o,
                 full, gains):
    n_all = wide.shape[0] // r_in
    run, heads_run, first = INNER // n_dp, HEADS // n_dp, core == 0
    full[...] = jnp.zeros_like(full)
    for n in range(n_all):
        for k in range(7):
            row, lane, count = small_place(n, k, r_in, n_all)
            target, at = ((full, k), (gains, 0), (norm_o, 0))[max(k - CONV, 0)]
            target[at : at + 1, n * count : (n + 1) * count] = wide[row : row + 1, lane : lane + count]
    for k in range(n_dp // 2):
        low, high = 2 * k * run, (2 * k + 1) * run
        kw_o[:, k * run : (k + 1) * run] = jnp.where(
            first, full[:, low : low + run], full[:, high : high + run]
        )
        gain_o[:, k * run : (k + 1) * run] = jnp.where(
            first, gains[:, low : low + run], gains[:, high : high + run]
        )
    kw_o[:, MINE:] = full[:, INNER:]
    source = lax.broadcasted_iota(jnp.int32, (LANES, LANES), 0)
    local = lax.broadcasted_iota(jnp.int32, (LANES, LANES), 1)
    position = ((local // heads_run) * 2 + core) * heads_run + local % heads_run
    chosen = (source == position) & (local < HEADS // 2)
    pick = jnp.where(chosen, 1.0, 0.0).astype(bf16)
    pick_o[...] = pick
    heads = dot(heads_in[...].astype(bf16), pick)
    row = lax.broadcasted_iota(jnp.int32, (8, LANES), 0)
    lane = lax.broadcasted_iota(jnp.int32, (8, LANES), 1)
    rate = jnp.where(lane < HEADS // 2, jnp.exp(heads), 0.0)
    heads_o[...] = jnp.where(row == 1, rate, heads)
    skip_o[...] = dot(heads.astype(bf16), ex[:LANES, :])[2:3]


def pack_kernel(n_dp, place, norm_sum, kw_sum, gain_sum, heads_sum, skip_sum, step_sum, pick, ex,
                packed_o, full, gains):
    n_all = packed_o.shape[0]
    taps_n, gain_n, norm_n = XBC // n_all, INNER // n_all, norm_sum.shape[1] // n_all
    part, run = norm_n // 4, INNER // n_dp
    keep = [jnp.where(place[1] == which, 1.0, 0.0) for which in range(2)]
    for k in range(n_dp // 2):
        for which in range(2):
            begin = (2 * k + which) * run
            full[:, begin : begin + run] = kw_sum[:, k * run : (k + 1) * run] * keep[which]
            gains[:, begin : begin + run] = gain_sum[:, k * run : (k + 1) * run] * keep[which]
    full[:, INNER:] = kw_sum[:, MINE:]
    skips = jnp.broadcast_to(skip_sum[...], (16, MINE))
    skips = sum(pool(part, ex) for part in split(skips))[:8]
    row = lax.broadcasted_iota(jnp.int32, (8, LANES), 0)
    heads = jnp.where(row == 2, skips, heads_sum[...])
    heads = sum(dot_nt(piece, pick[...]) for piece in split3(heads))
    packed_o[...] = jnp.zeros_like(packed_o)
    for n in range(n_all):
        packed_o[n, 0:5, :taps_n] = full[0:5, n * taps_n : (n + 1) * taps_n]
        packed_o[n, 5:6, :gain_n] = gains[:, n * gain_n : (n + 1) * gain_n]
        packed_o[n, 6:7, :norm_n] = norm_sum[:, n * norm_n : (n + 1) * norm_n]
        for k in range(3):
            packed_o[n, 7:8, k * HEADS : (k + 1) * HEADS] = heads[k : k + 1, :HEADS]
        for k in range(4):
            begin = n * norm_n + k * part
            packed_o[n, 8 : 8 + part, k * HEADS : (k + 1) * HEADS] = step_sum[
                begin : begin + part, :HEADS
            ]


def call(kernel, grid, in_specs, out_specs, out_shape, scratch=(), cost=0, needs=(), vmem=20):
    count = len(in_specs)

    def body(*refs):
        kernel(*refs[:count], *refs[count + len(needs) :])

    made = pl.pallas_call(
        body,
        grid=grid,
        in_specs=list(in_specs) + [pl.BlockSpec(memory_space=pl.ANY)] * len(needs),
        out_specs=out_specs,
        out_shape=out_shape,
        scratch_shapes=scratch,
        cost_estimate=pl.CostEstimate(
            flops=int(1 + cost * 1e9), transcendentals=0, bytes_accessed=int(1 + cost * 3.5e6)
        ),
        compiler_params=pltpu.CompilerParams(
            vmem_limit_bytes=vmem << 20, dimension_semantics=("arbitrary",) * len(grid)
        ),
    )
    return lambda *arrays: made(*arrays, *needs)


def sds(shape, dtype=f32):
    return jax.ShapeDtypeStruct(shape, dtype)


def main(value):
    return pltpu.with_memory_space_constraint(value, pltpu.HBM)


def on_device(
    tokens,
    cotangent,
    norm_weight,
    input_weight,
    kernel_weight,
    kernel_bias,
    step_bias,
    decay_log,
    skip_gain,
    gate_norm_weight,
    output_weight,
):
    n_dp, n_ctx = lax.axis_size("dp"), lax.axis_size("ctx")
    n_q, n_all = n_dp // 2, n_dp * n_ctx
    place, z = lax.axis_index("dp"), lax.axis_index("ctx")
    q, core = place >> 1, place & 1
    seqs, piece, width = tokens.shape
    length = 2 * piece
    blocks = length // BLOCK
    rows = seqs * length
    r_in, r_out = input_weight.shape[0], output_weight.shape[0]
    every = ("dp", "ctx")
    fast = n_q == 4 and n_ctx == 4 and r_in % 16 == 0
    where = jnp.stack([q, core, z]).astype(jnp.int32)
    smem = pl.BlockSpec(memory_space=pltpu.SMEM)

    def lanes(value, count, wide=LANES):
        return jnp.pad(value, ((0, count - value.shape[0]), (0, wide - value.shape[1])))

    def all_of(arrays):
        return [pl.BlockSpec(v.shape, lambda *_, n=len(v.shape): (0,) * n) for v in arrays]

    def once(kernel, arrays, made, scratch=(), cost=0, needs=(), placed=False):
        specs = ([smem] if placed else []) + all_of(arrays)
        single = not isinstance(made, list)
        outs = all_of([made])[0] if single else all_of(made)
        run = call(kernel, (1,), specs, outs, made, scratch, cost, needs)
        return run(*([where] if placed else []), *arrays)

    order = token_of(np.arange(BLOCK))
    turn = (order[:, None] == np.arange(BLOCK)[None]).astype(ml_dtypes.bfloat16)
    turn = jnp.asarray(turn)
    cuts = 2
    cut_s = pl.BlockSpec((piece // cuts, width), lambda i: (i, 0))
    both_cut_s = pl.BlockSpec((2, piece // cuts, width), lambda i: (0, i, 0))

    def piece_to_send(value, needs=()):
        made = sds((piece, width), bf16)
        run = call(send_piece_kernel, (cuts,), [smem, both_cut_s], cut_s, made, needs=needs)
        return run(where, value)

    def enter_line(value, send, needs=(), cost=0):
        made, got = sds((2, piece, width), bf16), swap(send, "ctx", 1)
        specs = [smem] + all_of([value, got, turn])
        out_s = pl.BlockSpec((1, piece, width), lambda i: (i, 0, 0))
        run = call(both_pieces_kernel, (2,), specs, out_s, made, (), cost, needs)
        return run(where, value, got, turn).reshape(length, width)

    def ends_of(value):
        end_s = pl.BlockSpec((BLOCK, width), lambda i: (length // BLOCK - 1, 0))
        made = sds((HALO, width), bf16)
        return call(ends_kernel, (1,), [end_s], all_of([made])[0], made)(value)

    def leave_cores(mine, other, needs=()):
        total = add(after(mine, *needs), swap(other, "dp", 1)).reshape(2, piece, width)
        return choose(total, z & 1, 0), choose(total, 1 - (z & 1), 0)


    tokens_send = piece_to_send(tokens)
    vectors = jnp.concatenate([kernel_weight.reshape(-1), kernel_bias, gate_norm_weight, norm_weight])
    own_columns, other_columns = once(
        functools.partial(prepare_kernel, n_dp, n_all),
        [input_weight, vectors[None]],
        [sds((r_in, FRONT + MINE), bf16)] * 2,
        cost=8,
        needs=[tokens_send],
        placed=True,
    )
    got = swap(other_columns, "dp", 1)
    half = r_in + r_out // 2
    if fast:
        front_shard, late_shard = once(
            shard_kernel,
            [own_columns, got, output_weight],
            [sds((2, r_in, FRONT), bf16), sds((2, half, width), bf16)],
        )

        def pair(first, second, needs=(), cost=0):
            first, second = (v.reshape((2, -1) + v.shape[-2:]) for v in (first, second))
            count = first.shape[1] + second.shape[1]
            made = sds((2, count) + first.shape[2:], bf16)
            specs = [
                pl.BlockSpec((1,) + v.shape[1:], lambda k: (k, 0, 0, 0)) for v in (first, second, made)
            ]
            run = call(pair_kernel, (2,), specs[:2], specs[2], made, (), cost, needs)
            return run(first, second)

        def across_parts(along_x, along_y, needs=()):
            made = [sds(along_x.shape[1:], bf16)] * 2
            block = (1, 1) + along_x.shape[2:]
            specs = [
                pl.BlockSpec(block, lambda i, half=half: (half, i, 0, 0)) for half in range(2)
            ]
            outs = [pl.BlockSpec(block[1:], lambda i: (i, 0, 0))] * 2
            run = call(halves_kernel, along_x.shape[1:2], specs, outs, made, (), 0, needs)
            return run(along_x, along_y)

        def across_of(send_y, send_x):
            return swap(send_y, "dp", 4), swap(send_x, "dp", 2)

        first_got = swap(front_shard, "ctx", 2)
        cot_send = piece_to_send(cotangent, needs=[front_shard])
        inside = enter_line(tokens, tokens_send, needs=[cot_send], cost=8)
        other = swap(inside, "dp", 1)
        ends = ends_of(inside)
        before = hop(ends, 2)
        near = pair(front_shard, first_got, needs=[ends])
        sides = sides_of(near)
        far = swap(near, "ctx", 1)
        late_shard = after(late_shard, near)
        late_got = swap(late_shard, "ctx", 2)
        across = across_of(*across_parts(*sides))
        far = after(far, *across)
        far_sides = sides_of(far)
        late_near = pair(late_shard, late_got, needs=[far, before], cost=8)
        far_across_send = across_parts(*far_sides, needs=[late_near])
        far_across = across_of(*far_across_send)
        late_far = swap(late_near, "ctx", 1)
        before_other = swap(before, "dp", 1)
        cot = enter_line(cotangent, cot_send, needs=far_across_send, cost=0.1)
        late_own = after(pair(late_near, late_far, needs=far_across_send, cost=8), *far_across)
        front_pieces = [near, *sides, *across, far, *far_sides, *far_across]
    else:
        shard = ordered(own_columns, got, core, 0)
        near = gather_line(shard[:, :, :FRONT], z, n_ctx, 1)
        far = swap(near, "ctx", 1)
        halves = gather_rest(near, far, z, n_ctx, q, n_q)
        front_pieces = [jnp.stack(halves, axis=1).reshape(width, FRONT)]
        inside = enter_line(tokens, tokens_send)
        other = swap(inside, "dp", 1)
        before = hop(ends_of(inside), 2)
        before_other = swap(before, "dp", 1)
        out_halves = output_weight.reshape(2, r_out // 2, width)
        late_shard = jnp.concatenate([shard[:, :, FRONT:], out_halves], axis=1)
        late_near = gather_line(late_shard, z, n_ctx, 1)
        late_far = swap(late_near, "ctx", 1)
        first, second = gather_rest(late_near, late_far, z, n_ctx, q, n_q)
        w_gate = jnp.stack([first[:, :, :r_in], second[:, :, :r_in]], axis=1).reshape(width, MINE)
        w_out = jnp.stack([first[:, :, r_in:], second[:, :, r_in:]], axis=2).reshape(MINE, width)

    ex = np.arange(LANES)[:, None] == (np.arange(MINE)[None] // HEAD)
    ex = ex.astype(ml_dtypes.bfloat16)
    ex = jnp.asarray(np.concatenate([ex, ex], axis=0))
    tri = order[:, None] >= order[None]
    tri = jnp.asarray(tri.astype(ml_dtypes.bfloat16))
    heads_in = lanes(jnp.stack([step_bias, decay_log, skip_gain]).astype(f32), 8)
    w_front, kw, gain, norm_full, heads, skip, pick = once(
        functools.partial(front_weights_kernel, n_dp, n_ctx, r_in),
        [heads_in, ex, *front_pieces],
        [sds((width, FRONT), bf16), sds((8, CONVD)), sds((1, MINE)), sds((1, width)),
         sds((8, LANES)), sds((1, MINE)), sds((LANES, LANES), bf16)],
        [pltpu.VMEM((width, LANES), f32), pltpu.VMEM((8, XBC), f32), pltpu.VMEM((1, INNER), f32)],
        cost=8,
        needs=[late_own, before_other, cot] if fast else (),
        placed=True,
    )
    if fast:
        late_sides = sides_of(late_own)
    else:
        cot = enter_line(cotangent, piece_to_send(cotangent))
    cot_other = swap(cot, "dp", 1)

    grid = (seqs, blocks)

    def here(shape, back=False):
        lead = len(shape)
        if back:
            return pl.BlockSpec(shape, lambda j, i: (j * blocks + blocks - 1 - i,) + (0,) * (lead - 1))
        return pl.BlockSpec(shape, lambda j, i: (j * blocks + i,) + (0,) * (lead - 1))

    def per_seq(shape):
        return pl.BlockSpec(shape, lambda j, i: (j,) + (0,) * (len(shape) - 1))

    def fixed(shape):
        return pl.BlockSpec(shape, lambda j, i: (0,) * len(shape))

    mine_s = pl.BlockSpec((BLOCK, width), lambda j, i: (i * (1 - j) + (blocks - 1) * j, 0))
    other_s = pl.BlockSpec((BLOCK, width), lambda j, i: (i * j, 0))
    part_s = sds((length, width), bf16)
    steps_n = seqs * blocks
    wide, heads_s, both = (BLOCK, MINE), (BLOCK, LANES), (BLOCK, 2 * STATE)
    state_s, row8 = (1, STATE, MINE), (1, 8, MINE)
    conv_specs = [
        fixed((8, CONVD)),
        fixed((8, LANES)),
        fixed((LANES, LANES)),
        fixed((BLOCK, BLOCK)),
        fixed((2 * LANES, MINE)),
    ]
    conv_args = (kw, heads, pick, tri, ex)
    ext_front = (1, BLOCK + HALO, FRONT)
    front_s = fixed((width, FRONT))
    whole_s, halo_s = fixed((length, width)), fixed((HALO, width))
    normed, px, x, u, bc, cum, cumt, entry, entry_factor, state_total, state_decay = call(
        features_kernel,
        grid,
        [whole_s, whole_s, halo_s, halo_s, fixed((1, width)), front_s] + conv_specs,
        [here((BLOCK, width)), here(ext_front), here(wide), here(wide), here(both), here(heads_s),
         here((1, LANES, BLOCK)), here(state_s), here(row8), per_seq(state_s), per_seq(row8)],
        [pltpu.HBM((rows, width), bf16), pltpu.HBM((steps_n, BLOCK + HALO, FRONT), bf16),
         pltpu.HBM((rows, MINE), bf16), pltpu.HBM((rows, MINE), bf16),
         pltpu.HBM((rows, 2 * STATE), bf16), pltpu.HBM((rows, LANES)  , f32),
         pltpu.HBM((steps_n, LANES, BLOCK), f32), pltpu.HBM((steps_n, STATE, MINE), bf16), sds((steps_n, 8, MINE)),
         sds((seqs, STATE, MINE), bf16), sds((seqs, 8, MINE))],
        [pltpu.VMEM((STATE, MINE), f32), pltpu.VMEM((1, MINE), f32),
         pltpu.VMEM((BLOCK + AHEAD, CONVD), f32), pltpu.VMEM((BLOCK, MINE), bf16),
         pltpu.VMEM((BLOCK, MINE), f32), pltpu.VMEM((BLOCK, MINE), f32)],
        cost=16,
    )(inside, other, before, before_other, norm_full, w_front, *conv_args)

    def relay(local, decay, steps):
        received = hop(local, steps)
        for _ in range(n_ctx // 2 - 2):
            received = hop((decay[:, :1] * received.astype(f32) + local.astype(f32)).astype(bf16), steps)
        return received

    incoming = relay(state_total, state_decay, 2)
    late_across_send = across_parts(*late_sides, needs=[state_total]) if fast else ()
    y = call(
        within_kernel,
        grid,
        [here(wide), here(both), here(heads_s), here((1, LANES, BLOCK))],
        here(wide),
        sds((rows, MINE), bf16),
        cost=8,
        needs=late_across_send,
    )(u, bc, cum, cumt)

    if fast:
        late_across = across_of(*late_across_send)
        w_gate, w_out = once(
            functools.partial(late_weights_kernel, n_ctx, r_in),
            [late_own, *late_sides, *late_across],
            [sds((width, MINE), bf16), sds((MINE, width), bf16)],
            placed=True,
            needs=[y],
        )

    mix, gate_raw, ds, entering, sums = call(
        gate_kernel,
        grid,
        [here((BLOCK, width)), mine_s, other_s, fixed((width, MINE)),
         fixed((MINE, width)), here(wide), here(wide), here(both), here(heads_s),
         here(state_s), here(row8), per_seq(state_s), fixed((1, MINE)), fixed((1, MINE)),
         fixed((2 * LANES, MINE))],
        [here(wide), here(wide), here(wide), here(state_s),
         pl.BlockSpec((8, BLOCK), lambda j, i: (0, j * blocks + i))],
        [pltpu.HBM((rows, MINE), bf16)] * 3
        + [pltpu.HBM((steps_n, STATE, MINE), bf16), sds((8, rows))],
        [pltpu.VMEM((BLOCK, LANES), f32)] * 2,
        cost=16,
    )(normed, cot, cot_other, w_gate, w_out, y, x, bc, cum, entry, entry_factor, incoming, skip, gain, ex)
    sums_got = swap(sums, "dp", 1)

    scaled, dy, dz, inner, leaving, leave_factor, grad_send, gain_sum, skip_sum = call(
        mixture_kernel,
        grid,
        [here(wide, True)] * 4
        + [here(both, True), here(heads_s, True)]
        + [pl.BlockSpec((8, BLOCK), lambda j, i: (0, j * blocks + blocks - 1 - i)),
           pl.BlockSpec((8, BLOCK), lambda j, i: (0, (1 - j) * blocks + blocks - 1 - i))]
        + [fixed((1, MINE)), fixed((1, MINE)), fixed((2 * LANES, MINE))],
        [here(wide, True)] * 3
        + [here(heads_s, True), here(state_s, True), here(row8, True), per_seq(state_s),
           fixed((1, MINE)), fixed((1, MINE))],
        [sds((rows, MINE), bf16)] * 3
        + [sds((rows, LANES)), sds((steps_n, STATE, MINE), bf16), sds((steps_n, 8, MINE)),
           sds((seqs, STATE, MINE), bf16), sds((1, MINE)), sds((1, MINE))],
        [pltpu.VMEM((STATE, MINE), f32), pltpu.VMEM((1, MINE), f32), pltpu.VMEM((BLOCK, MINE), bf16),
         pltpu.VMEM((BLOCK, MINE), bf16), pltpu.VMEM((BLOCK, MINE), f32), pltpu.VMEM((2, BLOCK, LANES), f32)],
        cost=12,
    )(*map(main, (mix, gate_raw, ds, x, bc, cum)), sums, sums_got, skip, gain, ex)
    grad_incoming = relay(grad_send, state_decay, -2)

    def parts_of(rows_n, columns):
        wide_part, narrow = (2, n_ctx, rows_n, columns), (n_ctx, rows_n, columns)
        return [sds(shape, bf16) for shape in [wide_part] * 3 + [narrow] * 2]

    made = parts_of(half, width) if fast else [sds((width, MINE), bf16), sds((MINE, width), bf16)]
    out_mine, out_other, du, dbc, *late_parts = call(
        functools.partial(middle_kernel, n_ctx, r_in),
        grid,
        [smem, here((BLOCK, width)), here(wide), here(wide), mine_s, other_s, fixed((MINE, width)),
         here(wide), here(wide), here(both), here(heads_s), here((1, LANES, BLOCK))],
        [mine_s, other_s, here(wide), here(both)] + all_of(made),
        [part_s, part_s, sds((rows, MINE), bf16), sds((rows, 2 * STATE))] + made,
        [pltpu.VMEM((width, MINE), f32), pltpu.VMEM((MINE, width), f32)],
        cost=24,
    )(where, normed, dz, scaled, cot, cot_other, w_out, u, dy, bc, cum, cumt)

    def join_of(along_x, along_y, got_x, got_y, needs=()):
        return add(after(along_x, *needs), got_y[0]), add(along_y, got_x[0])

    def own_of(own, got_x, got_y, last_x, last_y, needs=()):
        own = after(own, *needs)
        far_n = n_ctx // 2
        return [
            jnp.stack(
                [
                    add(own[0, part], got_y[1, part], last_x[part]),
                    add(own[1, part], got_x[1, part], last_y[part]),
                ]
            )
            for part in (slice(0, far_n), slice(far_n, n_ctx))
        ]

    def fold_of(near_part, got):
        return [add(near_part[:, slot], got[:, slot]) for slot in range(2)]

    if fast:
        late_first = swap(late_parts[1], "dp", 2), swap(late_parts[2], "dp", 4)

    gp, rim, tail, kw_sum, heads_sum = call(
        features_back_kernel,
        grid,
        [here(ext_front, True)]
        + conv_specs
        + [here(wide, True), here(wide, True), here(wide, True), here(both, True),
           here(heads_s, True), here(heads_s, True), here(state_s, True), here(state_s, True),
           here(row8, True), per_seq(state_s), fixed((1, MINE))],
        [pl.BlockSpec((1, BLOCK, FRONT), lambda j, i: (j, blocks - 1 - i, 0)),
         per_seq((1, 8, CONVD)), per_seq((1, 32, CONVD)), fixed((8, CONVD)), fixed((8, LANES))],
        [sds((seqs, length, FRONT), bf16), sds((seqs, 8, CONVD)),
         sds((seqs, 32, CONVD)), sds((8, CONVD)), sds((8, LANES))],
        [pltpu.VMEM((8, CONVD), f32), pltpu.VMEM((BLOCK + AHEAD, CONVD), f32),
         pltpu.VMEM((BLOCK + AHEAD, CONVD), f32), pltpu.VMEM((BLOCK, MINE), f32),
         pltpu.VMEM((3, BLOCK, MINE), f32), pltpu.VMEM((5, BLOCK, MINE), bf16)],
        cost=24,
    )(px, *conv_args, u, dy, du, dbc, inner, cum, entering, leaving, leave_factor, grad_incoming, skip)

    out_keep, out_send = leave_cores(out_mine, out_other, needs=[gp])
    out_got = swap(out_send, "ctx", 1)
    rim = hop(rim, -2)
    if fast:
        late_second = join_of(late_parts[3], late_parts[4], *late_first, needs=[gp])
        late_last = sides_of_each(*late_second)
    seq_wide = pl.BlockSpec((length, MINE), lambda j: (j, 0))
    seq_gp = pl.BlockSpec((1, length, FRONT), lambda j: (j, 0, 0))
    rims = [pl.BlockSpec((1, n, CONVD), lambda j: (j, 0, 0)) for n in (32, 8)]
    back_mine, back_other, norm_sum = call(
        normed_grads_kernel,
        (seqs,),
        all_of([inside, other]) + [seq_wide] + all_of([w_gate]) + [seq_gp] + rims + all_of([w_front]),
        all_of([part_s, part_s, sds((1, width))]),
        [part_s, part_s, sds((1, width))],
        [pltpu.VMEM((length, FRONT), bf16)],
        cost=12,
        needs=[*late_second, out_send] if fast else (),
    )(inside, other, dz, w_gate, gp, tail, rim, w_front)
    if fast:
        late_near, late_far = own_of(late_parts[0], *late_first, *late_last, needs=[back_mine])
        late_got = swap(late_far, "ctx", 1)
    made = parts_of(r_in, CONVD) if fast else [sds((width, CONVD), bf16)]
    d_step, *front_parts = call(
        functools.partial(front_grads_kernel, n_ctx, r_in),
        (seqs,),
        [smem, seq_wide, seq_gp] + rims,
        all_of([sds((width, LANES))] + made),
        [sds((width, LANES))] + made,
        [pltpu.VMEM((width, FRONT), f32), pltpu.VMEM((length, FRONT), bf16)],
        cost=10,
        needs=[late_far] if fast else (),
    )(where, normed, gp, tail, rim)
    if fast:
        front_first = swap(front_parts[1], "dp", 2), swap(front_parts[2], "dp", 4)
    back_keep, back_send = leave_cores(back_mine, back_other, needs=[d_step])
    back_got = swap(back_send, "ctx", 1)

    def finish(kernel, arrays, more, dtype, needs, cost):
        block_s = pl.BlockSpec((1, piece, width), lambda j: (j, 0, 0))
        specs = [smem] + [block_s] * len(arrays) + all_of(more)
        made = sds((seqs, piece, width), dtype)
        return call(kernel, (seqs,), specs, block_s, made, (), cost, needs)(where, *arrays, *more)

    if fast:
        late_keep, late_send = fold_of(late_near, late_got)
        late_got = swap(late_send, "ctx", 2)
    packed = once(
        functools.partial(pack_kernel, n_dp),
        [norm_sum, kw_sum, gain_sum, heads_sum, skip_sum, d_step, pick, ex],
        sds((n_all, 16, LANES)),
        [pltpu.VMEM((8, XBC), f32), pltpu.VMEM((1, INNER), f32)],
        cost=8,
        needs=[back_send, late_send] if fast else (),
        placed=True,
    )
    packed_got = lax.all_to_all(packed, every, 0, 0)
    activations = finish(
        activations_kernel, [tokens], [out_keep, out_got, turn], bf16, [packed], 8
    )
    if fast:
        front_second = join_of(front_parts[3], front_parts[4], *front_first, needs=[activations])
        front_last = sides_of_each(*front_second)
    tokens_grad = finish(
        tokens_grad_kernel,
        [tokens, cotangent],
        [back_keep, back_got, norm_full, turn],
        f32,
        [*front_second, late_got] if fast else (),
        8,
    )
    if fast:
        front_near, front_far = own_of(
            front_parts[0], *front_first, *front_last, needs=[tokens_grad, packed_got]
        )
        front_keep, front_send = fold_of(front_near, swap(front_far, "ctx", 1))
        front_got = swap(front_send, "ctx", 2)
    sums = once(
        sums_kernel, [packed_got], sds((16, LANES)), needs=[front_send] if fast else (), cost=8
    )
    if fast:
        own, send, output_weight_grad = once(
            ends_grads_kernel,
            [front_keep, front_got, late_keep, late_got],
            [sds((r_in, CONVD + MINE), bf16)] * 2 + [sds((r_out, width))],
            needs=[sums],
        )
    else:
        d_gate, d_out = late_parts
        d_out = d_out.reshape(n_q, n_ctx, 2, r_out // 2, width)
        d_gate = d_gate.reshape(n_q, 2, n_ctx, r_in, MINE)
        halves = [
            jnp.concatenate([d_gate[:, which], d_out[:, :, which]], axis=2) for which in range(2)
        ]
        late = scatter_both(*halves, z, n_ctx, q, n_q)
        d_conv = front_parts[0].reshape(n_q, 2, n_ctx, r_in, CONVD)
        early = scatter_both(d_conv[:, 0], d_conv[:, 1], z, n_ctx, q, n_q)
        both_cores = jnp.concatenate([early, late[:, :r_in]], axis=2)
        own, send = choose(both_cores, core, 0), choose(both_cores, 1 - core, 0)
        output_weight_grad = late[:, r_in:].reshape(r_out, width).astype(f32)
    got = swap(send, "dp", 1)
    input_weight_grad = once(
        functools.partial(input_grad_kernel, n_dp),
        [own, got, sums],
        sds((r_in, INNER + XBC + HEADS)),
        placed=True,
    )
    head_sums = sums[7, : 3 * HEADS].reshape(3, HEADS)
    return (
        activations,
        tokens_grad,
        sums[6, :r_in],
        input_weight_grad,
        sums[:CONV, : XBC // n_all],
        sums[CONV, : XBC // n_all],
        head_sums[0],
        head_sums[1],
        head_sums[2],
        sums[5, : INNER // n_all],
        output_weight_grad,
    )


def solution(mesh):
    data, rows_spec, vector = P("dp", "ctx", None), P(("dp", "ctx"), None), P(("dp", "ctx"))
    taps = P(None, ("dp", "ctx"))
    return jax.shard_map(
        on_device,
        mesh=mesh,
        in_specs=(data, data, vector, rows_spec, taps, vector, P(), P(), P(), vector, rows_spec),
        out_specs=(data, data, vector, rows_spec, taps, vector, P(), P(), P(), vector, rows_spec),
        check_vma=False,
    )
```
